32 devices in a mesh: batch: 16 (over z, y, x), blk: 2 (over core).
Axes of the slice: x: 2, y: 2, z: 4, core: 2. Of those that a mesh axis runs over, the one named last changes fastest.
Arguments:
- tokens_long: bfloat16 [16, 960, 768], P('batch', 'blk'), may hold values from -6 to 6
- tokens_mid: bfloat16 [16, 640, 768], P('batch', 'blk'), may hold values from -6 to 6
- tokens_short: bfloat16 [16, 320, 768], P('batch', 'blk'), may hold values from -6 to 6
- lengths_long: int32 [16], P('batch'), may hold values from 641 to 960, as said below
- lengths_mid: int32 [16], P('batch'), may hold values from 321 to 640, as said below
- lengths_short: int32 [16], P('batch'), may hold values from 161 to 320, as said below
- w_query: bfloat16 [768, 768], replicated, may hold values from -0.21875 to 0.21875
- b_query: float32 [768], replicated, may hold values from -1.75 to 1.75
- w_key: bfloat16 [768, 768], replicated, may hold values from -0.21875 to 0.21875
- w_value: bfloat16 [768, 768], replicated, may hold values from -0.21875 to 0.21875
- b_value: float32 [768], replicated, may hold values from -1.75 to 1.75
- w_out: bfloat16 [768, 768], replicated, may hold values from -1.75 to 1.75
- b_out: float32 [768], replicated, may hold values from -1.75 to 1.75
- gain_attn: float32 [768], replicated, may hold values from 0.5 to 1.5
- beta_attn: float32 [768], replicated, may hold values from -1.75 to 1.75
- w_inner: bfloat16 [768, 3072], replicated, may hold values from -0.21875 to 0.21875
- b_inner: float32 [3072], replicated, may hold values from -1.75 to 1.75
- w_outer: bfloat16 [3072, 768], replicated, may hold values from -0.109375 to 0.109375
- b_outer: float32 [768], replicated, may hold values from -1.75 to 1.75
- gain_ffn: float32 [768], replicated, may hold values from 0.5 to 1.5
- beta_ffn: float32 [768], replicated, may hold values from -1.75 to 1.75
- cotangent_long: bfloat16 [16, 960, 768], P('batch', 'blk'), may hold values from -6 to 6
- cotangent_mid: bfloat16 [16, 640, 768], P('batch', 'blk'), may hold values from -6 to 6
- cotangent_short: bfloat16 [16, 320, 768], P('batch', 'blk'), may hold values from -6 to 6
Outputs:
- out_long: bfloat16 [16, 960, 768], P('batch', 'blk')
- out_mid: bfloat16 [16, 640, 768], P('batch', 'blk')
- out_short: bfloat16 [16, 320, 768], P('batch', 'blk')
- grad_long: bfloat16 [16, 960, 768], P('batch', 'blk')
- grad_mid: bfloat16 [16, 640, 768], P('batch', 'blk')
- grad_short: bfloat16 [16, 320, 768], P('batch', 'blk')
- grad_w_query: float32 [768, 768], P('batch')
- grad_b_query: float32 [768], P('batch')
- grad_w_key: float32 [768, 768], P('batch')
- grad_w_value: float32 [768, 768], P('batch')
- grad_b_value: float32 [768], P('batch')
- grad_w_out: float32 [768, 768], P('batch')
- grad_b_out: float32 [768], P('batch')
- grad_gain_attn: float32 [768], P('batch')
- grad_beta_attn: float32 [768], P('batch')
- grad_w_inner: float32 [768, 3072], P('batch')
- grad_b_inner: float32 [3072], P('batch')
- grad_w_outer: float32 [3072, 768], P('batch')
- grad_b_outer: float32 [768], P('batch')
- grad_gain_ffn: float32 [768], P('batch')
- grad_beta_ffn: float32 [768], P('batch')
The draws below stay inside these ranges and needn't reach their ends.
Inputs may be any that keep to these rules, and one draw needn't show every extreme that they name: `lengths_long`: among all 16 pairs, one drawn from the seed has length 960. `lengths_mid`: among all 16 pairs, one drawn from the seed has length 640. `lengths_short`: among all 16 pairs, one drawn from the seed has length 320.
All inputs are finite; a program needn't handle non-finite values.
Results may differ from the reference program's by a relative error of at most 0.017.
Values may be sent and summed in bfloat16 or wider, within the bound.
No kernel may reach another device: no remote copies, remote signals or barrier semaphores. Data moves between devices by JAX's collectives and lax.ppermute only.
A program may use at most 256 MiB of HBM per device.

```python
import jax
import jax.numpy as jnp
from jax import lax

D = 768
HEADS = 12
FF = 3072
LONG = 960
MID = 640
SHORT = 320
C_LONG = 1
C_MID = 1
C_SHORT = 1
PAIRS_LONG = 16
PAIRS_MID = 16
PAIRS_SHORT = 16
N_BATCH = 16


def bucket_lengths(key, count, length, lowest):
    first_key, second_key = jax.random.split(key)
    total = N_BATCH * count
    drawn = jax.random.randint(first_key, (total,), lowest, length + 1)
    chosen = jax.random.randint(second_key, (1,), 0, total)
    slots = jnp.arange(total)
    filled = jnp.where(slots == chosen, length, drawn)
    return filled.astype(jnp.int32)


def draw_lengths_long(key, part):
    key = jax.random.fold_in(key, 7)
    return bucket_lengths(key, C_LONG, LONG, MID + 1)


def draw_lengths_mid(key, part):
    key = jax.random.fold_in(key, 8)
    return bucket_lengths(key, C_MID, MID, SHORT + 1)


def draw_lengths_short(key, part):
    key = jax.random.fold_in(key, 9)
    return bucket_lengths(key, C_SHORT, SHORT, SHORT // 2 + 1)


def steps_of(rng, dims, cuts, smallest, top_value):
    level, own = 1.0, jax.random.fold_in(rng, 6)
    for dim, parts in cuts:
        steps = jnp.exp(jax.random.uniform(jax.random.fold_in(own, dim), (parts,), jnp.float32, smallest / len(cuts), top_value / len(cuts)))
        level = level * jnp.repeat(steps, dims[dim] // parts).reshape([-1 if axis == dim else 1 for axis in range(len(dims))])
    return level


def noise(stream_key, dims, deviation, reach, cuts=(), kind=jnp.bfloat16):
    values = jax.random.normal(stream_key, dims, jnp.float32) * deviation
    if len(cuts) > 0:
        values = steps_of(stream_key, dims, cuts, -0.22, 0.18) * values
    return jnp.clip(values, min=-reach, max=reach).astype(kind)


def setup_inputs(seed: int = 0) -> dict:
    key_of = jax.random.split(jax.random.key(seed), 25)
    tokens_long = noise(key_of[0], (PAIRS_LONG, LONG, D), 1.0, 6.0, ((0, 16), (1, 2)))
    tokens_mid = noise(key_of[1], (PAIRS_MID, MID, D), 1.0, 6.0, ((0, 16), (1, 2)))
    tokens_short = noise(key_of[2], (PAIRS_SHORT, SHORT, D), 1.0, 6.0, ((0, 16), (1, 2)))
    lengths_long = draw_lengths_long(jax.random.fold_in(key_of[24], 71), 0)
    lengths_mid = draw_lengths_mid(jax.random.fold_in(key_of[24], 71), 0)
    lengths_short = draw_lengths_short(jax.random.fold_in(key_of[24], 71), 0)
    w_query = noise(key_of[6], (D, D), D ** -0.5, 0.21875)
    b_query = noise(key_of[7], (D,), 0.3, 1.75, (), jnp.float32)
    w_key = noise(key_of[8], (D, D), D ** -0.5, 0.21875)
    w_value = noise(key_of[9], (D, D), D ** -0.5, 0.21875)
    b_value = noise(key_of[10], (D,), 0.3, 1.75, (), jnp.float32)
    w_out = noise(key_of[11], (D, D), (D // 64) ** -0.5, 1.75)
    b_out = noise(key_of[12], (D,), 0.3, 1.75, (), jnp.float32)
    gain_attn = jnp.clip(1.0 + 0.1 * jax.random.normal(key_of[13], (D,), jnp.float32), 0.5, 1.5)
    beta_attn = noise(key_of[14], (D,), 0.3, 1.75, (), jnp.float32)
    w_inner = noise(key_of[15], (D, FF), D ** -0.5, 0.21875)
    b_inner = noise(key_of[16], (FF,), 0.3, 1.75, (), jnp.float32)
    w_outer = noise(key_of[17], (FF, D), FF ** -0.5, 0.109375)
    b_outer = noise(key_of[18], (D,), 0.3, 1.75, (), jnp.float32)
    gain_ffn = jnp.clip(1.0 + 0.1 * jax.random.normal(key_of[19], (D,), jnp.float32), 0.5, 1.5)
    beta_ffn = noise(key_of[20], (D,), 0.3, 1.75, (), jnp.float32)
    cotangent_long = noise(key_of[21], (PAIRS_LONG, LONG, D), 1.0, 6.0, ((0, 16), (1, 2)))
    cotangent_mid = noise(key_of[22], (PAIRS_MID, MID, D), 1.0, 6.0, ((0, 16), (1, 2)))
    cotangent_short = noise(key_of[23], (PAIRS_SHORT, SHORT, D), 1.0, 6.0, ((0, 16), (1, 2)))
    return dict(tokens_long=tokens_long, tokens_mid=tokens_mid, tokens_short=tokens_short, lengths_long=lengths_long, lengths_mid=lengths_mid, lengths_short=lengths_short, w_query=w_query, b_query=b_query, w_key=w_key, w_value=w_value, b_value=b_value, w_out=w_out, b_out=b_out, gain_attn=gain_attn, beta_attn=beta_attn, w_inner=w_inner, b_inner=b_inner, w_outer=w_outer, b_outer=b_outer, gain_ffn=gain_ffn, beta_ffn=beta_ffn, cotangent_long=cotangent_long, cotangent_mid=cotangent_mid, cotangent_short=cotangent_short)


@jax.custom_vjp
def low(v):
    return lax.optimization_barrier(v.astype(jnp.bfloat16)).astype(jnp.float32)

@jax.custom_vjp
def low_back(v):
    return v

def low_keep(v):
    return (low(v), None)

def low_pass(kept, grad):
    return (grad,)

def back_keep(v):
    return (v, None)

def back_low(kept, grad):
    return (low(grad),)
low.defvjp(low_keep, low_pass)
low_back.defvjp(back_keep, back_low)

def local_norm(field, gain, beta):
    centre = lax.optimization_barrier(jnp.mean(field, axis=-1, keepdims=True))
    centered = field - centre
    spread = lax.optimization_barrier(jnp.mean(centered * centered, axis=-1, keepdims=True))
    return centered * lax.rsqrt(spread + 1e-12) * gain + beta

def attend(query, keys, values, lengths, count, length):
    highest = lax.Precision.HIGHEST
    width = query.shape[1]
    head_size = width // HEADS
    query4 = query.reshape(count, length, HEADS, head_size)
    keys4 = keys.reshape(count, length, HEADS, head_size)
    values4 = values.reshape(count, length, HEADS, head_size)
    raw = head_size ** (-0.5) * jnp.einsum('sqhd,skhd->shqk', query4, keys4, precision=highest)
    valid = jnp.arange(length, dtype=jnp.int32)[None, :] < lengths[:, None]
    scores = low_back(jnp.where(valid[:, None, None, :], raw, -1000000000.0))
    top = lax.optimization_barrier(jnp.max(scores, axis=-1, keepdims=True))
    total = jnp.log(lax.optimization_barrier(jnp.sum(jnp.exp(scores - top), axis=-1, keepdims=True))) + top
    probs = low(jnp.exp(scores - total))
    mixed = jnp.einsum('shqk,skhd->sqhd', probs, values4, precision=highest)
    return mixed.reshape(count * length, width)

def group_forward(fields, bounds, w_query, b_query, w_key, w_value, b_value, w_out, b_out, gain_attn, beta_attn, w_inner, b_inner, w_outer, b_outer, gain_ffn, beta_ffn):
    highest = lax.Precision.HIGHEST
    width = fields[0].shape[2]
    rows = jnp.concatenate([field.reshape(-1, width) for field in fields], 0)
    query = low(low_back(jnp.dot(rows, w_query, precision=highest) + b_query))
    keys = low(low_back(jnp.dot(rows, w_key, precision=highest)))
    values = low(low_back(jnp.dot(rows, w_value, precision=highest) + b_value))
    pieces = []
    offset = 0
    for field, lengths in zip(fields, bounds):
        count, length = (field.shape[0], field.shape[1])
        size = count * length
        pieces.append(attend(query[offset:offset + size], keys[offset:offset + size], values[offset:offset + size], lengths, count, length))
        offset = offset + size
    mixed = low(low_back(jnp.concatenate(pieces, 0)))
    branch = low_back(jnp.dot(mixed, w_out, precision=highest) + b_out)
    first = local_norm(rows + branch, gain_attn, beta_attn)
    inner = low_back(jnp.dot(low(first), w_inner, precision=highest) + b_inner)
    hidden = low(jax.nn.gelu(inner, approximate=False))
    outer = low_back(jnp.dot(hidden, w_outer, precision=highest) + b_outer)
    return local_norm(first + outer, gain_ffn, beta_ffn)

def reference(tokens_long, tokens_mid, tokens_short, lengths_long, lengths_mid, lengths_short, w_query, b_query, w_key, w_value, b_value, w_out, b_out, gain_attn, beta_attn, w_inner, b_inner, w_outer, b_outer, gain_ffn, beta_ffn, cotangent_long, cotangent_mid, cotangent_short):
    params = tuple((a.astype(jnp.float32) for a in (w_query, b_query, w_key, w_value, b_value, w_out, b_out, gain_attn, beta_attn, w_inner, b_inner, w_outer, b_outer, gain_ffn, beta_ffn)))
    long_g = tokens_long.astype(jnp.float32).reshape(N_BATCH, C_LONG, LONG, D)
    mid_g = tokens_mid.astype(jnp.float32).reshape(N_BATCH, C_MID, MID, D)
    short_g = tokens_short.astype(jnp.float32).reshape(N_BATCH, C_SHORT, SHORT, D)
    long_len = lengths_long.reshape(N_BATCH, C_LONG).astype(jnp.int32)
    mid_len = lengths_mid.reshape(N_BATCH, C_MID).astype(jnp.int32)
    short_len = lengths_short.reshape(N_BATCH, C_SHORT).astype(jnp.int32)
    cot_rows = jnp.concatenate([cotangent_long.astype(jnp.float32).reshape(N_BATCH, C_LONG * LONG, D), cotangent_mid.astype(jnp.float32).reshape(N_BATCH, C_MID * MID, D), cotangent_short.astype(jnp.float32).reshape(N_BATCH, C_SHORT * SHORT, D)], 1)
    first_cut = C_LONG * LONG
    second_cut = first_cut + C_MID * MID

    def step(carry, item):
        part_long, part_mid, part_short, len_long, len_mid, len_short, part_cot = item

        def forward(field_long, field_mid, field_short, *weights):
            return group_forward((field_long, field_mid, field_short), (len_long, len_mid, len_short), *weights)
        result, back = jax.vjp(forward, part_long, part_mid, part_short, *params)
        grads = back(part_cot)
        carry = tuple((c + g for c, g in zip(carry, grads[3:])))
        low_result = result.astype(jnp.bfloat16)
        outs = (low_result[:first_cut].reshape(C_LONG, LONG, D), low_result[first_cut:second_cut].reshape(C_MID, MID, D), low_result[second_cut:].reshape(C_SHORT, SHORT, D), grads[0].astype(jnp.bfloat16), grads[1].astype(jnp.bfloat16), grads[2].astype(jnp.bfloat16))
        return (carry, outs)
    zeros = tuple((jnp.zeros(p.shape, jnp.float32) for p in params))
    sums, stacked = lax.scan(step, zeros, (long_g, mid_g, short_g, long_len, mid_len, short_len, cot_rows))
    out_long = stacked[0].reshape(PAIRS_LONG, LONG, D)
    out_mid = stacked[1].reshape(PAIRS_MID, MID, D)
    out_short = stacked[2].reshape(PAIRS_SHORT, SHORT, D)
    grad_long = stacked[3].reshape(PAIRS_LONG, LONG, D)
    grad_mid = stacked[4].reshape(PAIRS_MID, MID, D)
    grad_short = stacked[5].reshape(PAIRS_SHORT, SHORT, D)
    return (out_long, out_mid, out_short, grad_long, grad_mid, grad_short, sums[0], sums[1], sums[2], sums[3], sums[4], sums[5], sums[6], sums[7], sums[8], sums[9], sums[10], sums[11], sums[12], sums[13], sums[14])
```

```python
from functools import partial
from functools import reduce

import jax
import jax.numpy as jnp
from jax import lax
from jax.sharding import PartitionSpec as P

HEADS = 12


def from_behind(shard, axis, by):
    size = lax.axis_size(axis)
    return lax.ppermute(shard, axis, [(i, (i + by) % size) for i in range(size)])


def local_norm(field, gain, beta):
    centre = jnp.mean(field, axis=-1, keepdims=True)
    centered = field - centre
    spread = jnp.mean(centered * centered, axis=-1, keepdims=True)
    return centered * lax.rsqrt(spread + 1e-12) * gain + beta


def inner_product(left, right):
    return lax.dot_general(
        left, right, (((0,), (0,)), ((), ())), preferred_element_type=jnp.float32
    )


def outer_product(left, right):
    return lax.dot_general(
        left, right, (((1,), (1,)), ((), ())), preferred_element_type=jnp.float32
    )


def column_sums(values):
    return jnp.sum(values.astype(jnp.float32), axis=0)


def split_rows(flat, shapes):
    pieces = []
    offset = 0
    for count, local in shapes:
        pieces.append(flat[offset : offset + count * local].reshape(count, local, flat.shape[1]))
        offset = offset + count * local
    return pieces


def fetch_blocks(key_parts, value_parts):
    parts = lax.axis_size("blk")
    mine = lax.axis_index("blk")
    result = [[], [], []]
    for bucket in range(3):
        result[bucket].append((mine, key_parts[bucket], value_parts[bucket]))
    moved = from_behind(
        (key_parts[0], value_parts[0], key_parts[1], value_parts[1], key_parts[2], value_parts[2]),
        "blk",
        1,
    )
    for bucket in range(3):
        result[bucket].append(((mine - 1) % parts, moved[2 * bucket], moved[2 * bucket + 1]))
    return result


def return_grads(key_terms, value_terms):
    owned = [[key_terms[bucket][0], value_terms[bucket][0]] for bucket in range(3)]
    back = (
        from_behind(key_terms[0][1].astype(jnp.bfloat16), "blk", -1).astype(jnp.float32),
        from_behind(value_terms[0][1].astype(jnp.bfloat16), "blk", -1).astype(jnp.float32),
        from_behind(key_terms[1][1].astype(jnp.bfloat16), "blk", -1).astype(jnp.float32),
        from_behind(value_terms[1][1].astype(jnp.bfloat16), "blk", -1).astype(jnp.float32),
        from_behind(key_terms[2][1].astype(jnp.bfloat16), "blk", -1).astype(jnp.float32),
        from_behind(value_terms[2][1].astype(jnp.bfloat16), "blk", -1).astype(jnp.float32),
    )
    for bucket in range(3):
        owned[bucket][0] = owned[bucket][0] + back[2 * bucket]
        owned[bucket][1] = owned[bucket][1] + back[2 * bucket + 1]
    return [(owned[bucket][0], owned[bucket][1]) for bucket in range(3)]


def block_scores(query4, block_keys, owner, lengths, scale):
    count, local, width = block_keys.shape
    keys4 = block_keys.reshape(count, local, HEADS, width // HEADS)
    raw = scale * jnp.einsum("sqhd,skhd->shqk", query4, keys4, preferred_element_type=jnp.float32)
    places = owner * local + jnp.arange(local, dtype=jnp.int32)
    valid = places[None, :] < lengths[:, None]
    return jnp.where(valid[:, None, None, :], raw, -1000000000.0)


def swap(value, axis, bit):
    return lax.ppermute(value, axis, [(i, i ^ bit) for i in range(lax.axis_size(axis))])


def halve(value, remaining, bit):
    axis = remaining.index(bit)
    mine = (lax.axis_index("batch") >> bit) & 1
    send = lax.dynamic_index_in_dim(value, 1 - mine, axis, keepdims=False)
    keep = lax.dynamic_index_in_dim(value, mine, axis, keepdims=False)
    return send, keep


def add_low(keep, came):
    return (keep.astype(jnp.float32) + came.astype(jnp.float32)).astype(keep.dtype)


def scatter_sum(values, orders):
    bits = lax.axis_size("batch").bit_length() - 1
    remaining = [list(range(bits))[::-1] for _ in values]
    values = [value.reshape((2,) * bits + value.shape[1:]) for value in values]
    for step in range(bits):
        halves = [
            halve(value, left, order[step])
            for value, left, order in zip(values, remaining, orders)
        ]
        came = [swap(half[0], "batch", 1 << order[step]) for half, order in zip(halves, orders)]
        values = [add_low(half[1], other) for half, other in zip(halves, came)]
        for left, order in zip(remaining, orders):
            left.remove(order[step])
    return values


def bit_orders():
    bits = lax.axis_size("batch").bit_length() - 1
    last = list(range(3, bits))
    return [[0, 1, 2] + last, [1, 2, 0] + last, [2, 0, 1] + last]


def core_half(value, which):
    half = value.shape[-1] // 2
    return lax.dynamic_slice_in_dim(value, which * half, half, value.ndim - 1)


def reduce_grads(matrices, vectors):
    n = lax.axis_size("batch")
    core = lax.axis_index("blk")
    width = matrices[0].shape[1]
    rows = width // n
    blocks = []
    for matrix in matrices:
        low = matrix.astype(jnp.bfloat16)
        if matrix.shape[0] > width:
            times = matrix.shape[0] // width
            low = low.reshape(n, times, rows, width).swapaxes(1, 2)
        blocks.append(low.reshape(n, rows, -1))
    kept, sent = [
        jnp.concatenate([core_half(block, which) for block in blocks], -1)
        for which in (core, 1 - core)
    ]
    whole = add_low(kept, swap(sent, "blk", 1))
    small = jnp.concatenate([vector.reshape(n, -1) for vector in vectors], 1)
    small = small + swap(small, "blk", 1)
    *parts, small = scatter_sum(
        [*jnp.split(whole, 3, -1), small[:, None, :]], bit_orders() + bit_orders()[:1]
    )
    mine = jnp.concatenate(parts, -1)
    other = swap(mine, "blk", 1)
    low = jnp.where(core == 0, mine, other).astype(jnp.float32)
    high = jnp.where(core == 0, other, mine).astype(jnp.float32)
    results = []
    offset = 0
    for matrix, block in zip(matrices, blocks):
        size = block.shape[-1] // 2
        result = jnp.concatenate(
            [low[:, offset : offset + size], high[:, offset : offset + size]], 1
        )
        if matrix.shape[0] > width:
            result = result.reshape(rows, -1, width).swapaxes(0, 1).reshape(-1, width)
        results.append(result)
        offset += size
    offset = 0
    for vector in vectors:
        size = vector.shape[0] // n
        results.append(small[0, offset : offset + size])
        offset += size
    w_query, w_key, w_value, w_out, w_inner, w_outer = results[:6]
    b_query, b_value, b_out, gain_attn, beta_attn, b_inner, b_outer, gain_ffn, beta_ffn = results[6:]
    return (
        w_query, b_query, w_key, w_value, b_value, w_out, b_out, gain_attn, beta_attn,
        w_inner, b_inner, w_outer, b_outer, gain_ffn, beta_ffn,
    )


def per_device(
    tokens_long,
    tokens_mid,
    tokens_short,
    lengths_long,
    lengths_mid,
    lengths_short,
    w_query,
    b_query,
    w_key,
    w_value,
    b_value,
    w_out,
    b_out,
    gain_attn,
    beta_attn,
    w_inner,
    b_inner,
    w_outer,
    b_outer,
    gain_ffn,
    beta_ffn,
    cotangent_long,
    cotangent_mid,
    cotangent_short,
):
    fields = (tokens_long, tokens_mid, tokens_short)
    bounds = (lengths_long, lengths_mid, lengths_short)
    width = tokens_long.shape[2]
    head_size = width // HEADS
    scale = head_size ** (-0.5)
    shapes = [(field.shape[0], field.shape[1]) for field in fields]
    rows = jnp.concatenate([field.reshape(-1, width) for field in fields], 0)
    query = (jnp.dot(rows, w_query, preferred_element_type=jnp.float32) + b_query).astype(
        jnp.bfloat16
    )
    keys = jnp.dot(rows, w_key, preferred_element_type=jnp.float32).astype(jnp.bfloat16)
    values = (jnp.dot(rows, w_value, preferred_element_type=jnp.float32) + b_value).astype(
        jnp.bfloat16
    )
    query_parts = split_rows(query, shapes)
    key_parts = split_rows(keys, shapes)
    value_parts = split_rows(values, shapes)
    query_heads = [
        part.reshape(part.shape[0], part.shape[1], HEADS, head_size) for part in query_parts
    ]
    blocks = fetch_blocks(key_parts, value_parts)
    totals = []
    mixed_parts = []
    for bucket in range(3):
        count, local = shapes[bucket]
        scores = [
            block_scores(query_heads[bucket], block_keys, owner, bounds[bucket], scale)
            for owner, block_keys, block_values in blocks[bucket]
        ]
        top = reduce(jnp.maximum, [jnp.max(block, axis=-1, keepdims=True) for block in scores])
        total = (
            jnp.log(
                reduce(
                    jnp.add,
                    [jnp.sum(jnp.exp(block - top), axis=-1, keepdims=True) for block in scores],
                )
            )
            + top
        )
        attended = jnp.zeros((count, local, HEADS, head_size), jnp.float32)
        for (owner, block_keys, block_values), block in zip(blocks[bucket], scores):
            weights = jnp.exp(block - total).astype(jnp.bfloat16)
            attended = attended + jnp.einsum(
                "shqk,skhd->sqhd",
                weights,
                block_values.reshape(count, local, HEADS, head_size),
                preferred_element_type=jnp.float32,
            )
        totals.append(total)
        mixed_parts.append(attended.reshape(count * local, width))
    mixed = jnp.concatenate(mixed_parts, 0).astype(jnp.bfloat16)
    first_sum = (
        rows.astype(jnp.float32) + jnp.dot(mixed, w_out, preferred_element_type=jnp.float32) + b_out
    )
    first, first_back = jax.vjp(local_norm, first_sum, gain_attn, beta_attn)
    first_low = first.astype(jnp.bfloat16)
    inner = jnp.dot(first_low, w_inner, preferred_element_type=jnp.float32) + b_inner
    activated, gelu_back = jax.vjp(partial(jax.nn.gelu, approximate=False), inner)
    hidden = activated.astype(jnp.bfloat16)
    second_sum = first + jnp.dot(hidden, w_outer, preferred_element_type=jnp.float32) + b_outer
    normed, second_back = jax.vjp(local_norm, second_sum, gain_ffn, beta_ffn)
    out_parts = split_rows(normed.astype(jnp.bfloat16), shapes)
    grad_rows = jnp.concatenate(
        [cot.reshape(-1, width) for cot in (cotangent_long, cotangent_mid, cotangent_short)], 0
    ).astype(jnp.float32)
    grad_second, grad_gain_ffn, grad_beta_ffn = second_back(grad_rows)
    grad_outer_low = grad_second.astype(jnp.bfloat16)
    grad_w_outer = inner_product(hidden, grad_outer_low)
    grad_b_outer = column_sums(grad_outer_low)
    grad_hidden = outer_product(grad_outer_low, w_outer)
    grad_inner = gelu_back(grad_hidden)[0].astype(jnp.bfloat16)
    grad_w_inner = inner_product(first_low, grad_inner)
    grad_b_inner = column_sums(grad_inner)
    grad_first = outer_product(grad_inner, w_inner) + grad_second
    grad_first_sum, grad_gain_attn, grad_beta_attn = first_back(grad_first)
    grad_branch = grad_first_sum.astype(jnp.bfloat16)
    grad_w_out = inner_product(mixed, grad_branch)
    grad_b_out = column_sums(grad_branch)
    grad_mixed = outer_product(grad_branch, w_out).astype(jnp.bfloat16)
    grad_mixed_parts = split_rows(grad_mixed, shapes)
    blocks = fetch_blocks(key_parts, value_parts)
    query_terms = []
    key_terms = [[], [], []]
    value_terms = [[], [], []]
    for bucket in range(3):
        count, local = shapes[bucket]
        grad_heads = grad_mixed_parts[bucket].reshape(count, local, HEADS, head_size)
        probs = []
        grad_probs = []
        for owner, block_keys, block_values in blocks[bucket]:
            block = block_scores(query_heads[bucket], block_keys, owner, bounds[bucket], scale)
            probs.append(jnp.exp(block - totals[bucket]))
            grad_probs.append(
                jnp.einsum(
                    "sqhd,skhd->shqk",
                    grad_heads,
                    block_values.reshape(count, local, HEADS, head_size),
                    preferred_element_type=jnp.float32,
                )
            )
        delta = reduce(
            jnp.add,
            [jnp.sum(prob * grad, axis=-1, keepdims=True) for prob, grad in zip(probs, grad_probs)],
        )
        grad_query = jnp.zeros((count, local, HEADS, head_size), jnp.float32)
        for (owner, block_keys, block_values), prob, grad in zip(blocks[bucket], probs, grad_probs):
            grad_scores = (prob * (grad - delta)).astype(jnp.bfloat16)
            keys4 = block_keys.reshape(count, local, HEADS, head_size)
            grad_query = grad_query + scale * jnp.einsum(
                "shqk,skhd->sqhd", grad_scores, keys4, preferred_element_type=jnp.float32
            )
            key_terms[bucket].append(
                (
                    scale
                    * jnp.einsum(
                        "shqk,sqhd->skhd",
                        grad_scores,
                        query_heads[bucket],
                        preferred_element_type=jnp.float32,
                    )
                ).reshape(count, local, width)
            )
            value_terms[bucket].append(
                jnp.einsum(
                    "shqk,sqhd->skhd",
                    prob.astype(jnp.bfloat16),
                    grad_heads,
                    preferred_element_type=jnp.float32,
                ).reshape(count, local, width)
            )
        query_terms.append(grad_query.reshape(count * local, width))
    owned = return_grads(key_terms, value_terms)
    query_low = jnp.concatenate(query_terms, 0).astype(jnp.bfloat16)
    keys_low = jnp.concatenate([pair[0].reshape(-1, width) for pair in owned], 0).astype(
        jnp.bfloat16
    )
    values_low = jnp.concatenate([pair[1].reshape(-1, width) for pair in owned], 0).astype(
        jnp.bfloat16
    )
    grad_w_query = inner_product(rows, query_low)
    grad_b_query = column_sums(query_low)
    grad_w_key = inner_product(rows, keys_low)
    grad_w_value = inner_product(rows, values_low)
    grad_b_value = column_sums(values_low)
    grad_input = (
        grad_first_sum
        + outer_product(query_low, w_query)
        + outer_product(keys_low, w_key)
        + outer_product(values_low, w_value)
    ).astype(jnp.bfloat16)
    grad_parts = split_rows(grad_input, shapes)
    summed = reduce_grads(
        (grad_w_query, grad_w_key, grad_w_value, grad_w_out, grad_w_inner, grad_w_outer),
        (
            grad_b_query,
            grad_b_value,
            grad_b_out,
            grad_gain_attn,
            grad_beta_attn,
            grad_b_inner,
            grad_b_outer,
            grad_gain_ffn,
            grad_beta_ffn,
        ),
    )
    return (*out_parts, *grad_parts, *summed)


def solution(mesh):
    in_specs = (
        P("batch", "blk", None),
        P("batch", "blk", None),
        P("batch", "blk", None),
        P("batch"),
        P("batch"),
        P("batch"),
        P(),
        P(),
        P(),
        P(),
        P(),
        P(),
        P(),
        P(),
        P(),
        P(),
        P(),
        P(),
        P(),
        P(),
        P(),
        P("batch", "blk", None),
        P("batch", "blk", None),
        P("batch", "blk", None),
    )
    out_specs = (
        P("batch", "blk", None),
        P("batch", "blk", None),
        P("batch", "blk", None),
        P("batch", "blk", None),
        P("batch", "blk", None),
        P("batch", "blk", None),
        P("batch", None),
        P("batch"),
        P("batch", None),
        P("batch", None),
        P("batch"),
        P("batch", None),
        P("batch"),
        P("batch"),
        P("batch"),
        P("batch", None),
        P("batch"),
        P("batch", None),
        P("batch"),
        P("batch"),
        P("batch"),
    )
    return jax.shard_map(
        per_device, mesh=mesh, in_specs=in_specs, out_specs=out_specs, check_vma=False
    )
```

```python
from functools import partial

import jax
import jax.numpy as jnp
from jax import lax
from jax.experimental import pallas as pl
from jax.experimental.pallas import tpu as pltpu
from jax.sharding import PartitionSpec as P

HEADS = 12
LANES = 128
NT = (((1,), (1,)), ((), ()))
TN = (((0,), (0,)), ((), ()))
LOG2E = 1.4426950408889634
CHUNK = 512
LIMIT = 58 * 1024 * 1024
ANY = pl.BlockSpec(memory_space=pl.ANY)


def cost(flops):
    return pl.CostEstimate(flops=flops, bytes_accessed=20_000_000, transcendentals=0)


def shapes(*items):
    return [jax.ShapeDtypeStruct(shape, dtype) for shape, dtype in items]


def sum_rows(field):
    return jnp.sum(field, axis=0, keepdims=True)


def dot(left, right, dims=(((1,), (0,)), ((), ()))):
    return lax.dot_general(left, right, dims, preferred_element_type=jnp.float32)


def split_low(value):
    high = value.astype(jnp.bfloat16).astype(jnp.float32)
    rest = value - high
    middle = rest.astype(jnp.bfloat16).astype(jnp.float32)
    return high, middle, rest - middle


def lane_ids(rows):
    return lax.broadcasted_iota(jnp.int32, (rows, LANES), 1)


def pick_head(block, head):
    lanes = lane_ids(block.shape[0])
    half = LANES // 2
    keep = (lanes < half) if head == 0 else (lanes >= half)
    return jnp.where(keep, block.astype(jnp.float32), 0.0).astype(jnp.bfloat16)


def pick_extra(block, head):
    lanes = lane_ids(block.shape[0])
    keep = (lanes == 0) | ((lanes >= 1 + 3 * head) & (lanes < 4 + 3 * head))
    return jnp.where(keep, block.astype(jnp.float32), 0.0).astype(jnp.bfloat16)


def place_extra(first, pieces):
    lanes = lane_ids(pieces[0].shape[0])
    block = jnp.where(lanes == 0, first, 0.0)
    for place, piece in enumerate(pieces):
        block = jnp.where(lanes == 1 + place, piece, block)
    return block.astype(jnp.bfloat16)


def fill_extra(locals_, scalars, extra):
    core = scalars[3]
    offset = 0
    for bucket, local in enumerate(locals_):
        length = scalars[bucket]
        for half in range(2):
            owner = core if half == 0 else 1 - core
            lanes = lane_ids(local)
            places = lax.broadcasted_iota(jnp.int32, (local, LANES), 0) + owner * local
            bias = jnp.where(places < length, 0.0, -1e9)
            block = jnp.where(lanes == 0, bias, jnp.where(lanes < 7, 1.0, 0.0))
            extra[pl.ds(offset, local), :] = block.astype(jnp.bfloat16)
            offset += local


def forward_kernel(locals_, scalars, x_long, x_mid, x_short, y_long, y_mid, y_short,
                   w_query, w_key, w_value, b_query, b_value,
                   qa_out, keys_out, values_out, mixed_out, x_out,
                   x, extra, sems):
    group = pl.program_id(0)

    @pl.when(group == 0)
    def _():
        copies = []
        offset = 0
        for bucket, (mine, other) in enumerate(((x_long, y_long), (x_mid, y_mid), (x_short, y_short))):
            local = locals_[bucket]
            for half, ref in enumerate((mine, other)):
                copy = pltpu.make_async_copy(ref.at[0], x.at[pl.ds(offset, local)], sems.at[2 * bucket + half])
                copy.start()
                copies.append(copy)
                offset += local
        fill_extra(locals_, scalars, extra)
        for copy in copies:
            copy.wait()
        x_out[...] = x[...]

    w_pair = jnp.concatenate([w_key[...], w_value[...]], 1)
    both = dot(x[...], w_pair)
    keys = both[:, :LANES].astype(jnp.bfloat16)
    values = (both[:, LANES:] + b_value[...]).astype(jnp.bfloat16)
    keys_out[...] = keys
    values_out[...] = values
    key_rows = 0
    rows = 0
    for local in locals_:
        total_keys = 2 * local
        ks = slice(key_rows, key_rows + total_keys)
        query = ((dot(x[pl.ds(key_rows, local), :], w_query[...]) + b_query[...]) * (0.125 * LOG2E)).astype(jnp.bfloat16)
        one = jnp.where(lane_ids(local) == 0, 1.0, 0.0).astype(jnp.bfloat16)
        key_block = jnp.concatenate([keys[ks], extra[pl.ds(key_rows, total_keys), :]], 1)
        ones = jnp.ones((total_keys, LANES), jnp.bfloat16)
        mixed = None
        pieces = []
        for head in range(2):
            scores = dot(jnp.concatenate([pick_head(query, head), one], 1), key_block, NT)
            top = jnp.max(scores, axis=-1, keepdims=True)
            weights = jnp.exp2(scores - top).astype(jnp.bfloat16)
            found = dot(weights, jnp.concatenate([pick_head(values[ks], head), ones], 1))
            bulk = found[:, LANES:]
            part = found[:, :LANES] / bulk
            mixed = part if mixed is None else mixed + part
            pieces.extend(split_low(-(top + jnp.log2(bulk))))
        mixed_out[pl.ds(rows, local), :] = mixed.astype(jnp.bfloat16)
        qa_out[pl.ds(rows, local), :] = jnp.concatenate([query, place_extra(1.0, pieces)], 1)
        key_rows += total_keys
        rows += local


def attend_forward(scalars, mine, others, w_query, w_key, w_value, b_query, b_value):
    locals_ = tuple(part.shape[1] for part in mine)
    rows = sum(locals_)
    width = w_query.shape[0]
    groups = width // LANES
    low = jnp.bfloat16
    column = pl.BlockSpec((width, LANES), lambda g: (0, g))
    bias = pl.BlockSpec((1, LANES), lambda g: (0, g))
    anywhere = pl.BlockSpec(memory_space=pl.ANY)
    return pl.pallas_call(
        partial(forward_kernel, locals_),
        grid=(groups,),
        in_specs=[pl.BlockSpec(memory_space=pltpu.SMEM)] + [anywhere] * 6 + [column] * 3 + [bias] * 2,
        out_specs=[
            pl.BlockSpec((rows, 2 * LANES), lambda g: (0, g)),
            pl.BlockSpec((2 * rows, LANES), lambda g: (0, g)),
            pl.BlockSpec((2 * rows, LANES), lambda g: (0, g)),
            pl.BlockSpec((rows, LANES), lambda g: (0, g)),
            pl.BlockSpec((2 * rows, width), lambda g: (0, 0)),
        ],
        out_shape=[
            jax.ShapeDtypeStruct((rows, 2 * width), low),
            jax.ShapeDtypeStruct((2 * rows, width), low),
            jax.ShapeDtypeStruct((2 * rows, width), low),
            jax.ShapeDtypeStruct((rows, width), low),
            jax.ShapeDtypeStruct((2 * rows, width), low),
        ],
        scratch_shapes=[
            pltpu.VMEM((2 * rows, width), low),
            pltpu.VMEM((2 * rows, LANES), low),
            pltpu.SemaphoreType.DMA((6,)),
        ],
        compiler_params=pltpu.CompilerParams(vmem_limit_bytes=LIMIT),
        cost_estimate=cost(30_000_000_000),
        name="attend_forward",
    )(scalars, *mine, *others, w_query, w_key, w_value, b_query.reshape(1, -1), b_value.reshape(1, -1))


def backward_kernel(locals_, scalars, qa, keys, values, mixed, grad_mixed, x,
                    grad_query, grad_keys, grad_values, grad_w, grad_b, extra):
    @pl.when(pl.program_id(0) == 0)
    def _():
        fill_extra(locals_, scalars, extra)

    key_rows = 0
    rows = 0
    for local in locals_:
        total_keys = 2 * local
        ks = pl.ds(key_rows, total_keys)
        qs = pl.ds(rows, local)
        query = qa[qs, :LANES]
        more = qa[qs, LANES:]
        cot = grad_mixed[qs, :]
        product = cot.astype(jnp.float32) * mixed[qs, :].astype(jnp.float32)
        lanes = lane_ids(local)
        pieces = []
        for head in range(2):
            keep = (lanes < 64) if head == 0 else (lanes >= 64)
            delta = jnp.sum(jnp.where(keep, product, 0.0), axis=-1, keepdims=True)
            pieces.extend(split_low(-jnp.broadcast_to(delta, (local, LANES))))
        cot_more = place_extra(0.0, pieces)
        key = keys[ks, :]
        marks = extra[ks, :]
        key_block = jnp.concatenate([key, marks], 1)
        value_block = jnp.concatenate([values[ks, :], marks], 1)
        sums = [None, None, None]
        for head in range(2):
            query_one = pick_head(query, head)
            cot_one = pick_head(cot, head)
            probs = jnp.exp2(dot(key_block, jnp.concatenate([query_one, pick_extra(more, head)], 1), NT))
            change = dot(value_block, jnp.concatenate([cot_one, pick_extra(cot_more, head)], 1), NT)
            grad_scores = (probs * change).astype(jnp.bfloat16)
            terms = (
                dot(grad_scores, pick_head(key, head), TN),
                dot(grad_scores, query_one),
                dot(probs.astype(jnp.bfloat16), cot_one),
            )
            sums = [term if old is None else old + term for old, term in zip(sums, terms)]
        grad_query[qs, :] = (sums[0] * 0.125).astype(jnp.bfloat16)
        grad_keys[ks, :] = (sums[1] * (1.0 / LOG2E)).astype(jnp.bfloat16)
        grad_values[ks, :] = sums[2].astype(jnp.bfloat16)
        key_rows += total_keys
        rows += local
    pair = jnp.concatenate([grad_keys[...], grad_values[...]], 1)
    both = dot(x[...], pair, TN)
    grad_w[0, 1] = both[:, :LANES].astype(jnp.bfloat16)
    grad_w[0, 2] = both[:, LANES:].astype(jnp.bfloat16)
    key_rows = 0
    rows = 0
    total = None
    for local in locals_:
        term = dot(x[pl.ds(key_rows, local), :], grad_query[pl.ds(rows, local), :], TN)
        total = term if total is None else total + term
        key_rows += 2 * local
        rows += local
    grad_w[0, 0] = total.astype(jnp.bfloat16)
    grad_b[0:1, :] = sum_rows(grad_query[...].astype(jnp.float32))
    grad_b[1:2, :] = sum_rows(grad_values[...].astype(jnp.float32))


def attend_backward(scalars, locals_, qa, keys, values, mixed, grad_mixed, x, first, count):
    rows = sum(locals_)
    width = x.shape[1]
    low = jnp.bfloat16

    def col(n, w=LANES):
        return pl.BlockSpec((n, w), lambda g, s: (0, g + first))

    def out(n):
        return pl.BlockSpec((n, LANES), lambda g, s: (0, g))

    return pl.pallas_call(
        partial(backward_kernel, locals_),
        grid_spec=pltpu.PrefetchScalarGridSpec(
            num_scalar_prefetch=1,
            grid=(count,),
            in_specs=[col(rows, 2 * LANES), col(2 * rows), col(2 * rows), col(rows), col(rows),
                      pl.BlockSpec((2 * rows, width), lambda g, s: (0, 0))],
            out_specs=[out(rows), out(2 * rows), out(2 * rows),
                       pl.BlockSpec((1, 3, width, LANES), lambda g, s: ((g + s[3]) % 2, 0, 0, 0)), out(8)],
            scratch_shapes=[pltpu.VMEM((2 * rows, LANES), low)],
        ),
        out_shape=shapes(
            ((rows, LANES * count), low), ((2 * rows, LANES * count), low), ((2 * rows, LANES * count), low),
            ((2, 3, width, LANES), low), ((8, LANES * count), jnp.float32),
        ),
        compiler_params=pltpu.CompilerParams(vmem_limit_bytes=LIMIT),
        cost_estimate=cost(count * 6_000_000_000),
        name="attend_backward",
    )(scalars, qa, keys, values, mixed, grad_mixed, x)


def gelu_and_slope(inner):
    size = jnp.abs(inner)
    bell = jnp.exp2(inner * inner * (-0.5 * LOG2E))
    t = 1.0 / (1.0 + (0.3275911 * 0.7071067811865476) * size)
    series = 0.5 * 1.061405429
    for term in (-0.5 * 1.453152027, 0.5 * 1.421413741, -0.5 * 0.284496736, 0.5 * 0.254829592):
        series = series * t + term
    tail = series * t * bell
    share = jnp.where(inner >= 0.0, 1.0 - tail, tail)
    return inner * share, share + inner * bell * 0.3989422804014327


def mean_of(field):
    return jnp.sum(field, axis=-1, keepdims=True) * (1.0 / field.shape[-1])


def normalize(field):
    centered = field - mean_of(field)
    inverse = lax.rsqrt(mean_of(centered * centered) + 1e-12)
    return centered * inverse, inverse


def norm_back(grad, normed, inverse):
    return inverse * (grad - mean_of(grad) - normed * mean_of(grad * normed))


def store_halves(core, keep, send, low, high):
    first = core == 0
    keep[...] = jnp.where(first, low, high).astype(keep.dtype)
    send[...] = jnp.where(first, high, low).astype(send.dtype)


def start_copies(pairs, sems):
    copies = [pltpu.make_async_copy(src, dst, sems.at[i]) for i, (src, dst) in enumerate(pairs)]
    for copy in copies:
        copy.start()
    return copies


def ffn_forward_kernel(blocks, scalars, mixed, tok_long, tok_mid, tok_short, cot_long, cot_mid, cot_short,
                       w_out, b_out, gain_attn, beta_attn, w_inner, b_inner, w_outer, b_outer, gain_ffn, beta_ffn,
                       out_long, out_mid, out_short, normed1, inverse1, slope, grad_outer, grad_second,
                       vectors, keep_all, send_all,
                       w_out_s, w_inner_s, w_outer_s, hidden_s, sems):
    width, inner_width = w_inner.shape
    chunks = inner_width // CHUNK
    pairs = [(w_out, w_out_s)]
    for j in range(chunks):
        cs = pl.ds(j * CHUNK, CHUNK)
        pairs.append((w_inner.at[:, cs], w_inner_s.at[:, cs]))
        pairs.append((w_outer.at[cs, :], w_outer_s.at[cs, :]))
    copies = start_copies(pairs, sems)
    toks = ((tok_long,), (tok_mid, tok_short))
    cots = ((cot_long,), (cot_mid, cot_short))
    outs = ((out_long,), (out_mid, out_short))
    join = lambda refs: jnp.concatenate([ref[0] for ref in refs], 0).astype(jnp.float32)
    start = 0
    sums = []
    for block, rows in enumerate(blocks):
        rs = pl.ds(start, rows)
        if block == 0:
            copies[0].wait()
        field = join(toks[block]) + dot(mixed[rs, :], w_out_s[...]) + b_out[...]
        n1, r1 = normalize(field)
        normed1[rs, :] = n1
        inverse1[rs, :] = jnp.broadcast_to(r1, (rows, LANES))
        first = n1 * gain_attn[...] + beta_attn[...]
        first_low = first.astype(jnp.bfloat16)
        total = first + b_outer[...]
        for j in range(chunks):
            cs = pl.ds(j * CHUNK, CHUNK)
            if block == 0:
                copies[1 + 2 * j].wait()
                copies[2 + 2 * j].wait()
            inner = dot(first_low, w_inner_s[:, cs]) + b_inner[:, cs]
            value, rate = gelu_and_slope(inner)
            hidden = value.astype(jnp.bfloat16)
            hidden_s[rs, cs] = hidden
            slope[rs, cs] = rate.astype(jnp.bfloat16)
            total = total + dot(hidden, w_outer_s[cs, :])
        n2, r2 = normalize(total)
        result = (n2 * gain_ffn[...] + beta_ffn[...]).astype(jnp.bfloat16)
        at = 0
        for ref in outs[block]:
            size = ref.shape[1]
            ref[0] = result[at : at + size]
            at += size
        cot = join(cots[block])
        back = norm_back(cot * gain_ffn[...], n2, r2)
        grad_second[rs, :] = back
        low = back.astype(jnp.bfloat16)
        grad_outer[rs, :] = low
        sums.append((sum_rows(cot * n2), sum_rows(cot), sum_rows(low.astype(jnp.float32))))
        start += rows
    for i in range(3):
        vectors[pl.ds(i, 1), :] = sums[0][i] + sums[1][i]
    core = scalars[3]
    half = width // 2
    for p in range(3):
        keep, send = keep_all.at[p], send_all.at[p]
        pair = jnp.concatenate(
            [grad_outer[:, pl.ds(p * LANES, LANES)], grad_outer[:, pl.ds(half + p * LANES, LANES)]], 1
        )
        for j in range(chunks):
            cs = pl.ds(j * CHUNK, CHUNK)
            both = dot(hidden_s[:, cs], pair, TN)
            store_halves(core, keep.at[cs, :], send.at[cs, :], both[:, :LANES], both[:, LANES:])


def ffn_forward(scalars, mixed, toks, cots, w_out, b_out, gain_attn, beta_attn, w_inner, b_inner, w_outer, b_outer, gain_ffn, beta_ffn):
    rows, width = mixed.shape
    inner_width = w_inner.shape[1]
    low, full = jnp.bfloat16, jnp.float32
    blocks = (toks[0].shape[1], toks[1].shape[1] + toks[2].shape[1])
    row = lambda v: v.reshape(1, -1)
    vm = pl.BlockSpec(memory_space=pltpu.VMEM)
    copies = 1 + 2 * (inner_width // CHUNK)
    return pl.pallas_call(
        partial(ffn_forward_kernel, blocks),
        in_specs=[pl.BlockSpec(memory_space=pltpu.SMEM)] + [vm] * 7
        + [ANY, vm, vm, vm, ANY, vm, ANY, vm, vm, vm],
        out_specs=[vm] * 11,
        out_shape=shapes(
            *[(tok.shape, low) for tok in toks],
            ((rows, width), full), ((rows, LANES), full), ((rows, inner_width), low),
            ((rows, width), low), ((rows, width), full), ((8, width), full),
            *[((3, inner_width, LANES), low)] * 2,
        ),
        scratch_shapes=[
            pltpu.VMEM(w_out.shape, low), pltpu.VMEM(w_inner.shape, low), pltpu.VMEM(w_outer.shape, low),
            pltpu.VMEM((rows, inner_width), low), pltpu.SemaphoreType.DMA((copies,)),
        ],
        compiler_params=pltpu.CompilerParams(vmem_limit_bytes=LIMIT),
        cost_estimate=cost(30_000_000_000),
        name="ffn_forward",
    )(scalars, mixed, *toks, *cots, w_out, row(b_out), row(gain_attn), row(beta_attn), w_inner, row(b_inner),
      w_outer, row(b_outer), row(gain_ffn), row(beta_ffn))


def ffn_backward_kernel(blocks, scalars, mixed, normed1, inverse1, slope, grad_outer, grad_second,
                        w_out, gain_attn, beta_attn, w_inner, w_outer,
                        grad_sum, grad_mixed, vectors, bias_inner,
                        keep_all, send_all, keep_out, send_out,
                        w_out_s, w_inner_s, w_outer_s, first_s, inner_s, branch_s, sems):
    width, inner_width = w_inner.shape
    chunks = inner_width // CHUNK
    pairs = []
    for j in range(chunks):
        cs = pl.ds(j * CHUNK, CHUNK)
        pairs.append((w_outer.at[cs, :], w_outer_s.at[cs, :]))
        pairs.append((w_inner.at[:, cs], w_inner_s.at[:, cs]))
    pairs.append((w_out, w_out_s))
    copies = start_copies(pairs, sems)
    start = 0
    sums = []
    biases = [None] * chunks
    for block, rows in enumerate(blocks):
        rs = pl.ds(start, rows)
        total = grad_second[rs, :]
        cot = grad_outer[rs, :]
        for j in range(chunks):
            cs = pl.ds(j * CHUNK, CHUNK)
            if block == 0:
                copies[2 * j].wait()
                copies[2 * j + 1].wait()
            change = dot(cot, w_outer_s[cs, :], NT) * slope[rs, cs].astype(jnp.float32)
            low = change.astype(jnp.bfloat16)
            inner_s[rs, cs] = low
            term = sum_rows(low.astype(jnp.float32))
            biases[j] = term if block == 0 else biases[j] + term
            total = total + dot(low, w_inner_s[:, cs], NT)
        n1 = normed1[rs, :]
        first_s[rs, :] = (n1 * gain_attn[...] + beta_attn[...]).astype(jnp.bfloat16)
        back = norm_back(total * gain_attn[...], n1, inverse1[rs, :][:, :1])
        grad_sum[rs, :] = back
        low = back.astype(jnp.bfloat16)
        branch_s[rs, :] = low
        sums.append((sum_rows(total * n1), sum_rows(total), sum_rows(low.astype(jnp.float32))))
        if block == 0:
            copies[2 * chunks].wait()
        grad_mixed[rs, :] = dot(low, w_out_s[...], NT).astype(jnp.bfloat16)
        start += rows
    for i in range(3):
        vectors[pl.ds(i, 1), :] = sums[0][i] + sums[1][i]
    for j in range(chunks):
        bias_inner[:, pl.ds(j * CHUNK, CHUNK)] = biases[j]
    core = scalars[3]
    half = inner_width // 2
    part = half // 3
    first_low = first_s[...]
    for p in range(3):
        keep, send = keep_all.at[p], send_all.at[p]
        for q in range(part // 256):
            at = p * part + q * 256
            low = dot(first_low, inner_s[:, pl.ds(at, 256)], TN)
            high = dot(first_low, inner_s[:, pl.ds(half + at, 256)], TN)
            cs = pl.ds(q * 256, 256)
            store_halves(core, keep.at[:, cs], send.at[:, cs], low, high)
    half = width // 2
    for p in range(3):
        cs = pl.ds(p * LANES, LANES)
        pair = jnp.concatenate([branch_s[:, cs], branch_s[:, pl.ds(half + p * LANES, LANES)]], 1)
        both = dot(mixed[...], pair, TN)
        store_halves(core, keep_out.at[p], send_out.at[p], both[:, :LANES], both[:, LANES:])


def ffn_backward(scalars, blocks, mixed, normed1, inverse1, slope, grad_outer, grad_second, w_out, gain_attn, beta_attn, w_inner, w_outer):
    rows, width = mixed.shape
    inner_width = w_inner.shape[1]
    low, full = jnp.bfloat16, jnp.float32
    row = lambda v: v.reshape(1, -1)
    vm = pl.BlockSpec(memory_space=pltpu.VMEM)
    copies = 1 + 2 * (inner_width // CHUNK)
    return pl.pallas_call(
        partial(ffn_backward_kernel, blocks),
        in_specs=[pl.BlockSpec(memory_space=pltpu.SMEM)] + [vm] * 6 + [ANY, vm, vm, ANY, ANY],
        out_specs=[vm] * 8,
        out_shape=shapes(
            ((rows, width), full), ((rows, width), low), ((8, width), full), ((1, inner_width), full),
            *[((3, width, inner_width // 6), low)] * 2, *[((3, width, LANES), low)] * 2,
        ),
        scratch_shapes=[
            pltpu.VMEM(w_out.shape, low), pltpu.VMEM(w_inner.shape, low), pltpu.VMEM(w_outer.shape, low),
            pltpu.VMEM((rows, width), low), pltpu.VMEM((rows, inner_width), low), pltpu.VMEM((rows, width), low),
            pltpu.SemaphoreType.DMA((copies,)),
        ],
        compiler_params=pltpu.CompilerParams(vmem_limit_bytes=LIMIT),
        cost_estimate=cost(30_000_000_000),
        name="ffn_backward",
    )(scalars, mixed, normed1, inverse1, slope, grad_outer, grad_second, w_out, row(gain_attn), row(beta_attn), w_inner, w_outer)


def input_kernel(locals_, grad_sum, w_query, w_key, w_value, *refs):
    pieces = (len(refs) - 2) // 3
    queries, keys, values = refs[:pieces], refs[pieces : 2 * pieces], refs[2 * pieces : 3 * pieces]
    own, send = refs[3 * pieces :]
    join = lambda parts, rows: jnp.concatenate([part[rows, :] for part in parts], 1)
    start = 0
    for local in locals_:
        rs = pl.ds(start, local)
        for half in range(2):
            ks = pl.ds(2 * start + half * local, local)
            total = dot(join(keys, ks), w_key[...], NT) + dot(join(values, ks), w_value[...], NT)
            if half == 0:
                own[rs, :] = grad_sum[rs, :] + total + dot(join(queries, rs), w_query[...], NT)
            else:
                send[rs, :] = total.astype(jnp.bfloat16)
        start += local


def input_grads(locals_, grad_sum, w_query, w_key, w_value, queries, keys, values):
    rows, width = grad_sum.shape
    vm = pl.BlockSpec(memory_space=pltpu.VMEM)
    return pl.pallas_call(
        partial(input_kernel, locals_),
        in_specs=[vm] * (4 + 3 * len(queries)),
        out_specs=[vm] * 2,
        out_shape=shapes(((rows, width), jnp.float32), ((rows, width), jnp.bfloat16)),
        compiler_params=pltpu.CompilerParams(vmem_limit_bytes=LIMIT),
        cost_estimate=cost(2 * 5 * rows * width * width),
        name="input_grads",
    )(grad_sum, w_query, w_key, w_value, *queries, *keys, *values)


def swap(value, axis, bit):
    return lax.ppermute(value, axis, [(i, i ^ bit) for i in range(lax.axis_size(axis))])


def add_low(keep, came):
    return (keep.astype(jnp.float32) + came.astype(jnp.float32)).astype(keep.dtype)


class Scatter:
    def __init__(self, values):
        self.bits = lax.axis_size("batch").bit_length() - 1
        last = list(range(3, self.bits))
        self.orders = [[0, 1, 2] + last, [1, 2, 0] + last, [2, 0, 1] + last]
        self.left = [list(range(self.bits))[::-1] for _ in values]
        self.values = [value.reshape((2,) * self.bits + value.shape[1:]) for value in values]
        self.step = 0

    def start(self):
        self.kept, self.came = [], []
        for value, order, left in zip(self.values, self.orders, self.left):
            bit = order[self.step]
            axis = left.index(bit)
            mine = (lax.axis_index("batch") >> bit) & 1
            send = lax.dynamic_index_in_dim(value, 1 - mine, axis, keepdims=False)
            self.kept.append(lax.dynamic_index_in_dim(value, mine, axis, keepdims=False))
            self.came.append(swap(send, "batch", 1 << bit))
            left.remove(bit)

    def finish(self):
        self.values = [add_low(keep, came) for keep, came in zip(self.kept, self.came)]
        self.step += 1

    def run(self, steps):
        for _ in range(steps):
            self.start()
            self.finish()


def by_shard(value, n):
    return [part.reshape(n, -1, part.shape[-1]) for part in value]


def per_device(
    tokens_long, tokens_mid, tokens_short, lengths_long, lengths_mid, lengths_short,
    w_query, b_query, w_key, w_value, b_value, w_out, b_out, gain_attn, beta_attn,
    w_inner, b_inner, w_outer, b_outer, gain_ffn, beta_ffn,
    cotangent_long, cotangent_mid, cotangent_short,
):
    toks = (tokens_long, tokens_mid, tokens_short)
    cots = (cotangent_long, cotangent_mid, cotangent_short)
    locals_ = tuple(tok.shape[1] for tok in toks)
    width = w_query.shape[0]
    inner_width = w_inner.shape[1]
    n = lax.axis_size("batch")
    rows = width // n
    core = lax.axis_index("blk")
    scalars = jnp.concatenate([lengths_long, lengths_mid, lengths_short, core.astype(jnp.int32)[None]])
    others = [swap(tok, "blk", 1) for tok in toks]
    qa, keys, values, mixed, x = attend_forward(scalars, toks, others, w_query, w_key, w_value, b_query, b_value)
    (
        out_long, out_mid, out_short, normed1, inverse1, slope, grad_outer, grad_second,
        vectors2, keep_outer, send_outer,
    ) = ffn_forward(scalars, mixed, toks, cots, w_out, b_out, gain_attn, beta_attn, w_inner, b_inner, w_outer, b_outer, gain_ffn, beta_ffn)
    came_outer = swap(send_outer, "blk", 1)
    blocks = (locals_[0], locals_[1] + locals_[2])
    grad_sum, grad_mixed, vectors1, bias_inner, keep_inner, send_inner, keep_out, send_out = ffn_backward(
        scalars, blocks, mixed, normed1, inverse1, slope, grad_outer, grad_second, w_out, gain_attn, beta_attn, w_inner, w_outer
    )
    came_inner, came_out = swap(send_inner, "blk", 1), swap(send_out, "blk", 1)
    outer = add_low(keep_outer, came_outer)
    pieces = []
    step_count = len(range(0, width // LANES, 2))
    for piece in range(step_count):
        if piece == 1:
            inner = add_low(keep_inner, came_inner)
            outs = add_low(keep_out, came_out)
            parts = []
            for p in range(3):
                a = outer[p].reshape(n, -1, LANES)
                b = inner[p].reshape(n, rows, -1, LANES).swapaxes(1, 2).reshape(n, -1, LANES)
                c = outs[p].reshape(n, rows, LANES)
                parts.append(jnp.concatenate([a, b, c], 1))
            big = Scatter(parts)
            big.start()
        elif piece > 1:
            big.finish()
            big.start()
        if piece > 0:
            ready, grad_mixed = lax.optimization_barrier((big.kept, grad_mixed))
            big.kept = ready
        pieces.append(attend_backward(scalars, locals_, qa, keys, values, mixed, grad_mixed, x, 2 * piece, 2))
    own, send = input_grads(
        locals_, grad_sum, w_query, w_key, w_value, *[[piece[i] for piece in pieces] for i in range(3)]
    )
    came = [swap(piece[3][1], "blk", 1) for piece in pieces]
    sums = [add_low(piece[3][0], other) for piece, other in zip(pieces, came)]
    bias_rows = jnp.concatenate([piece[4][:2, :] for piece in pieces], 1)
    small = jnp.concatenate(
        [vector.reshape(n, rows) for vector in (bias_rows[0], bias_rows[1], vectors1[2], vectors1[0], vectors1[1])]
        + [bias_inner.reshape(n, -1)]
        + [vector.reshape(n, rows) for vector in (vectors2[2], vectors2[0], vectors2[1])],
        1,
    )
    small = small + swap(small, "blk", 1)
    per_row = LANES * len(pieces)
    height = -(-small.shape[1] // per_row)
    packed = jnp.pad(small, ((0, 0), (0, height * per_row - small.shape[1]))).astype(jnp.bfloat16)
    parts = [
        jnp.concatenate([total[i].reshape(n, rows, LANES) for total in sums], 2) for i in range(3)
    ]
    parts[0] = jnp.concatenate([parts[0], packed.reshape(n, height, per_row)], 1)
    tail = Scatter(parts)
    big.finish()
    tail.run(1)
    came = swap(send, "blk", 1)
    grads = (own + came.astype(jnp.float32)).astype(jnp.bfloat16)
    grad_parts = []
    start = 0
    for tok, local in zip(toks, locals_):
        grad_parts.append(grads[start : start + local].reshape(tok.shape))
        start += local
    tail.run(tail.bits - 1)
    big.run(big.bits - big.step)
    mine = jnp.concatenate([part.reshape(-1) for part in (*big.values, *tail.values)])
    other = swap(mine, "blk", 1)
    flat = [jnp.where(core == 0, mine, other), jnp.where(core == 0, other, mine)]
    flat = [half.astype(jnp.float32) for half in flat]
    sizes = [part.size for part in (*big.values, *tail.values)]
    cut = []
    for half in flat:
        at = 0
        found = []
        for size, like in zip(sizes, (*big.values, *tail.values)):
            found.append(half[at : at + size].reshape(like.shape))
            at += size
        cut.append(found)
    outer_rows = inner_width // n
    inner_rows = rows * (inner_width // 6 // LANES)
    grad_w_outer = jnp.concatenate([part[:outer_rows] for found in cut for part in found[:3]], 1)
    grad_w_inner = jnp.concatenate(
        [
            part[outer_rows : outer_rows + inner_rows].reshape(-1, rows, LANES).swapaxes(0, 1).reshape(rows, -1)
            for found in cut
            for part in found[:3]
        ],
        1,
    )
    grad_w_out = jnp.concatenate([part[outer_rows + inner_rows :] for found in cut for part in found[:3]], 1)
    thirds = []
    for i in range(3):
        halves = [found[3 + i][:rows].reshape(rows, -1, 1, LANES) for found in cut]
        thirds.append(jnp.concatenate(halves, 2).reshape(rows, width))
    bits = cut[0][3][rows:].reshape(-1)
    order = (rows,) * 5 + (inner_width // n,) + (rows,) * 3
    found = []
    at = 0
    for size in order:
        found.append(bits[at : at + size])
        at += size
    grad_b_query, grad_b_value, grad_b_out, grad_gain_attn, grad_beta_attn, grad_b_inner, grad_b_outer, grad_gain_ffn, grad_beta_ffn = found
    return (
        out_long, out_mid, out_short, *grad_parts, thirds[0], grad_b_query, thirds[1], thirds[2], grad_b_value,
        grad_w_out, grad_b_out, grad_gain_attn, grad_beta_attn, grad_w_inner, grad_b_inner, grad_w_outer, grad_b_outer,
        grad_gain_ffn, grad_beta_ffn,
    )


def solution(mesh):
    in_specs = (
        P("batch", "blk", None),
        P("batch", "blk", None),
        P("batch", "blk", None),
        P("batch"),
        P("batch"),
        P("batch"),
        P(),
        P(),
        P(),
        P(),
        P(),
        P(),
        P(),
        P(),
        P(),
        P(),
        P(),
        P(),
        P(),
        P(),
        P(),
        P("batch", "blk", None),
        P("batch", "blk", None),
        P("batch", "blk", None),
    )
    out_specs = (
        P("batch", "blk", None),
        P("batch", "blk", None),
        P("batch", "blk", None),
        P("batch", "blk", None),
        P("batch", "blk", None),
        P("batch", "blk", None),
        P("batch", None),
        P("batch"),
        P("batch", None),
        P("batch", None),
        P("batch"),
        P("batch", None),
        P("batch"),
        P("batch"),
        P("batch"),
        P("batch", None),
        P("batch"),
        P("batch", None),
        P("batch"),
        P("batch"),
        P("batch"),
    )
    return jax.shard_map(
        per_device, mesh=mesh, in_specs=in_specs, out_specs=out_specs, check_vma=False
    )
```

```python
from functools import partial

import jax
import jax.numpy as jnp
from jax import lax
from jax.experimental import pallas as pl
from jax.experimental.pallas import tpu as pltpu
from jax.sharding import PartitionSpec as P

HEADS = 12
LANES = 128
NT = (((1,), (1,)), ((), ()))
TN = (((0,), (0,)), ((), ()))
LOG2E = 1.4426950408889634
CHUNK = 512
LIMIT = 58 * 1024 * 1024
ANY = pl.BlockSpec(memory_space=pl.ANY)


def cost():
    return pl.CostEstimate(flops=100_000_000, bytes_accessed=1_000_000, transcendentals=0)


def shapes(*items):
    return [jax.ShapeDtypeStruct(shape, dtype) for shape, dtype in items]


def sum_rows(field):
    return jnp.sum(field, axis=0, keepdims=True)


def dot(left, right, dims=(((1,), (0,)), ((), ()))):
    return lax.dot_general(left, right, dims, preferred_element_type=jnp.float32)


def split_low(value):
    high = value.astype(jnp.bfloat16).astype(jnp.float32)
    rest = value - high
    middle = rest.astype(jnp.bfloat16).astype(jnp.float32)
    return high, middle, rest - middle


def lane_ids(rows):
    return lax.broadcasted_iota(jnp.int32, (rows, LANES), 1)


def pick_head(block, head):
    lanes = lane_ids(block.shape[0])
    half = LANES // 2
    keep = (lanes < half) if head == 0 else (lanes >= half)
    return jnp.where(keep, block.astype(jnp.float32), 0.0).astype(jnp.bfloat16)


def pick_extra(block, head):
    lanes = lane_ids(block.shape[0])
    keep = (lanes == 0) | ((lanes >= 1 + 3 * head) & (lanes < 4 + 3 * head))
    return jnp.where(keep, block.astype(jnp.float32), 0.0).astype(jnp.bfloat16)


def place_extra(first, pieces):
    lanes = lane_ids(pieces[0].shape[0])
    block = jnp.where(lanes == 0, first, 0.0)
    for place, piece in enumerate(pieces):
        block = jnp.where(lanes == 1 + place, piece, block)
    return block.astype(jnp.bfloat16)


def fill_extra(locals_, scalars, extra):
    core = scalars[3]
    offset = 0
    for bucket, local in enumerate(locals_):
        length = scalars[bucket]
        for half in range(2):
            owner = core if half == 0 else 1 - core
            lanes = lane_ids(local)
            places = lax.broadcasted_iota(jnp.int32, (local, LANES), 0) + owner * local
            bias = jnp.where(places < length, 0.0, -1e9)
            block = jnp.where(lanes == 0, bias, jnp.where(lanes < 7, 1.0, 0.0))
            extra[pl.ds(offset, local), :] = block.astype(jnp.bfloat16)
            offset += local


def forward_kernel(locals_, scalars, x_long, x_mid, x_short, y_long, y_mid, y_short,
                   w_query, w_key, w_value, b_query, b_value,
                   qa_out, keys_out, values_out, mixed_out, x_out,
                   x, extra, sems):
    group = pl.program_id(0)

    @pl.when(group == 0)
    def _():
        copies = []
        offset = 0
        for bucket, (mine, other) in enumerate(((x_long, y_long), (x_mid, y_mid), (x_short, y_short))):
            local = locals_[bucket]
            for half, ref in enumerate((mine, other)):
                copy = pltpu.make_async_copy(ref.at[0], x.at[pl.ds(offset, local)], sems.at[2 * bucket + half])
                copy.start()
                copies.append(copy)
                offset += local
        fill_extra(locals_, scalars, extra)
        for copy in copies:
            copy.wait()
        x_out[...] = x[...]

    w_pair = jnp.concatenate([w_key[...], w_value[...]], 1)
    both = dot(x[...], w_pair)
    keys = both[:, :LANES].astype(jnp.bfloat16)
    values = (both[:, LANES:] + b_value[...][None, :]).astype(jnp.bfloat16)
    keys_out[...] = keys
    values_out[...] = values
    key_rows = 0
    rows = 0
    for local in locals_:
        total_keys = 2 * local
        ks = slice(key_rows, key_rows + total_keys)
        query = ((dot(x[pl.ds(key_rows, local), :], w_query[...]) + b_query[...][None, :]) * (0.125 * LOG2E)).astype(jnp.bfloat16)
        one = jnp.where(lane_ids(local) == 0, 1.0, 0.0).astype(jnp.bfloat16)
        key_block = jnp.concatenate([keys[ks], extra[pl.ds(key_rows, total_keys), :]], 1)
        ones = jnp.ones((total_keys, LANES), jnp.bfloat16)
        mixed = None
        pieces = []
        for head in range(2):
            scores = dot(jnp.concatenate([pick_head(query, head), one], 1), key_block, NT)
            top = jnp.max(scores, axis=-1, keepdims=True)
            weights = jnp.exp2(scores - top).astype(jnp.bfloat16)
            found = dot(weights, jnp.concatenate([pick_head(values[ks], head), ones], 1))
            bulk = found[:, LANES:]
            part = found[:, :LANES] / bulk
            mixed = part if mixed is None else mixed + part
            pieces.extend(split_low(-(top + jnp.log2(bulk))))
        mixed_out[pl.ds(rows, local), :] = mixed.astype(jnp.bfloat16)
        qa_out[pl.ds(rows, local), :] = jnp.concatenate([query, place_extra(1.0, pieces)], 1)
        key_rows += total_keys
        rows += local


def attend_forward(scalars, mine, others, w_query, w_key, w_value, b_query, b_value):
    locals_ = tuple(part.shape[1] for part in mine)
    rows = sum(locals_)
    width = w_query.shape[0]
    groups = width // LANES
    low = jnp.bfloat16
    column = pl.BlockSpec((width, LANES), lambda g: (0, g))
    bias = pl.BlockSpec((LANES,), lambda g: (g,))
    anywhere = pl.BlockSpec(memory_space=pl.ANY)
    return pl.pallas_call(
        partial(forward_kernel, locals_),
        grid=(groups,),
        in_specs=[pl.BlockSpec(memory_space=pltpu.SMEM)] + [anywhere] * 6 + [column] * 3 + [bias] * 2,
        out_specs=[
            pl.BlockSpec((rows, 2 * LANES), lambda g: (0, g)),
            pl.BlockSpec((2 * rows, LANES), lambda g: (0, g)),
            pl.BlockSpec((2 * rows, LANES), lambda g: (0, g)),
            pl.BlockSpec((rows, LANES), lambda g: (0, g)),
            pl.BlockSpec((2 * rows, width), lambda g: (0, 0)),
        ],
        out_shape=[
            jax.ShapeDtypeStruct((rows, 2 * width), low),
            jax.ShapeDtypeStruct((2 * rows, width), low),
            jax.ShapeDtypeStruct((2 * rows, width), low),
            jax.ShapeDtypeStruct((rows, width), low),
            jax.ShapeDtypeStruct((2 * rows, width), low),
        ],
        scratch_shapes=[
            pltpu.VMEM((2 * rows, width), low),
            pltpu.VMEM((2 * rows, LANES), low),
            pltpu.SemaphoreType.DMA((6,)),
        ],
        compiler_params=pltpu.CompilerParams(vmem_limit_bytes=LIMIT),
        cost_estimate=cost(),
        name="attend_forward",
    )(scalars, *mine, *others, w_query, w_key, w_value, b_query, b_value)


def backward_kernel(locals_, offset, scalars, qa, keys, values, mixed, grad_mixed, x, vectors_in,
                    grad_query, grad_keys, grad_values, keep_w, send_w, vectors, extra):
    group = pl.program_id(0)

    @pl.when(group == 0)
    def _():
        fill_extra(locals_, scalars, extra)
        vectors[...] = vectors_in[...]

    key_rows = 0
    rows = 0
    for local in locals_:
        total_keys = 2 * local
        ks = pl.ds(key_rows, total_keys)
        qs = pl.ds(rows, local)
        query = qa[qs, :LANES]
        more = qa[qs, LANES:]
        cot = grad_mixed[qs, :]
        product = cot.astype(jnp.float32) * mixed[qs, :].astype(jnp.float32)
        lanes = lane_ids(local)
        pieces = []
        for head in range(2):
            keep = (lanes < 64) if head == 0 else (lanes >= 64)
            delta = jnp.sum(jnp.where(keep, product, 0.0), axis=-1, keepdims=True)
            pieces.extend(split_low(-jnp.broadcast_to(delta, (local, LANES))))
        cot_more = place_extra(0.0, pieces)
        key = keys[ks, :]
        marks = extra[ks, :]
        key_block = jnp.concatenate([key, marks], 1)
        value_block = jnp.concatenate([values[ks, :], marks], 1)
        sums = [None, None, None]
        for head in range(2):
            query_one = pick_head(query, head)
            cot_one = pick_head(cot, head)
            probs = jnp.exp2(dot(key_block, jnp.concatenate([query_one, pick_extra(more, head)], 1), NT))
            change = dot(value_block, jnp.concatenate([cot_one, pick_extra(cot_more, head)], 1), NT)
            grad_scores = (probs * change).astype(jnp.bfloat16)
            terms = (
                dot(grad_scores, pick_head(key, head), TN),
                dot(grad_scores, query_one),
                dot(probs.astype(jnp.bfloat16), cot_one),
            )
            sums = [term if old is None else old + term for old, term in zip(sums, terms)]
        grad_query[qs, :] = (sums[0] * 0.125).astype(jnp.bfloat16)
        grad_keys[ks, :] = (sums[1] * (1.0 / LOG2E)).astype(jnp.bfloat16)
        grad_values[ks, :] = sums[2].astype(jnp.bfloat16)
        key_rows += total_keys
        rows += local
    pair = jnp.concatenate([grad_keys[...], grad_values[...]], 1)
    both = dot(x[...], pair, TN)
    grad_w = [None, both[:, :LANES].astype(jnp.bfloat16), both[:, LANES:].astype(jnp.bfloat16)]
    key_rows = 0
    rows = 0
    total = None
    for local in locals_:
        term = dot(x[pl.ds(key_rows, local), :], grad_query[pl.ds(rows, local), :], TN)
        total = term if total is None else total + term
        key_rows += 2 * local
        rows += local
    grad_w[0] = total.astype(jnp.bfloat16)
    keeping = group == scalars[3]

    @pl.when(keeping)
    def _():
        for i in range(3):
            keep_w[i] = grad_w[i]

    @pl.when(jnp.logical_not(keeping))
    def _():
        for i in range(3):
            send_w[i] = grad_w[i]

    cs = pl.ds(pl.multiple_of((group + offset) * LANES, LANES), LANES)
    vectors[10:11, cs] = sum_rows(grad_query[...].astype(jnp.float32))
    vectors[11:12, cs] = sum_rows(grad_values[...].astype(jnp.float32))


def attend_backward(scalars, locals_, qa, keys, values, mixed, grad_mixed, x, vectors, first, count):
    rows = sum(locals_)
    width = x.shape[1]
    low = jnp.bfloat16

    def col(n, w=LANES):
        return pl.BlockSpec((n, w), lambda g, s: (0, g + first))

    def out(n):
        return pl.BlockSpec((n, LANES), lambda g, s: (0, g))

    def whole(shape):
        return pl.BlockSpec(shape, lambda g, s: (0,) * len(shape))

    return pl.pallas_call(
        partial(backward_kernel, locals_, first),
        grid_spec=pltpu.PrefetchScalarGridSpec(
            num_scalar_prefetch=1,
            grid=(count,),
            in_specs=[col(rows, 2 * LANES), col(2 * rows), col(2 * rows), col(rows), col(rows),
                      whole((2 * rows, width)), whole(vectors.shape)],
            out_specs=[out(rows), out(2 * rows), out(2 * rows), whole((3, width, LANES)), whole((3, width, LANES)), whole(vectors.shape)],
            scratch_shapes=[pltpu.VMEM((2 * rows, LANES), low)],
        ),
        out_shape=shapes(
            ((rows, LANES * count), low), ((2 * rows, LANES * count), low), ((2 * rows, LANES * count), low),
            ((3, width, LANES), low), ((3, width, LANES), low), (vectors.shape, jnp.float32),
        ),
        compiler_params=pltpu.CompilerParams(vmem_limit_bytes=LIMIT),
        cost_estimate=cost(),
        name="attend_backward",
    )(scalars, qa, keys, values, mixed, grad_mixed, x, vectors)


def gelu_and_slope(inner):
    size = jnp.abs(inner)
    bell = jnp.exp2(inner * inner * (-0.5 * LOG2E))
    t = 1.0 / (1.0 + (0.3275911 * 0.7071067811865476) * size)
    series = 0.5 * 1.061405429
    for term in (-0.5 * 1.453152027, 0.5 * 1.421413741, -0.5 * 0.284496736, 0.5 * 0.254829592):
        series = series * t + term
    tail = series * t * bell
    share = jnp.where(inner >= 0.0, 1.0 - tail, tail)
    return inner * share, share + inner * bell * 0.3989422804014327


def mean_of(field):
    return jnp.sum(field, axis=-1, keepdims=True) * (1.0 / field.shape[-1])


def normalize(field):
    centered = field - mean_of(field)
    inverse = lax.rsqrt(mean_of(centered * centered) + 1e-12)
    return centered * inverse, inverse


def norm_back(grad, normed, inverse):
    return inverse * (grad - mean_of(grad) - normed * mean_of(grad * normed))


def store_halves(core, keep, send, low, high):
    first = core == 0
    keep[...] = jnp.where(first, low, high).astype(keep.dtype)
    send[...] = jnp.where(first, high, low).astype(send.dtype)


def start_copies(pairs, sems):
    copies = [pltpu.make_async_copy(src, dst, sems.at[i]) for i, (src, dst) in enumerate(pairs)]
    for copy in copies:
        copy.start()
    return copies


def ffn_forward_kernel(blocks, scalars, mixed, tok_long, tok_mid, tok_short, cot_long, cot_mid, cot_short,
                       w_out, b_out, gain_attn, beta_attn, w_inner, b_inner, w_outer, b_outer, gain_ffn, beta_ffn,
                       out_long, out_mid, out_short, normed1, inverse1, slope, grad_outer, grad_second,
                       vectors, keep_all, send_all,
                       w_out_s, w_inner_s, w_outer_s, hidden_s, sems):
    width, inner_width = w_inner.shape
    chunks = inner_width // CHUNK
    pairs = [(w_out, w_out_s)]
    for j in range(chunks):
        cs = pl.ds(j * CHUNK, CHUNK)
        pairs.append((w_inner.at[:, cs], w_inner_s.at[:, cs]))
        pairs.append((w_outer.at[cs, :], w_outer_s.at[cs, :]))
    copies = start_copies(pairs, sems)
    toks = ((tok_long,), (tok_mid, tok_short))
    cots = ((cot_long,), (cot_mid, cot_short))
    outs = ((out_long,), (out_mid, out_short))
    join = lambda refs: jnp.concatenate([ref[0] for ref in refs], 0).astype(jnp.float32)
    start = 0
    sums = []
    for block, rows in enumerate(blocks):
        rs = pl.ds(start, rows)
        if block == 0:
            copies[0].wait()
        field = join(toks[block]) + dot(mixed[rs, :], w_out_s[...]) + b_out[...][None, :]
        n1, r1 = normalize(field)
        normed1[rs, :] = n1
        inverse1[rs, :] = jnp.broadcast_to(r1, (rows, LANES))
        first = n1 * gain_attn[...][None, :] + beta_attn[...][None, :]
        first_low = first.astype(jnp.bfloat16)
        total = first + b_outer[...][None, :]
        for j in range(chunks):
            cs = pl.ds(j * CHUNK, CHUNK)
            if block == 0:
                copies[1 + 2 * j].wait()
                copies[2 + 2 * j].wait()
            inner = dot(first_low, w_inner_s[:, cs]) + b_inner[cs][None, :]
            value, rate = gelu_and_slope(inner)
            hidden = value.astype(jnp.bfloat16)
            hidden_s[rs, cs] = hidden
            slope[rs, cs] = rate.astype(jnp.bfloat16)
            total = total + dot(hidden, w_outer_s[cs, :])
        n2, r2 = normalize(total)
        result = (n2 * gain_ffn[...][None, :] + beta_ffn[...][None, :]).astype(jnp.bfloat16)
        at = 0
        for ref in outs[block]:
            size = ref.shape[1]
            ref[0] = result[at : at + size]
            at += size
        cot = join(cots[block])
        back = norm_back(cot * gain_ffn[...][None, :], n2, r2)
        grad_second[rs, :] = back
        low = back.astype(jnp.bfloat16)
        grad_outer[rs, :] = low
        sums.append((sum_rows(cot * n2), sum_rows(cot), sum_rows(low.astype(jnp.float32))))
        start += rows
    for i in range(3):
        vectors[pl.ds(i, 1), :] = sums[0][i] + sums[1][i]
    core = scalars[3]
    half = width // 2
    for p in range(3):
        keep, send = keep_all.at[p], send_all.at[p]
        pair = jnp.concatenate(
            [grad_outer[:, pl.ds(p * LANES, LANES)], grad_outer[:, pl.ds(half + p * LANES, LANES)]], 1
        )
        for j in range(chunks):
            cs = pl.ds(j * CHUNK, CHUNK)
            both = dot(hidden_s[:, cs], pair, TN)
            store_halves(core, keep.at[cs, :], send.at[cs, :], both[:, :LANES], both[:, LANES:])


def ffn_forward(scalars, mixed, toks, cots, w_out, b_out, gain_attn, beta_attn, w_inner, b_inner, w_outer, b_outer, gain_ffn, beta_ffn):
    rows, width = mixed.shape
    inner_width = w_inner.shape[1]
    low, full = jnp.bfloat16, jnp.float32
    blocks = (toks[0].shape[1], toks[1].shape[1] + toks[2].shape[1])
    vm = pl.BlockSpec(memory_space=pltpu.VMEM)
    copies = 1 + 2 * (inner_width // CHUNK)
    return pl.pallas_call(
        partial(ffn_forward_kernel, blocks),
        in_specs=[pl.BlockSpec(memory_space=pltpu.SMEM)] + [vm] * 7
        + [ANY, vm, vm, vm, ANY, vm, ANY, vm, vm, vm],
        out_specs=[vm] * 11,
        out_shape=shapes(
            *[(tok.shape, low) for tok in toks],
            ((rows, width), full), ((rows, LANES), full), ((rows, inner_width), low),
            ((rows, width), low), ((rows, width), full), ((8, width), full),
            *[((3, inner_width, LANES), low)] * 2,
        ),
        scratch_shapes=[
            pltpu.VMEM(w_out.shape, low), pltpu.VMEM(w_inner.shape, low), pltpu.VMEM(w_outer.shape, low),
            pltpu.VMEM((rows, inner_width), low), pltpu.SemaphoreType.DMA((copies,)),
        ],
        compiler_params=pltpu.CompilerParams(vmem_limit_bytes=LIMIT),
        cost_estimate=cost(),
        name="ffn_forward",
    )(scalars, mixed, *toks, *cots, w_out, b_out, gain_attn, beta_attn, w_inner, b_inner,
      w_outer, b_outer, gain_ffn, beta_ffn)


def ffn_backward_kernel(blocks, scalars, mixed, normed1, inverse1, slope, grad_outer, grad_second, vectors2,
                        w_out, gain_attn, beta_attn, w_inner, w_outer,
                        grad_sum, grad_mixed, vectors, keep_all, send_all,
                        w_out_s, w_inner_s, w_outer_s, first_s, inner_s, branch_s, sems):
    width, inner_width = w_inner.shape
    chunks = inner_width // CHUNK
    pairs = []
    for j in range(chunks):
        cs = pl.ds(j * CHUNK, CHUNK)
        pairs.append((w_outer.at[cs, :], w_outer_s.at[cs, :]))
        pairs.append((w_inner.at[:, cs], w_inner_s.at[:, cs]))
    pairs.append((w_out, w_out_s))
    copies = start_copies(pairs, sems)
    start = 0
    sums = []
    biases = [None] * chunks
    for block, rows in enumerate(blocks):
        rs = pl.ds(start, rows)
        total = grad_second[rs, :]
        cot = grad_outer[rs, :]
        for j in range(chunks):
            cs = pl.ds(j * CHUNK, CHUNK)
            if block == 0:
                copies[2 * j].wait()
                copies[2 * j + 1].wait()
            change = dot(cot, w_outer_s[cs, :], NT) * slope[rs, cs].astype(jnp.float32)
            low = change.astype(jnp.bfloat16)
            inner_s[rs, cs] = low
            term = sum_rows(low.astype(jnp.float32))
            biases[j] = term if block == 0 else biases[j] + term
            total = total + dot(low, w_inner_s[:, cs], NT)
        n1 = normed1[rs, :]
        first_s[rs, :] = (n1 * gain_attn[...][None, :] + beta_attn[...][None, :]).astype(jnp.bfloat16)
        back = norm_back(total * gain_attn[...][None, :], n1, inverse1[rs, :][:, :1])
        grad_sum[rs, :] = back
        low = back.astype(jnp.bfloat16)
        branch_s[rs, :] = low
        sums.append((sum_rows(total * n1), sum_rows(total), sum_rows(low.astype(jnp.float32))))
        if block == 0:
            copies[2 * chunks].wait()
        grad_mixed[rs, :] = dot(low, w_out_s[...], NT).astype(jnp.bfloat16)
        start += rows
    for i in range(3):
        vectors[pl.ds(3 + i, 1), :] = sums[0][i] + sums[1][i]
    vectors[0:3, :] = vectors2[0:3, :]
    line = jnp.concatenate(biases, 1)
    for i in range(inner_width // width):
        vectors[pl.ds(6 + i, 1), :] = line[:, i * width : (i + 1) * width]
    vectors[10:16, :] = jnp.zeros((6, width), jnp.float32)
    core = scalars[3]
    half = inner_width // 2
    part = half // 3
    first_low = first_s[...]
    for p in range(3):
        keep, send = keep_all.at[p], send_all.at[p]
        for q in range(part // 256):
            at = p * part + q * 256
            low = dot(first_low, inner_s[:, pl.ds(at, 256)], TN)
            high = dot(first_low, inner_s[:, pl.ds(half + at, 256)], TN)
            cs = pl.ds(q * 256, 256)
            store_halves(core, keep.at[:, cs], send.at[:, cs], low, high)
    half = width // 2
    for p in range(3):
        cs = pl.ds(p * LANES, LANES)
        pair = jnp.concatenate([branch_s[:, cs], branch_s[:, pl.ds(half + p * LANES, LANES)]], 1)
        both = dot(mixed[...], pair, TN)
        cs = pl.ds(part, LANES)
        store_halves(core, keep_all.at[p, :, cs], send_all.at[p, :, cs], both[:, :LANES], both[:, LANES:])


def ffn_backward(scalars, blocks, mixed, normed1, inverse1, slope, grad_outer, grad_second, vectors2, w_out, gain_attn, beta_attn, w_inner, w_outer):
    rows, width = mixed.shape
    inner_width = w_inner.shape[1]
    low, full = jnp.bfloat16, jnp.float32
    vm = pl.BlockSpec(memory_space=pltpu.VMEM)
    copies = 1 + 2 * (inner_width // CHUNK)
    return pl.pallas_call(
        partial(ffn_backward_kernel, blocks),
        in_specs=[pl.BlockSpec(memory_space=pltpu.SMEM)] + [vm] * 7 + [ANY, vm, vm, ANY, ANY],
        out_specs=[vm] * 5,
        out_shape=shapes(
            ((rows, width), full), ((rows, width), low), ((16, width), full),
            *[((3, width, inner_width // 6 + LANES), low)] * 2,
        ),
        scratch_shapes=[
            pltpu.VMEM(w_out.shape, low), pltpu.VMEM(w_inner.shape, low), pltpu.VMEM(w_outer.shape, low),
            pltpu.VMEM((rows, width), low), pltpu.VMEM((rows, inner_width), low), pltpu.VMEM((rows, width), low),
            pltpu.SemaphoreType.DMA((copies,)),
        ],
        compiler_params=pltpu.CompilerParams(vmem_limit_bytes=LIMIT),
        cost_estimate=cost(),
        name="ffn_backward",
    )(scalars, mixed, normed1, inverse1, slope, grad_outer, grad_second, vectors2, w_out, gain_attn, beta_attn, w_inner, w_outer)


def input_kernel(locals_, grad_sum, w_query, w_key, w_value, *refs):
    pieces = (len(refs) - 2) // 3
    queries, keys, values = refs[:pieces], refs[pieces : 2 * pieces], refs[2 * pieces : 3 * pieces]
    own, send = refs[3 * pieces :]
    join = lambda parts, rows: jnp.concatenate([part[rows, :] for part in parts], 1)
    start = 0
    for local in locals_:
        rs = pl.ds(start, local)
        for half in range(2):
            ks = pl.ds(2 * start + half * local, local)
            total = dot(join(keys, ks), w_key[...], NT) + dot(join(values, ks), w_value[...], NT)
            if half == 0:
                own[rs, :] = grad_sum[rs, :] + total + dot(join(queries, rs), w_query[...], NT)
            else:
                send[rs, :] = total.astype(jnp.bfloat16)
        start += local


def input_grads(locals_, grad_sum, w_query, w_key, w_value, queries, keys, values):
    rows, width = grad_sum.shape
    vm = pl.BlockSpec(memory_space=pltpu.VMEM)
    return pl.pallas_call(
        partial(input_kernel, locals_),
        in_specs=[vm] * (4 + 3 * len(queries)),
        out_specs=[vm] * 2,
        out_shape=shapes(((rows, width), jnp.float32), ((rows, width), jnp.bfloat16)),
        compiler_params=pltpu.CompilerParams(vmem_limit_bytes=LIMIT),
        cost_estimate=cost(),
        name="input_grads",
    )(grad_sum, w_query, w_key, w_value, *queries, *keys, *values)


def swap(value, axis, bit):
    return lax.ppermute(value, axis, [(i, i ^ bit) for i in range(lax.axis_size(axis))])


def up16(rows):
    return -(-rows // 16) * 16


def add_full(keep, came):
    return keep.astype(jnp.float32) + came.astype(jnp.float32)


def halves_of(shards, left, bit):
    place = left.index(bit)
    return 2**place, shards // 2 ** (place + 1)


def half_spec(array, above, below, lead=None):
    shape = (1, 2, 1) + array.shape[-2:]
    if lead is None:
        return pl.BlockSpec(shape, lambda k, s: (k // below, 0, k % below, 0, 0))
    return pl.BlockSpec((1,) + shape, lambda k, s: (lead, k // below, 0, k % below, 0, 0))


def call_halving(body, name, scalars, steps, operands, specs, outs):
    blocks = [(1,) + out for out in outs for _ in range(2)]
    return pl.pallas_call(
        body,
        grid_spec=pltpu.PrefetchScalarGridSpec(
            num_scalar_prefetch=1,
            grid=(steps,),
            in_specs=specs,
            out_specs=[pl.BlockSpec(block, lambda k, s: (k, 0, 0)) for block in blocks],
        ),
        out_shape=shapes(*[((steps,) + block[1:], jnp.bfloat16) for block in blocks]),
        compiler_params=pltpu.CompilerParams(vmem_limit_bytes=LIMIT),
        cost_estimate=cost(),
        name=name,
    )(scalars, *operands)


def bit_of(scalars, bit):
    return (scalars[4] >> bit) & 1


def ffn_merge_kernel(bits, scalars, *refs):
    ins, outs = refs[:12], refs[12:]
    for p in range(3):
        keep_outer, came_outer, keep_inner, came_inner = ins[4 * p : 4 * p + 4]
        mine = bit_of(scalars, bits[p])
        for out, which in zip(outs[2 * p : 2 * p + 2], (1 - mine, mine)):
            first = add_full(keep_outer[0, 0, which, 0], came_outer[0, 0, which, 0])
            rows = first.shape[0]
            out[0, pl.ds(0, rows), :] = first.astype(out.dtype)
            second = add_full(keep_inner[0, 0, which, 0], came_inner[0, 0, which, 0]).astype(out.dtype)
            at = up16(rows)
            rows = second.shape[0]
            for q in range(second.shape[1] // LANES):
                out[0, pl.ds(at, rows), :] = second[:, q * LANES : (q + 1) * LANES]
                at += up16(rows)


def ffn_merge(n, bits, scalars, keep_outer, came_outer, keep_inner, came_inner):
    operands, specs = [], []
    left = list(range(n.bit_length() - 1))[::-1]
    for p in range(3):
        above, below = halves_of(n, left, bits[p])
        for array in (keep_outer, came_outer, keep_inner, came_inner):
            view = array.reshape(3, above, 2, below, array.shape[1] // n, array.shape[2])
            operands.append(view)
            specs.append(half_spec(view, above, below, p))
    height = up16(keep_outer.shape[1] // n) + keep_inner.shape[2] // LANES * up16(keep_inner.shape[1] // n)
    return call_halving(
        partial(ffn_merge_kernel, bits), "ffn_merge", scalars, n // 2, operands, specs, [(height, LANES)] * 3
    )


def attend_merge_kernel(bits, scalars, *refs):
    count = (len(refs) - 6) // 6
    ins, outs = refs[: 6 * count], refs[6 * count :]
    for p in range(3):
        mine = bit_of(scalars, bits[p])
        for out, which in zip(outs[2 * p : 2 * p + 2], (1 - mine, mine)):
            at = 0
            for t in range(count):
                keep, came = ins[2 * (p * count + t) : 2 * (p * count + t) + 2]
                total = add_full(keep[0, 0, which, 0], came[0, 0, which, 0])
                rows = total.shape[0]
                out[0, pl.ds(at, rows), :] = total.astype(out.dtype)
                at += up16(rows)


def attend_merge(n, bits, scalars, keeps, cames):
    operands, specs = [], []
    left = list(range(n.bit_length() - 1))[::-1]
    for p in range(3):
        above, below = halves_of(n, left, bits[p])
        for pair in zip(keeps, cames):
            for array in pair:
                view = array.reshape(3, above, 2, below, array.shape[1] // n, array.shape[2])
                operands.append(view)
                specs.append(half_spec(view, above, below, p))
    height = len(keeps) * up16(keeps[0].shape[1] // n)
    return call_halving(
        partial(attend_merge_kernel, bits), "attend_merge", scalars, n // 2, operands, specs, [(height, LANES)] * 3
    )


def advance_kernel(bits, scalars, *refs):
    count = len(bits)
    for p, bit in enumerate(bits):
        keep, came = refs[2 * p : 2 * p + 2]
        mine = bit_of(scalars, bit)
        for out, which in zip(refs[2 * (count + p) : 2 * (count + p) + 2], (1 - mine, mine)):
            out[0] = add_full(keep[0, which, 0], came[0, which, 0]).astype(out.dtype)


def advance(name, scalars, lefts, bits, keeps, cames):
    operands, specs = [], []
    shards = keeps[0].shape[0]
    for left, bit, keep, came in zip(lefts, bits, keeps, cames):
        above, below = halves_of(shards, left, bit)
        for array in (keep, came):
            view = array.reshape(above, 2, below, *array.shape[1:])
            operands.append(view)
            specs.append(half_spec(view, above, below))
    return call_halving(
        partial(advance_kernel, bits), name, scalars, shards // 2, operands, specs, [keep.shape[1:] for keep in keeps]
    )


def join_kernel(bit, count, scalars, *refs):
    send, kept = refs[2 * count :]
    mine = bit_of(scalars, bit)
    at = 0
    for p in range(count):
        keep, came = refs[2 * p : 2 * p + 2]
        rows = keep.shape[-2]
        for out, which in ((send, 1 - mine), (kept, mine)):
            out[0, pl.ds(at, rows), :] = add_full(keep[0, which, 0], came[0, which, 0]).astype(out.dtype)
        at += rows


def join(scalars, left, bit, keeps, cames):
    operands, specs = [], []
    shards = keeps[0].shape[0]
    above, below = halves_of(shards, left, bit)
    for keep, came in zip(keeps, cames):
        for array in (keep, came):
            view = array.reshape(above, 2, below, *array.shape[1:])
            operands.append(view)
            specs.append(half_spec(view, above, below))
    height = sum(keep.shape[1] for keep in keeps)
    return call_halving(
        partial(join_kernel, bit, len(keeps)), "join_portions", scalars, shards // 2, operands, specs, [(height, LANES)]
    )


def last_kernel(keep, came, out):
    out[...] = add_full(keep[0], came[0]).astype(out.dtype)


def last_sum(keep, came):
    vm = pl.BlockSpec(memory_space=pltpu.VMEM)
    return pl.pallas_call(
        last_kernel,
        in_specs=[vm] * 2,
        out_specs=vm,
        out_shape=jax.ShapeDtypeStruct(keep.shape[1:], keep.dtype),
        cost_estimate=cost(),
        name="last_sum",
    )(keep, came)


def result_kernel(count, scalars, mine, other, w_outer, w_inner, w_out, w_query, w_key, w_value):
    first = scalars[3] == 0
    width = w_out.shape[1]
    rows = w_out.shape[0]
    at = 0

    def place(ref, left, right, size):
        nonlocal at
        a = mine[pl.ds(at, size), :].astype(jnp.float32)
        b = other[pl.ds(at, size), :].astype(jnp.float32)
        ref[:, pl.ds(left, LANES)] = jnp.where(first, a, b)
        ref[:, pl.ds(right, LANES)] = jnp.where(first, b, a)
        at += up16(size)

    half = width // 2
    inner_half = w_inner.shape[1] // 2
    for p in range(3):
        place(w_outer, p * LANES, half + p * LANES, w_outer.shape[0])
        for q in range(inner_half // 3 // LANES):
            column = p * (inner_half // 3) + q * LANES
            place(w_inner, column, inner_half + column, rows)
        place(w_out, p * LANES, half + p * LANES, rows)
    for ref in (w_query, w_key, w_value):
        for t in range(count):
            place(ref, 2 * t * LANES, (2 * t + 1) * LANES, rows)


def results(scalars, mine, other, n, width, inner_width, count):
    vm = pl.BlockSpec(memory_space=pltpu.VMEM)
    full = jnp.float32
    square = ((width // n, width), full)
    return pl.pallas_call(
        partial(result_kernel, count),
        in_specs=[pl.BlockSpec(memory_space=pltpu.SMEM), vm, vm],
        out_specs=[vm] * 6,
        out_shape=shapes(((inner_width // n, width), full), ((width // n, inner_width), full), square, square, square, square),
        cost_estimate=cost(),
        name="results",
    )(scalars, mine, other)


class Chain:
    def __init__(self, name, scalars, orders, arrays):
        self.name, self.scalars, self.orders = name, scalars, orders
        bits = len(orders[0])
        self.lefts = [[bit for bit in range(bits)[::-1] if bit != order[0]] for order in orders]
        self.step = 0
        self.hold(arrays)

    def hold(self, arrays):
        self.sends, self.keeps = list(arrays[0::2]), list(arrays[1::2])

    def send(self):
        self.cames = [swap(value, "batch", 1 << order[self.step]) for value, order in zip(self.sends, self.orders)]
        self.step += 1

    def advance(self):
        bits = [order[self.step] for order in self.orders]
        self.hold(advance(self.name, self.scalars, self.lefts, bits, self.keeps, self.cames))
        for left, bit in zip(self.lefts, bits):
            left.remove(bit)

    def before(self, value):
        tied = lax.optimization_barrier((value, *self.sends))
        self.sends = list(tied[1:])
        return tied[0]


def per_device(
    tokens_long, tokens_mid, tokens_short, lengths_long, lengths_mid, lengths_short,
    w_query, b_query, w_key, w_value, b_value, w_out, b_out, gain_attn, beta_attn,
    w_inner, b_inner, w_outer, b_outer, gain_ffn, beta_ffn,
    cotangent_long, cotangent_mid, cotangent_short,
):
    toks = (tokens_long, tokens_mid, tokens_short)
    cots = (cotangent_long, cotangent_mid, cotangent_short)
    locals_ = tuple(tok.shape[1] for tok in toks)
    width = w_query.shape[0]
    inner_width = w_inner.shape[1]
    n = lax.axis_size("batch")
    bits = n.bit_length() - 1
    later = list(range(3, bits))
    orders = [[0, 1, 2] + later, [1, 2, 0] + later, [2, 0, 1] + later]
    firsts = [order[0] for order in orders]
    core = lax.axis_index("blk")
    place = lax.axis_index("batch")
    scalars = jnp.concatenate(
        [lengths_long, lengths_mid, lengths_short, jnp.stack([core, place]).astype(jnp.int32)]
    )
    others = [swap(tok, "blk", 1) for tok in toks]
    qa, keys, values, mixed, x = attend_forward(scalars, toks, others, w_query, w_key, w_value, b_query, b_value)
    (
        out_long, out_mid, out_short, normed1, inverse1, slope, grad_outer, grad_second, vectors, keep_outer, send_outer,
    ) = ffn_forward(
        scalars, mixed, toks, cots, w_out, b_out, gain_attn, beta_attn, w_inner, b_inner, w_outer, b_outer, gain_ffn, beta_ffn
    )
    came_outer = swap(send_outer, "blk", 1)
    blocks = (locals_[0], locals_[1] + locals_[2])
    grad_sum, grad_mixed, vectors, keep_inner, send_inner = ffn_backward(
        scalars, blocks, mixed, normed1, inverse1, slope, grad_outer, grad_second, vectors,
        w_out, gain_attn, beta_attn, w_inner, w_outer,
    )
    came_inner = swap(send_inner, "blk", 1)
    pieces = []
    cames = []
    count = width // LANES // 2
    chain = None
    for piece in range(count):
        if piece == 1:
            chain = Chain("ffn_step", scalars, orders, ffn_merge(n, firsts, scalars, keep_outer, came_outer, keep_inner, came_inner))
        elif piece > 1:
            chain.advance()
        if piece > 0:
            grad_mixed = chain.before(grad_mixed)
            chain.send()
        found = attend_backward(scalars, locals_, qa, keys, values, mixed, grad_mixed, x, vectors, 2 * piece, 2)
        pieces.append(found)
        cames.append(swap(found[4], "blk", 1))
        vectors = found[5]
    vectors = lax.psum(vectors, ("batch", "blk"))
    chain.advance()
    grad_sum = chain.before(grad_sum)
    chain.send()
    own, send = input_grads(
        locals_, grad_sum, w_query, w_key, w_value, *[[piece[i] for piece in pieces] for i in range(3)]
    )
    tail = Chain("attend_step", scalars, orders, attend_merge(n, firsts, scalars, [piece[3] for piece in pieces], cames))
    send = tail.before(send)
    tail.send()
    came = swap(send, "blk", 1)
    for _ in range(2):
        tail.advance()
        tail.send()
    left = chain.lefts[0]
    keeps, cames = chain.keeps + tail.keeps, chain.cames + tail.cames
    for bit in later:
        sent, keep = join(scalars, left, bit, keeps, cames)
        left = [other for other in left if other != bit]
        keeps, cames = [keep], [swap(sent, "batch", 1 << bit)]
    grads = (own + came.astype(jnp.float32)).astype(jnp.bfloat16)
    grad_parts = []
    start = 0
    for tok, local in zip(toks, locals_):
        grad_parts.append(grads[start : start + local].reshape(tok.shape))
        start += local
    mine = last_sum(keeps[0], cames[0])
    grad_w_outer, grad_w_inner, grad_w_out, grad_w_query, grad_w_key, grad_w_value = results(
        scalars, mine, swap(mine, "blk", 1), n, width, inner_width, count
    )
    rows = width // n

    def own_part(first, size):
        line = vectors[first : first + size].reshape(-1)
        return lax.dynamic_slice_in_dim(line, place * (size * rows), size * rows)

    return (
        out_long, out_mid, out_short, *grad_parts, grad_w_query, own_part(10, 1), grad_w_key, grad_w_value, own_part(11, 1),
        grad_w_out, own_part(5, 1), own_part(3, 1), own_part(4, 1), grad_w_inner, own_part(6, inner_width // width),
        grad_w_outer, own_part(2, 1), own_part(0, 1), own_part(1, 1),
    )


def solution(mesh):
    in_specs = (
        P("batch", "blk", None),
        P("batch", "blk", None),
        P("batch", "blk", None),
        P("batch"),
        P("batch"),
        P("batch"),
        P(),
        P(),
        P(),
        P(),
        P(),
        P(),
        P(),
        P(),
        P(),
        P(),
        P(),
        P(),
        P(),
        P(),
        P(),
        P("batch", "blk", None),
        P("batch", "blk", None),
        P("batch", "blk", None),
    )
    out_specs = (
        P("batch", "blk", None),
        P("batch", "blk", None),
        P("batch", "blk", None),
        P("batch", "blk", None),
        P("batch", "blk", None),
        P("batch", "blk", None),
        P("batch", None),
        P("batch"),
        P("batch", None),
        P("batch", None),
        P("batch"),
        P("batch", None),
        P("batch"),
        P("batch"),
        P("batch"),
        P("batch", None),
        P("batch"),
        P("batch", None),
        P("batch"),
        P("batch"),
        P("batch"),
    )
    return jax.shard_map(
        per_device, mesh=mesh, in_specs=in_specs, out_specs=out_specs, check_vma=False
    )
```

```python
from functools import partial

import jax
import jax.numpy as jnp
from jax import lax
from jax.experimental import pallas as pl
from jax.experimental.pallas import tpu as pltpu
from jax.sharding import PartitionSpec as P

HEADS = 12
LANES = 128
NT = (((1,), (1,)), ((), ()))
TN = (((0,), (0,)), ((), ()))
LOG2E = 1.4426950408889634
CHUNK = 512
LIMIT = 58 * 1024 * 1024
MIDDLE = 58 * 1024 * 1024
SMALL = 24 * 1024 * 1024
STEPS = 4
ANY = pl.BlockSpec(memory_space=pl.ANY)


def cost(microseconds):
    return pl.CostEstimate(flops=microseconds * 1_100_000_000, bytes_accessed=1_000_000, transcendentals=0)


def shapes(*items):
    return [jax.ShapeDtypeStruct(shape, dtype) for shape, dtype in items]


def sum_rows(field):
    return jnp.sum(field, axis=0, keepdims=True)


def dot(left, right, dims=(((1,), (0,)), ((), ()))):
    return lax.dot_general(left, right, dims, preferred_element_type=jnp.float32)


def split_low(value):
    high = value.astype(jnp.bfloat16).astype(jnp.float32)
    rest = value - high
    middle = rest.astype(jnp.bfloat16).astype(jnp.float32)
    return high, middle, rest - middle


def lane_ids(rows):
    return lax.broadcasted_iota(jnp.int32, (rows, LANES), 1)


def pick_head(block, head):
    lanes = lane_ids(block.shape[0])
    half = LANES // 2
    keep = (lanes < half) if head == 0 else (lanes >= half)
    return jnp.where(keep, block.astype(jnp.float32), 0.0).astype(jnp.bfloat16)


def pick_extra(block, head):
    lanes = lane_ids(block.shape[0])
    keep = (lanes == 0) | ((lanes >= 1 + 3 * head) & (lanes < 4 + 3 * head))
    return jnp.where(keep, block.astype(jnp.float32), 0.0).astype(jnp.bfloat16)


def place_extra(first, pieces):
    lanes = lane_ids(pieces[0].shape[0])
    block = jnp.where(lanes == 0, first, 0.0)
    for place, piece in enumerate(pieces):
        block = jnp.where(lanes == 1 + place, piece, block)
    return block.astype(jnp.bfloat16)


def fill_extra(locals_, scalars, extra):
    core = scalars[3]
    offset = 0
    for bucket, local in enumerate(locals_):
        length = scalars[bucket]
        for half in range(2):
            owner = core if half == 0 else 1 - core
            lanes = lane_ids(local)
            places = lax.broadcasted_iota(jnp.int32, (local, LANES), 0) + owner * local
            bias = jnp.where(places < length, 0.0, -1e9)
            block = jnp.where(lanes == 0, bias, jnp.where(lanes < 7, 1.0, 0.0))
            extra[pl.ds(offset, local), :] = block.astype(jnp.bfloat16)
            offset += local


def forward_kernel(locals_, scalars, x_long, x_mid, x_short, y_long, y_mid, y_short,
                   w_query, w_key, w_value, b_query, b_value,
                   qa_out, keys_out, values_out, mixed_out, x_out, extra,
                   x, sems):
    group = pl.program_id(0)

    @pl.when(group == 0)
    def _():
        copies = []
        offset = 0
        for bucket, (mine, other) in enumerate(((x_long, y_long), (x_mid, y_mid), (x_short, y_short))):
            local = locals_[bucket]
            for half, ref in enumerate((mine, other)):
                copy = pltpu.make_async_copy(ref.at[0], x.at[pl.ds(offset, local)], sems.at[2 * bucket + half])
                copy.start()
                copies.append(copy)
                offset += local
        fill_extra(locals_, scalars, extra)
        for copy in copies:
            copy.wait()
        x_out[...] = x[...]

    w_pair = jnp.concatenate([w_key[...], w_value[...]], 1)
    both = dot(x[...], w_pair)
    keys = both[:, :LANES].astype(jnp.bfloat16)
    values = (both[:, LANES:] + b_value[...][None, :]).astype(jnp.bfloat16)
    keys_out[...] = keys
    values_out[...] = values
    key_rows = 0
    rows = 0
    for local in locals_:
        total_keys = 2 * local
        ks = slice(key_rows, key_rows + total_keys)
        query = ((dot(x[pl.ds(key_rows, local), :], w_query[...]) + b_query[...][None, :]) * (0.125 * LOG2E)).astype(jnp.bfloat16)
        one = jnp.where(lane_ids(local) == 0, 1.0, 0.0).astype(jnp.bfloat16)
        key_block = jnp.concatenate([keys[ks], extra[pl.ds(key_rows, total_keys), :]], 1)
        ones = jnp.ones((total_keys, LANES), jnp.bfloat16)
        mixed = None
        pieces = []
        for head in range(2):
            scores = dot(jnp.concatenate([pick_head(query, head), one], 1), key_block, NT)
            top = jnp.max(scores, axis=-1, keepdims=True)
            weights = jnp.exp2(scores - top).astype(jnp.bfloat16)
            found = dot(weights, jnp.concatenate([pick_head(values[ks], head), ones], 1))
            bulk = found[:, LANES:]
            part = found[:, :LANES] / bulk
            mixed = part if mixed is None else mixed + part
            pieces.extend(split_low(-(top + jnp.log2(bulk))))
        mixed_out[pl.ds(rows, local), :] = mixed.astype(jnp.bfloat16)
        qa_out[pl.ds(rows, local), :] = jnp.concatenate([query, place_extra(1.0, pieces)], 1)
        key_rows += total_keys
        rows += local


def attend_forward(scalars, mine, others, w_query, w_key, w_value, b_query, b_value):
    locals_ = tuple(part.shape[1] for part in mine)
    rows = sum(locals_)
    width = w_query.shape[0]
    groups = width // LANES
    low = jnp.bfloat16
    column = pl.BlockSpec((width, LANES), lambda g: (0, g))
    bias = pl.BlockSpec((LANES,), lambda g: (g,))
    anywhere = pl.BlockSpec(memory_space=pl.ANY)
    return pl.pallas_call(
        partial(forward_kernel, locals_),
        grid=(groups,),
        in_specs=[pl.BlockSpec(memory_space=pltpu.SMEM)] + [anywhere] * 6 + [column] * 3 + [bias] * 2,
        out_specs=[
            pl.BlockSpec((rows, 2 * LANES), lambda g: (0, g)),
            pl.BlockSpec((2 * rows, LANES), lambda g: (0, g)),
            pl.BlockSpec((2 * rows, LANES), lambda g: (0, g)),
            pl.BlockSpec((rows, LANES), lambda g: (0, g)),
            pl.BlockSpec((2 * rows, width), lambda g: (0, 0)),
            pl.BlockSpec((2 * rows, LANES), lambda g: (0, 0)),
        ],
        out_shape=[
            jax.ShapeDtypeStruct((rows, 2 * width), low),
            jax.ShapeDtypeStruct((2 * rows, width), low),
            jax.ShapeDtypeStruct((2 * rows, width), low),
            jax.ShapeDtypeStruct((rows, width), low),
            jax.ShapeDtypeStruct((2 * rows, width), low),
            jax.ShapeDtypeStruct((2 * rows, LANES), low),
        ],
        scratch_shapes=[
            pltpu.VMEM((2 * rows, width), low),
            pltpu.SemaphoreType.DMA((6,)),
        ],
        compiler_params=pltpu.CompilerParams(vmem_limit_bytes=LIMIT),
        cost_estimate=cost(33),
        name="attend_forward",
    )(scalars, *mine, *others, w_query, w_key, w_value, b_query, b_value)


def backward_kernel(locals_, group, scalars, qa, keys, values, mixed, grad_mixed, x, extra, vectors_in, *refs):
    if group % 2:
        earlier, *refs = refs
    grad_query, grad_keys, grad_values, vectors, *grad_w_refs = refs
    vectors[...] = vectors_in[...]

    key_rows = 0
    rows = 0
    for local in locals_:
        total_keys = 2 * local
        ks = pl.ds(key_rows, total_keys)
        qs = pl.ds(rows, local)
        query = qa[qs, :LANES]
        more = qa[qs, LANES:]
        cot = grad_mixed[qs, :]
        product = cot.astype(jnp.float32) * mixed[qs, :].astype(jnp.float32)
        lanes = lane_ids(local)
        pieces = []
        for head in range(2):
            keep = (lanes < 64) if head == 0 else (lanes >= 64)
            delta = jnp.sum(jnp.where(keep, product, 0.0), axis=-1, keepdims=True)
            pieces.extend(split_low(-jnp.broadcast_to(delta, (local, LANES))))
        cot_more = place_extra(0.0, pieces)
        key = keys[ks, :]
        marks = extra[ks, :]
        key_block = jnp.concatenate([key, marks], 1)
        value_block = jnp.concatenate([values[ks, :], marks], 1)
        sums = [None, None, None]
        for head in range(2):
            query_one = pick_head(query, head)
            cot_one = pick_head(cot, head)
            probs = jnp.exp2(dot(key_block, jnp.concatenate([query_one, pick_extra(more, head)], 1), NT))
            change = dot(value_block, jnp.concatenate([cot_one, pick_extra(cot_more, head)], 1), NT)
            grad_scores = (probs * change).astype(jnp.bfloat16)
            terms = (
                dot(grad_scores, pick_head(key, head), TN),
                dot(grad_scores, query_one),
                dot(probs.astype(jnp.bfloat16), cot_one),
            )
            sums = [term if old is None else old + term for old, term in zip(sums, terms)]
        grad_query[qs, :] = (sums[0] * 0.125).astype(jnp.bfloat16)
        grad_keys[ks, :] = (sums[1] * (1.0 / LOG2E)).astype(jnp.bfloat16)
        grad_values[ks, :] = sums[2].astype(jnp.bfloat16)
        key_rows += total_keys
        rows += local
    pair = jnp.concatenate([grad_keys[...], grad_values[...]], 1)
    both = dot(x[...], pair, TN)
    grad_w = [None, both[:, :LANES].astype(jnp.bfloat16), both[:, LANES:].astype(jnp.bfloat16)]
    key_rows = 0
    rows = 0
    total = None
    for local in locals_:
        term = dot(x[pl.ds(key_rows, local), :], grad_query[pl.ds(rows, local), :], TN)
        total = term if total is None else total + term
        key_rows += 2 * local
        rows += local
    grad_w[0] = total.astype(jnp.bfloat16)
    for i in range(3):
        if group % 2:
            store_halves(scalars[3], grad_w_refs[0].at[i], grad_w_refs[1].at[i], earlier[i], grad_w[i])
        else:
            grad_w_refs[0][i] = grad_w[i]
    cs = pl.ds(group * LANES, LANES)
    vectors[6:7, cs] = sum_rows(grad_query[...].astype(jnp.float32))
    vectors[7:8, cs] = sum_rows(grad_values[...].astype(jnp.float32))


def attend_backward(scalars, locals_, qa, keys, values, mixed, grad_mixed, x, extra, vectors, group, earlier):
    rows = sum(locals_)
    width = x.shape[1]
    low = jnp.bfloat16

    def col(n, w=LANES):
        return pl.BlockSpec((n, w), lambda g: (0, group))

    def whole(shape):
        return pl.BlockSpec(shape, lambda g: (0,) * len(shape))

    weights = (3, width, LANES)
    last = group % 2
    return pl.pallas_call(
        partial(backward_kernel, locals_, group),
        grid=(1,),
        in_specs=[pl.BlockSpec(memory_space=pltpu.SMEM), col(rows, 2 * LANES), col(2 * rows), col(2 * rows), col(rows), col(rows),
                  whole(x.shape), whole(extra.shape), whole(vectors.shape)] + [whole(weights)] * last,
        out_specs=[whole((rows, LANES)), whole((2 * rows, LANES)), whole((2 * rows, LANES)), whole(vectors.shape)]
        + [whole(weights)] * (1 + last),
        out_shape=shapes(
            ((rows, LANES), low), ((2 * rows, LANES), low), ((2 * rows, LANES), low), (vectors.shape, jnp.float32),
            *[(weights, low)] * (1 + last),
        ),
        compiler_params=pltpu.CompilerParams(vmem_limit_bytes=MIDDLE),
        cost_estimate=cost(9),
        name="attend_backward",
    )(scalars, qa, keys, values, mixed, grad_mixed, x, extra, vectors, *([earlier] if last else []))


def gelu_and_slope(inner):
    size = jnp.abs(inner)
    bell = jnp.exp2(inner * inner * (-0.5 * LOG2E))
    t = 1.0 / (1.0 + (0.3275911 * 0.7071067811865476) * size)
    series = 0.5 * 1.061405429
    for term in (-0.5 * 1.453152027, 0.5 * 1.421413741, -0.5 * 0.284496736, 0.5 * 0.254829592):
        series = series * t + term
    tail = series * t * bell
    share = jnp.where(inner >= 0.0, 1.0 - tail, tail)
    return inner * share, share + inner * bell * 0.3989422804014327


def mean_of(field):
    return jnp.sum(field, axis=-1, keepdims=True) * (1.0 / field.shape[-1])


def normalize(field):
    centered = field - mean_of(field)
    inverse = lax.rsqrt(mean_of(centered * centered) + 1e-12)
    return centered * inverse, inverse


def norm_back(grad, normed, inverse):
    return inverse * (grad - mean_of(grad) - normed * mean_of(grad * normed))


def store_halves(core, keep, send, low, high):
    first = core == 0
    keep[...] = jnp.where(first, low, high).astype(keep.dtype)
    send[...] = jnp.where(first, high, low).astype(send.dtype)


def start_copies(pairs, sems):
    copies = [pltpu.make_async_copy(src, dst, sems.at[i]) for i, (src, dst) in enumerate(pairs)]
    for copy in copies:
        copy.start()
    return copies


def ffn_forward_kernel(blocks, scalars, mixed, tok_long, tok_mid, tok_short, cot_long, cot_mid, cot_short,
                       w_out, b_out, gain_attn, beta_attn, w_inner, b_inner, w_outer, b_outer, gain_ffn, beta_ffn,
                       out_long, out_mid, out_short, normed1, inverse1, slope, grad_outer, grad_second,
                       vectors, keep_all, send_all,
                       w_out_s, w_inner_s, w_outer_s, hidden_s, sems):
    width, inner_width = w_inner.shape
    chunks = inner_width // CHUNK
    pairs = [(w_out, w_out_s)]
    for j in range(chunks):
        cs = pl.ds(j * CHUNK, CHUNK)
        pairs.append((w_inner.at[:, cs], w_inner_s.at[:, cs]))
        pairs.append((w_outer.at[cs, :], w_outer_s.at[cs, :]))
    copies = start_copies(pairs, sems)
    toks = ((tok_long,), (tok_mid, tok_short))
    cots = ((cot_long,), (cot_mid, cot_short))
    outs = ((out_long,), (out_mid, out_short))
    join = lambda refs: jnp.concatenate([ref[0] for ref in refs], 0).astype(jnp.float32)
    start = 0
    sums = []
    for block, rows in enumerate(blocks):
        rs = pl.ds(start, rows)
        if block == 0:
            copies[0].wait()
        field = join(toks[block]) + dot(mixed[rs, :], w_out_s[...]) + b_out[...][None, :]
        n1, r1 = normalize(field)
        normed1[rs, :] = n1
        inverse1[rs, :] = jnp.broadcast_to(r1, (rows, LANES))
        first = n1 * gain_attn[...][None, :] + beta_attn[...][None, :]
        first_low = first.astype(jnp.bfloat16)
        total = first + b_outer[...][None, :]
        for j in range(chunks):
            cs = pl.ds(j * CHUNK, CHUNK)
            if block == 0:
                copies[1 + 2 * j].wait()
                copies[2 + 2 * j].wait()
            inner = dot(first_low, w_inner_s[:, cs]) + b_inner[cs][None, :]
            value, rate = gelu_and_slope(inner)
            hidden = value.astype(jnp.bfloat16)
            hidden_s[rs, cs] = hidden
            slope[rs, cs] = rate.astype(jnp.bfloat16)
            total = total + dot(hidden, w_outer_s[cs, :])
        n2, r2 = normalize(total)
        result = (n2 * gain_ffn[...][None, :] + beta_ffn[...][None, :]).astype(jnp.bfloat16)
        at = 0
        for ref in outs[block]:
            size = ref.shape[1]
            ref[0] = result[at : at + size]
            at += size
        cot = join(cots[block])
        back = norm_back(cot * gain_ffn[...][None, :], n2, r2)
        grad_second[rs, :] = back
        low = back.astype(jnp.bfloat16)
        grad_outer[rs, :] = low
        sums.append((sum_rows(cot * n2), sum_rows(cot), sum_rows(low.astype(jnp.float32))))
        start += rows
    for i in range(3):
        vectors[pl.ds(i, 1), :] = sums[0][i] + sums[1][i]
    core = scalars[3]
    half = width // 2
    for p in range(3):
        keep, send = keep_all.at[p], send_all.at[p]
        pair = jnp.concatenate(
            [grad_outer[:, pl.ds(p * LANES, LANES)], grad_outer[:, pl.ds(half + p * LANES, LANES)]], 1
        )
        for j in range(chunks):
            cs = pl.ds(j * CHUNK, CHUNK)
            both = dot(hidden_s[:, cs], pair, TN)
            store_halves(core, keep.at[cs, :], send.at[cs, :], both[:, :LANES], both[:, LANES:])


def ffn_forward(scalars, mixed, toks, cots, w_out, b_out, gain_attn, beta_attn, w_inner, b_inner, w_outer, b_outer, gain_ffn, beta_ffn):
    rows, width = mixed.shape
    inner_width = w_inner.shape[1]
    low, full = jnp.bfloat16, jnp.float32
    blocks = (toks[0].shape[1], toks[1].shape[1] + toks[2].shape[1])
    vm = pl.BlockSpec(memory_space=pltpu.VMEM)
    copies = 1 + 2 * (inner_width // CHUNK)
    return pl.pallas_call(
        partial(ffn_forward_kernel, blocks),
        in_specs=[pl.BlockSpec(memory_space=pltpu.SMEM)] + [vm] * 7
        + [ANY, vm, vm, vm, ANY, vm, ANY, vm, vm, vm],
        out_specs=[vm] * 11,
        out_shape=shapes(
            *[(tok.shape, low) for tok in toks],
            ((rows, width), full), ((rows, LANES), full), ((rows, inner_width), low),
            ((rows, width), low), ((rows, width), full), ((8, width), full),
            *[((3, inner_width, LANES), low)] * 2,
        ),
        scratch_shapes=[
            pltpu.VMEM(w_out.shape, low), pltpu.VMEM(w_inner.shape, low), pltpu.VMEM(w_outer.shape, low),
            pltpu.VMEM((rows, inner_width), low), pltpu.SemaphoreType.DMA((copies,)),
        ],
        compiler_params=pltpu.CompilerParams(vmem_limit_bytes=LIMIT),
        cost_estimate=cost(34),
        name="ffn_forward",
    )(scalars, mixed, *toks, *cots, w_out, b_out, gain_attn, beta_attn, w_inner, b_inner,
      w_outer, b_outer, gain_ffn, beta_ffn)


def ffn_backward_kernel(blocks, scalars, mixed, normed1, inverse1, slope, grad_outer, grad_second, vectors2,
                        w_out, gain_attn, beta_attn, w_inner, w_outer,
                        grad_sum, grad_mixed, vectors, keep_all, send_all,
                        w_out_s, w_inner_s, w_outer_s, first_s, inner_s, branch_s, sems):
    width, inner_width = w_inner.shape
    chunks = inner_width // CHUNK
    pairs = []
    for j in range(chunks):
        cs = pl.ds(j * CHUNK, CHUNK)
        pairs.append((w_outer.at[cs, :], w_outer_s.at[cs, :]))
        pairs.append((w_inner.at[:, cs], w_inner_s.at[:, cs]))
    pairs.append((w_out, w_out_s))
    copies = start_copies(pairs, sems)
    start = 0
    sums = []
    biases = [None] * chunks
    for block, rows in enumerate(blocks):
        rs = pl.ds(start, rows)
        total = grad_second[rs, :]
        cot = grad_outer[rs, :]
        for j in range(chunks):
            cs = pl.ds(j * CHUNK, CHUNK)
            if block == 0:
                copies[2 * j].wait()
                copies[2 * j + 1].wait()
            change = dot(cot, w_outer_s[cs, :], NT) * slope[rs, cs].astype(jnp.float32)
            low = change.astype(jnp.bfloat16)
            inner_s[rs, cs] = low
            term = sum_rows(low.astype(jnp.float32))
            biases[j] = term if block == 0 else biases[j] + term
            total = total + dot(low, w_inner_s[:, cs], NT)
        n1 = normed1[rs, :]
        first_s[rs, :] = (n1 * gain_attn[...][None, :] + beta_attn[...][None, :]).astype(jnp.bfloat16)
        back = norm_back(total * gain_attn[...][None, :], n1, inverse1[rs, :][:, :1])
        grad_sum[rs, :] = back
        low = back.astype(jnp.bfloat16)
        branch_s[rs, :] = low
        sums.append((sum_rows(total * n1), sum_rows(total), sum_rows(low.astype(jnp.float32))))
        if block == 0:
            copies[2 * chunks].wait()
        grad_mixed[rs, :] = dot(low, w_out_s[...], NT).astype(jnp.bfloat16)
        start += rows
    for i in range(3):
        vectors[pl.ds(3 + i, 1), :] = sums[0][i] + sums[1][i]
    vectors[0:3, :] = vectors2[0:3, :]
    line = jnp.concatenate(biases, 1)
    for i in range(inner_width // width):
        vectors[pl.ds(16 + i, 1), :] = line[:, i * width : (i + 1) * width]
    vectors[6:16, :] = jnp.zeros((10, width), jnp.float32)
    core = scalars[3]
    half = inner_width // 2
    part = half // 3
    first_low = first_s[...]
    for p in range(3):
        keep, send = keep_all.at[p], send_all.at[p]
        for q in range(part // 256):
            at = p * part + q * 256
            low = dot(first_low, inner_s[:, pl.ds(at, 256)], TN)
            high = dot(first_low, inner_s[:, pl.ds(half + at, 256)], TN)
            cs = pl.ds(q * 256, 256)
            store_halves(core, keep.at[:, cs], send.at[:, cs], low, high)
    half = width // 2
    for p in range(3):
        cs = pl.ds(p * LANES, LANES)
        pair = jnp.concatenate([branch_s[:, cs], branch_s[:, pl.ds(half + p * LANES, LANES)]], 1)
        both = dot(mixed[...], pair, TN)
        cs = pl.ds(part, LANES)
        store_halves(core, keep_all.at[p, :, cs], send_all.at[p, :, cs], both[:, :LANES], both[:, LANES:])


def ffn_backward(scalars, blocks, mixed, normed1, inverse1, slope, grad_outer, grad_second, vectors2, w_out, gain_attn, beta_attn, w_inner, w_outer):
    rows, width = mixed.shape
    inner_width = w_inner.shape[1]
    low, full = jnp.bfloat16, jnp.float32
    vm = pl.BlockSpec(memory_space=pltpu.VMEM)
    copies = 1 + 2 * (inner_width // CHUNK)
    return pl.pallas_call(
        partial(ffn_backward_kernel, blocks),
        in_specs=[pl.BlockSpec(memory_space=pltpu.SMEM)] + [vm] * 7 + [ANY, vm, vm, ANY, ANY],
        out_specs=[vm] * 5,
        out_shape=shapes(
            ((rows, width), full), ((rows, width), low), ((16 + inner_width // width, width), full),
            *[((3, width, inner_width // 6 + LANES), low)] * 2,
        ),
        scratch_shapes=[
            pltpu.VMEM(w_out.shape, low), pltpu.VMEM(w_inner.shape, low), pltpu.VMEM(w_outer.shape, low),
            pltpu.VMEM((rows, width), low), pltpu.VMEM((rows, inner_width), low), pltpu.VMEM((rows, width), low),
            pltpu.SemaphoreType.DMA((copies,)),
        ],
        compiler_params=pltpu.CompilerParams(vmem_limit_bytes=LIMIT),
        cost_estimate=cost(30),
        name="ffn_backward",
    )(scalars, mixed, normed1, inverse1, slope, grad_outer, grad_second, vectors2, w_out, gain_attn, beta_attn, w_inner, w_outer)


def input_kernel(locals_, half, *refs):
    out = refs[-1]
    if half == 0:
        grad_sum, w_query, *refs = refs
    w_key, w_value, *parts = refs[:-1]
    count = len(parts) // (3 - half)
    keys, values, queries = parts[:count], parts[count : 2 * count], parts[2 * count :]
    beside = lambda blocks, rows: jnp.concatenate([block[rows, :] for block in blocks], 1)
    start = 0
    for local in locals_:
        rs = pl.ds(start, local)
        ks = pl.ds(2 * start + half * local, local)
        total = dot(beside(keys, ks), w_key[...], NT) + dot(beside(values, ks), w_value[...], NT)
        if half == 0:
            total = total + grad_sum[rs, :] + dot(beside(queries, rs), w_query[...], NT)
        out[rs, :] = total.astype(out.dtype)
        start += local


def input_grads(locals_, half, dtype, operands):
    vm = pl.BlockSpec(memory_space=pltpu.VMEM)
    rows, width = sum(locals_), operands[0].shape[1]
    return pl.pallas_call(
        partial(input_kernel, locals_, half),
        in_specs=[vm] * len(operands),
        out_specs=vm,
        out_shape=jax.ShapeDtypeStruct((rows, width), dtype),
        compiler_params=pltpu.CompilerParams(vmem_limit_bytes=MIDDLE),
        cost_estimate=cost(8 - 2 * half),
        name="input_grads",
    )(*operands)


def swap(value, axis, bit):
    return lax.ppermute(value, axis, [(i, i ^ bit) for i in range(lax.axis_size(axis))])


def up16(rows):
    return -(-rows // 16) * 16


def halves_of(shards, left, bit):
    place = left.index(bit)
    return 2**place, shards // 2 ** (place + 1)


def steps_of(pairs):
    steps = min(pairs, STEPS)
    return steps, pairs // steps


def half_spec(array, above, below, lead=None):
    _, many = steps_of(above * below)
    if below >= many:
        block = (1, 2, many)
        index = lambda k: (k * many // below, 0, k * many % below // many)
    else:
        block = (many // below, 2, below)
        index = lambda k: (k, 0, 0)
    shape = block + array.shape[-2:]
    if lead is None:
        return pl.BlockSpec(shape, lambda k, s: index(k) + (0, 0))
    return pl.BlockSpec((None,) + shape, lambda k, s: (lead,) + index(k) + (0, 0))


def pairs_in(ref):
    above, below = ref.shape[0], ref.shape[2]
    return [(a * below + b, a, b) for a in range(above) for b in range(below)]


def call_halving(body, name, scalars, pairs, operands, specs, outs):
    steps, many = steps_of(pairs)
    blocks = [(many,) + tuple(out) for out in outs for _ in range(2)]
    return pl.pallas_call(
        body,
        grid_spec=pltpu.PrefetchScalarGridSpec(
            num_scalar_prefetch=1,
            grid=(steps,),
            in_specs=specs,
            out_specs=[pl.BlockSpec(block, lambda k, s: (k, 0, 0)) for block in blocks],
        ),
        out_shape=shapes(*[((pairs,) + block[1:], jnp.bfloat16) for block in blocks]),
        compiler_params=pltpu.CompilerParams(vmem_limit_bytes=SMALL),
        cost_estimate=cost(2),
        name=name,
    )(scalars, *operands)


def bit_of(scalars, bit):
    return (scalars[4] >> bit) & 1


def ffn_merge_kernel(bits, scalars, *refs):
    ins, outs = refs[:12], refs[12:]
    for p in range(3):
        keep_outer, came_outer, keep_inner, came_inner = ins[4 * p : 4 * p + 4]
        mine = bit_of(scalars, bits[p])
        for out, which in zip(outs[2 * p : 2 * p + 2], (1 - mine, mine)):
            for k, a, b in pairs_in(keep_outer):
                first = keep_outer[a, which, b] + came_outer[a, which, b]
                rows = first.shape[0]
                out[k, pl.ds(0, rows), :] = first
                second = keep_inner[a, which, b] + came_inner[a, which, b]
                at = up16(rows)
                rows = second.shape[0]
                for q in range(second.shape[1] // LANES):
                    out[k, pl.ds(at, rows), :] = second[:, q * LANES : (q + 1) * LANES]
                    at += up16(rows)


def ffn_merge(n, bits, scalars, keep_outer, came_outer, keep_inner, came_inner):
    operands, specs = [], []
    left = list(range(n.bit_length() - 1))[::-1]
    for p in range(3):
        above, below = halves_of(n, left, bits[p])
        for array in (keep_outer, came_outer, keep_inner, came_inner):
            view = array.reshape(3, above, 2, below, array.shape[1] // n, array.shape[2])
            operands.append(view)
            specs.append(half_spec(view, above, below, p))
    height = up16(keep_outer.shape[1] // n) + keep_inner.shape[2] // LANES * up16(keep_inner.shape[1] // n)
    return call_halving(
        partial(ffn_merge_kernel, bits), "ffn_merge", scalars, n // 2, operands, specs, [(height, LANES)] * 3
    )


def own_columns(line, start, size):
    width = line.shape[1]
    lanes = -(-size // LANES) * LANES
    from_ = lax.broadcasted_iota(jnp.int32, (width, lanes), 0)
    to = lax.broadcasted_iota(jnp.int32, (width, lanes), 1)
    chosen = jnp.where((from_ == start + to) & (to < size), 1.0, 0.0).astype(jnp.bfloat16)
    return dot(line.astype(jnp.bfloat16), chosen)


def attend_merge_kernel(n, bits, scalars, vectors, vectors_came, *refs):
    count = (len(refs) - 6) // 6
    ins, outs = refs[: 6 * count], refs[6 * count :]
    many = outs[0].shape[0]
    for p in range(3):
        mine = bit_of(scalars, bits[p])
        for out, which in zip(outs[2 * p : 2 * p + 2], (1 - mine, mine)):
            at = 0
            for t in range(count):
                keep, came = ins[2 * (p * count + t) : 2 * (p * count + t) + 2]
                for k, a, b in pairs_in(keep):
                    total = keep[a, which, b] + came[a, which, b]
                    rows = total.shape[0]
                    out[k, pl.ds(at, rows), :] = total
                at += up16(rows)
            if p > 0:
                continue
            below = 2 ** bits[0]
            for k in range(many):
                pair = pl.program_id(0) * many + k
                shard = (pair // below * 2 + which) * below + pair % below
                small = vectors[...] + vectors_came[...]
                width = small.shape[1]
                found = own_columns(small, shard * (width // n), width // n)
                inner = small.shape[0] - 16
                per = inner * width // n
                span = n // inner
                line = jnp.zeros((1, width), jnp.float32)
                for i in range(inner):
                    line = jnp.where(shard // span == i, small[16 + i : 17 + i], line)
                wide = own_columns(jnp.broadcast_to(line, (8, width)), shard % span * per, per)
                groups = [wide[:1, g * LANES : (g + 1) * LANES] for g in range(wide.shape[1] // LANES)]
                block = jnp.concatenate([found[: 16 - len(groups)]] + groups, 0)
                out[k, pl.ds(at, 16), :] = block.astype(out.dtype)


def attend_merge(n, bits, scalars, vectors, vectors_came, keeps, cames):
    whole = pl.BlockSpec(vectors.shape, lambda k, s: (0, 0))
    operands, specs = [vectors, vectors_came], [whole, whole]
    left = list(range(n.bit_length() - 1))[::-1]
    for p in range(3):
        above, below = halves_of(n, left, bits[p])
        for pair in zip(keeps, cames):
            for array in pair:
                view = array.reshape(3, above, 2, below, array.shape[1] // n, array.shape[2])
                operands.append(view)
                specs.append(half_spec(view, above, below, p))
    height = len(keeps) * up16(keeps[0].shape[1] // n)
    return call_halving(
        partial(attend_merge_kernel, n, bits), "attend_merge", scalars, n // 2, operands, specs,
        [(height + 16, LANES), (height, LANES), (height, LANES)],
    )


def advance_kernel(bits, scalars, *refs):
    count = len(bits)
    for p, bit in enumerate(bits):
        keep, came = refs[2 * p : 2 * p + 2]
        mine = bit_of(scalars, bit)
        for out, which in zip(refs[2 * (count + p) : 2 * (count + p) + 2], (1 - mine, mine)):
            for k, a, b in pairs_in(keep):
                out[k] = keep[a, which, b] + came[a, which, b]


def advance(name, scalars, lefts, bits, keeps, cames):
    operands, specs = [], []
    shards = keeps[0].shape[0]
    for left, bit, keep, came in zip(lefts, bits, keeps, cames):
        above, below = halves_of(shards, left, bit)
        for array in (keep, came):
            view = array.reshape(above, 2, below, *array.shape[1:])
            operands.append(view)
            specs.append(half_spec(view, above, below))
    return call_halving(
        partial(advance_kernel, bits), name, scalars, shards // 2, operands, specs, [keep.shape[1:] for keep in keeps]
    )


def join_kernel(bit, count, scalars, *refs):
    send, kept = refs[2 * count :]
    mine = bit_of(scalars, bit)
    at = 0
    for p in range(count):
        keep, came = refs[2 * p : 2 * p + 2]
        rows = keep.shape[-2]
        for out, which in ((send, 1 - mine), (kept, mine)):
            for k, a, b in pairs_in(keep):
                out[k, pl.ds(at, rows), :] = keep[a, which, b] + came[a, which, b]
        at += rows


def join(scalars, left, bit, keeps, cames):
    operands, specs = [], []
    shards = keeps[0].shape[0]
    above, below = halves_of(shards, left, bit)
    for keep, came in zip(keeps, cames):
        for array in (keep, came):
            view = array.reshape(above, 2, below, *array.shape[1:])
            operands.append(view)
            specs.append(half_spec(view, above, below))
    height = sum(keep.shape[1] for keep in keeps)
    return call_halving(
        partial(join_kernel, bit, len(keeps)), "join_portions", scalars, shards // 2, operands, specs, [(height, LANES)]
    )


def last_kernel(keep, came, out):
    out[...] = keep[0] + came[0]


def last_sum(keep, came):
    vm = pl.BlockSpec(memory_space=pltpu.VMEM)
    return pl.pallas_call(
        last_kernel,
        in_specs=[vm] * 2,
        out_specs=vm,
        out_shape=jax.ShapeDtypeStruct(keep.shape[1:], keep.dtype),
        cost_estimate=cost(2),
        name="last_sum",
    )(keep, came)


def placer(scalars, mine, other):
    first = scalars[3] == 0
    at = 0

    def place(ref, left, right, size):
        nonlocal at
        a = mine[pl.ds(at, size), :].astype(jnp.float32)
        b = other[pl.ds(at, size), :].astype(jnp.float32)
        ref[:, pl.ds(left, LANES)] = jnp.where(first, a, b)
        ref[:, pl.ds(right, LANES)] = jnp.where(first, b, a)
        at += up16(size)

    def skip(size):
        nonlocal at
        at += size
        return at - size

    return place, skip


def ffn_result_kernel(scalars, mine, other, w_outer, w_inner, w_out):
    place, _ = placer(scalars, mine, other)
    rows, width = w_out.shape
    half = width // 2
    inner_half = w_inner.shape[1] // 2
    for p in range(3):
        place(w_outer, p * LANES, half + p * LANES, w_outer.shape[0])
        for q in range(inner_half // 3 // LANES):
            column = p * (inner_half // 3) + q * LANES
            place(w_inner, column, inner_half + column, rows)
        place(w_out, p * LANES, half + p * LANES, rows)


def attend_result_kernel(count, scalars, mine, other, w_query, w_key, w_value, b_inner, *lines):
    place, skip = placer(scalars, mine, other)
    rows = w_query.shape[0]
    for ref in (w_query, w_key, w_value):
        for t in range(count):
            place(ref, 2 * t * LANES, (2 * t + 1) * LANES, rows)
        if ref is w_query:
            small = mine[pl.ds(skip(16), 16), :].astype(jnp.float32)
    for i, ref in enumerate(lines):
        ref[...] = small[i, :rows]
    size = b_inner.shape[0]
    groups = -(-size // LANES)
    for g in range(groups):
        part = min(LANES, size - g * LANES)
        b_inner[pl.ds(g * LANES, part)] = small[16 - groups + g, :part]


def results(body, name, scalars, mine, outs):
    vm = pl.BlockSpec(memory_space=pltpu.VMEM)
    return pl.pallas_call(
        body,
        in_specs=[pl.BlockSpec(memory_space=pltpu.SMEM), vm, vm],
        out_specs=[vm] * len(outs),
        out_shape=shapes(*[(out, jnp.float32) for out in outs]),
        compiler_params=pltpu.CompilerParams(vmem_limit_bytes=SMALL),
        cost_estimate=cost(2),
        name=name,
    )(scalars, mine, swap(mine, "blk", 1))


def finish_kernel(own, came, *outs):
    start = 0
    for out in outs:
        rs = pl.ds(start, out.shape[1])
        out[0] = (own[rs, :] + came[rs, :].astype(jnp.float32)).astype(out.dtype)
        start += out.shape[1]


def finish_grads(toks, own, came):
    vm = pl.BlockSpec(memory_space=pltpu.VMEM)
    return pl.pallas_call(
        finish_kernel,
        in_specs=[vm] * 2,
        out_specs=[vm] * len(toks),
        out_shape=shapes(*[(tok.shape, tok.dtype) for tok in toks]),
        compiler_params=pltpu.CompilerParams(vmem_limit_bytes=SMALL),
        cost_estimate=cost(2),
        name="finish_grads",
    )(own, came)


def tie(*groups):
    flat, tree = jax.tree.flatten(groups)
    return jax.tree.unflatten(tree, lax.optimization_barrier(flat))


class Chain:
    def __init__(self, name, scalars, orders, arrays):
        self.name, self.scalars, self.orders = name, scalars, orders
        bits = len(orders[0])
        self.lefts = [[bit for bit in range(bits)[::-1] if bit != order[0]] for order in orders]
        self.step = 0
        self.hold(arrays)

    def hold(self, arrays):
        self.sends, self.keeps = list(arrays[0::2]), list(arrays[1::2])

    def send(self):
        self.cames = [swap(value, "batch", 1 << order[self.step]) for value, order in zip(self.sends, self.orders)]
        self.step += 1

    def advance(self):
        bits = [order[self.step] for order in self.orders]
        if any(left != self.lefts[0] for left in self.lefts):
            self.hold(advance(self.name, self.scalars, self.lefts, bits, self.keeps, self.cames))
        else:
            self.hold(join(self.scalars, self.lefts[0], bits[0], self.keeps, self.cames))
            self.lefts, self.orders = self.lefts[:1], self.orders[:1]
        for left, bit in zip(self.lefts, bits):
            left.remove(bit)

    def more(self):
        return self.step < len(self.orders[0])


def per_device(
    tokens_long, tokens_mid, tokens_short, lengths_long, lengths_mid, lengths_short,
    w_query, b_query, w_key, w_value, b_value, w_out, b_out, gain_attn, beta_attn,
    w_inner, b_inner, w_outer, b_outer, gain_ffn, beta_ffn,
    cotangent_long, cotangent_mid, cotangent_short,
):
    toks = (tokens_long, tokens_mid, tokens_short)
    cots = (cotangent_long, cotangent_mid, cotangent_short)
    locals_ = tuple(tok.shape[1] for tok in toks)
    width = w_query.shape[0]
    inner_width = w_inner.shape[1]
    n = lax.axis_size("batch")
    bits = n.bit_length() - 1
    later = list(range(3, bits))
    orders = [[0, 1, 2] + later, [1, 2, 0] + later, [2, 0, 1] + later]
    firsts = [order[0] for order in orders]
    core = lax.axis_index("blk")
    place = lax.axis_index("batch")
    scalars = jnp.concatenate(
        [lengths_long, lengths_mid, lengths_short, jnp.stack([core, place]).astype(jnp.int32)]
    )
    others = [swap(tok, "blk", 1) for tok in toks]
    qa, keys, values, mixed, x, extra = attend_forward(scalars, toks, others, w_query, w_key, w_value, b_query, b_value)
    (
        out_long, out_mid, out_short, normed1, inverse1, slope, grad_outer, grad_second, vectors, keep_outer, send_outer,
    ) = ffn_forward(
        scalars, mixed, toks, cots, w_out, b_out, gain_attn, beta_attn, w_inner, b_inner, w_outer, b_outer, gain_ffn, beta_ffn
    )
    came_outer = swap(send_outer, "blk", 1)
    blocks = (locals_[0], locals_[1] + locals_[2])
    grad_sum, grad_mixed, vectors, keep_inner, send_inner = ffn_backward(
        scalars, blocks, mixed, normed1, inverse1, slope, grad_outer, grad_second, vectors,
        w_out, gain_attn, beta_attn, w_inner, w_outer,
    )
    came_inner = swap(send_inner, "blk", 1)
    pieces = []
    keeps, cames = [], []
    groups = width // LANES
    chain = None
    earlier = None
    for group in range(groups):
        if group == 1:
            vectors, keep_outer, keep_inner = tie(vectors, keep_outer, keep_inner)
            merged = ffn_merge(n, firsts, scalars, keep_outer, came_outer, keep_inner, came_inner)
            chain = Chain("ffn_step", scalars, orders, merged)
        if group > 2:
            done = (group - 1) // 2
            vectors, chain.keeps, cames[:done] = tie(vectors, chain.keeps, cames[:done])
            chain.advance()
        if group == 1 or group > 2:
            vectors, chain.sends = tie(vectors, chain.sends)
            chain.send()
        found = attend_backward(scalars, locals_, qa, keys, values, mixed, grad_mixed, x, extra, vectors, group, earlier)
        pieces.append(found[:3])
        vectors = found[3]
        earlier = found[4]
        if group % 2:
            keeps.append(found[4])
            cames.append(swap(found[5], "blk", 1))
    vectors_came = swap(vectors, "blk", 1)
    grad_queries, grad_keys, grad_values = zip(*pieces)
    send = input_grads(locals_, 1, jnp.bfloat16, (w_key, w_value, *grad_keys, *grad_values))
    chain.cames, send = tie(chain.cames, send)
    while chain.more():
        chain.advance()
        chain.send()
    keeps, send = tie(keeps, send)
    tail = Chain("attend_step", scalars, orders, attend_merge(n, firsts, scalars, vectors, vectors_came, keeps, cames))
    grad_sum, tail.sends = tie(grad_sum, tail.sends)
    tail.send()
    came = swap(send, "blk", 1)
    own = input_grads(
        locals_, 0, jnp.float32, (grad_sum, w_query, w_key, w_value, *grad_keys, *grad_values, *grad_queries)
    )
    own, tail.keeps = tie(own, tail.keeps)
    tail.advance()
    chain.keeps, own, tail.sends = tie(chain.keeps, own, tail.sends)
    tail.send()
    whole = last_sum(chain.keeps[0], chain.cames[0])
    grad_parts = list(finish_grads(toks, own, came))
    square = (width // n, width)
    grad_w_outer, grad_w_inner, grad_w_out = results(
        ffn_result_kernel, "ffn_results", scalars, whole, [(inner_width // n, width), (width // n, inner_width), square]
    )
    grad_parts, tail.keeps = tie(grad_parts, tail.keeps)
    tail.advance()
    tail.send()
    while tail.more():
        tail.advance()
        tail.send()
    (
        grad_w_query, grad_w_key, grad_w_value, grad_b_inner, grad_gain_ffn, grad_beta_ffn, grad_b_outer,
        grad_gain_attn, grad_beta_attn, grad_b_out, grad_b_query, grad_b_value,
    ) = results(
        partial(attend_result_kernel, groups // 2), "attend_results", scalars, last_sum(tail.keeps[0], tail.cames[0]),
        [square] * 3 + [(inner_width // n,)] + [(width // n,)] * 8,
    )
    return (
        out_long, out_mid, out_short, *grad_parts, grad_w_query, grad_b_query, grad_w_key, grad_w_value, grad_b_value,
        grad_w_out, grad_b_out, grad_gain_attn, grad_beta_attn, grad_w_inner, grad_b_inner, grad_w_outer, grad_b_outer,
        grad_gain_ffn, grad_beta_ffn,
    )


def solution(mesh):
    in_specs = (
        P("batch", "blk", None),
        P("batch", "blk", None),
        P("batch", "blk", None),
        P("batch"),
        P("batch"),
        P("batch"),
        P(),
        P(),
        P(),
        P(),
        P(),
        P(),
        P(),
        P(),
        P(),
        P(),
        P(),
        P(),
        P(),
        P(),
        P(),
        P("batch", "blk", None),
        P("batch", "blk", None),
        P("batch", "blk", None),
    )
    out_specs = (
        P("batch", "blk", None),
        P("batch", "blk", None),
        P("batch", "blk", None),
        P("batch", "blk", None),
        P("batch", "blk", None),
        P("batch", "blk", None),
        P("batch", None),
        P("batch"),
        P("batch", None),
        P("batch", None),
        P("batch"),
        P("batch", None),
        P("batch"),
        P("batch"),
        P("batch"),
        P("batch", None),
        P("batch"),
        P("batch", None),
        P("batch"),
        P("batch"),
        P("batch"),
    )
    return jax.shard_map(
        per_device, mesh=mesh, in_specs=in_specs, out_specs=out_specs, check_vma=False
    )
```

```python
from functools import partial

import jax
import jax.numpy as jnp
from jax import lax
from jax.experimental import pallas as pl
from jax.experimental.pallas import tpu as pltpu
from jax.sharding import PartitionSpec as P

HEADS = 12
LANES = 128
NT = (((1,), (1,)), ((), ()))
TN = (((0,), (0,)), ((), ()))
LOG2E = 1.4426950408889634
CHUNK = 1024
LIMIT = 58 * 1024 * 1024
MIDDLE = 58 * 1024 * 1024
FFN_LIMIT = 60 * 1024 * 1024
SMALL = 24 * 1024 * 1024
STEPS = 4
ANY = pl.BlockSpec(memory_space=pl.ANY)


def cost(microseconds):
    return pl.CostEstimate(flops=microseconds * 1_100_000_000, bytes_accessed=1_000_000, transcendentals=0)


def shapes(*items):
    return [jax.ShapeDtypeStruct(shape, dtype) for shape, dtype in items]


def sum_rows(field):
    return jnp.sum(field, axis=0, keepdims=True)


def dot(left, right, dims=(((1,), (0,)), ((), ()))):
    return lax.dot_general(left, right, dims, preferred_element_type=jnp.float32)


def split_low(value):
    high = value.astype(jnp.bfloat16).astype(jnp.float32)
    rest = value - high
    middle = rest.astype(jnp.bfloat16).astype(jnp.float32)
    return high, middle, rest - middle


def lane_ids(rows):
    return lax.broadcasted_iota(jnp.int32, (rows, LANES), 1)


def pick_head(block, head):
    lanes = lane_ids(block.shape[0])
    half = LANES // 2
    keep = (lanes < half) if head == 0 else (lanes >= half)
    return jnp.where(keep, block.astype(jnp.float32), 0.0).astype(jnp.bfloat16)


def pick_extra(block, head):
    lanes = lane_ids(block.shape[0])
    keep = (lanes == 0) | ((lanes >= 1 + 3 * head) & (lanes < 4 + 3 * head))
    return jnp.where(keep, block.astype(jnp.float32), 0.0).astype(jnp.bfloat16)


def place_extra(first, pieces):
    lanes = lane_ids(pieces[0].shape[0])
    block = jnp.where(lanes == 0, first, 0.0)
    for place, piece in enumerate(pieces):
        block = jnp.where(lanes == 1 + place, piece, block)
    return block.astype(jnp.bfloat16)


class Copies:
    def __init__(self, sems):
        self.sems, self.used, self.waiting = sems, 0, {}

    def start(self, name, source, target):
        copy = pltpu.make_async_copy(source, target, self.sems.at[self.used])
        copy.start()
        self.used += 1
        self.waiting[name] = copy

    def wait(self, name):
        copy = self.waiting.pop(name, None)
        if copy is not None:
            copy.wait()

    def wait_all(self):
        for name in list(self.waiting):
            self.wait(name)


def fill_extra(locals_, scalars, extra):
    core = scalars[3]
    offset = 0
    for half in range(2):
        for bucket, local in enumerate(locals_):
            owner = core if half == 0 else 1 - core
            lanes = lane_ids(local)
            places = lax.broadcasted_iota(jnp.int32, (local, LANES), 0) + owner * local
            bias = jnp.where(places < scalars[bucket], 0.0, -1e9)
            block = jnp.where(lanes == 0, bias, jnp.where(lanes < 7, 1.0, 0.0))
            extra[pl.ds(offset, local), :] = block.astype(jnp.bfloat16)
            offset += local


def spans_of(locals_):
    spans = []
    start = 0
    for local in locals_:
        spans.append((slice(start, start + local), slice(sum(locals_) + start, sum(locals_) + start + local)))
        start += local
    return spans


def pipelined(items, first, rest):
    ready = first(items[0])
    for place, item in enumerate(items):
        following = first(items[place + 1]) if place + 1 < len(items) else None
        rest(item, ready)
        ready = following


def forward_kernel(locals_, scalars, x_long, x_mid, x_short, y_long, y_mid, y_short,
                   w_query, w_key, w_value, b_query, b_value,
                   qa_out, keys_out, values_out, mixed_out, turned_out, extra, x, sems):
    step = pl.program_id(0)
    rows = sum(locals_)

    @pl.when(step == 0)
    def _():
        copies = Copies(sems)
        offset = 0
        for i, ref in enumerate((x_long, x_mid, x_short, y_long, y_mid, y_short)):
            copies.start(i, ref.at[0], x.at[pl.ds(offset, ref.shape[1])])
            offset += ref.shape[1]
        fill_extra(locals_, scalars, extra)
        copies.wait_all()

    wide = w_query.shape[1]
    pairs = wide // LANES
    both = dot(x[...], jnp.concatenate([w_key[...], w_value[...]], 1))
    keys = both[:, :wide].astype(jnp.bfloat16)
    values = (both[:, wide:] + b_value[...][None, :]).astype(jnp.bfloat16)
    keys_out[...] = keys
    values_out[...] = values
    queries = ((dot(x[pl.ds(0, rows), :], w_query[...]) + b_query[...][None, :]) * (0.125 * LOG2E)).astype(jnp.bfloat16)
    chunk = turned_out.shape[1]
    for i in range(chunk // LANES):
        start = pl.multiple_of(step * chunk + i * LANES, LANES)
        turned_out[:, pl.ds(i * LANES, LANES)] = x[pl.ds(start, LANES), :].T

    spans = spans_of(locals_)
    joint = lambda value, bucket: jnp.concatenate([value[span] for span in spans[bucket]], 0)
    cols = [slice(pair * LANES, (pair + 1) * LANES) for pair in range(pairs)]
    key_blocks = {}
    found = {}

    def scores_of(item):
        bucket, pair, head = item
        local = locals_[bucket]
        if head == 0:
            marks = jnp.concatenate([extra[span, :] for span in spans[bucket]], 0)
            key_blocks[bucket, pair] = jnp.concatenate([joint(keys[:, cols[pair]], bucket), marks], 1)
        one = jnp.where(lane_ids(local) == 0, 1.0, 0.0).astype(jnp.bfloat16)
        query = pick_head(queries[spans[bucket][0], cols[pair]], head)
        return dot(jnp.concatenate([query, one], 1), key_blocks[bucket, pair], NT)

    def mix(item, scores):
        bucket, pair, head = item
        top = jnp.max(scores, axis=-1, keepdims=True)
        weights = jnp.exp2(scores - top).astype(jnp.bfloat16)
        value = pick_head(joint(values[:, cols[pair]], bucket), head)
        result = dot(weights, jnp.concatenate([value, jnp.ones(value.shape, jnp.bfloat16)], 1))
        bulk = result[:, LANES:]
        found[item] = result[:, :LANES] / bulk, split_low(-(top + jnp.log2(bulk)))
        if head == 1:
            (left, some), (right, more) = found.pop((bucket, pair, 0)), found.pop(item)
            own = spans[bucket][0]
            mixed_out[own, cols[pair]] = (left + right).astype(jnp.bfloat16)
            at = 2 * pair * LANES
            qa_out[own, at : at + LANES] = queries[own, cols[pair]]
            qa_out[own, at + LANES : at + 2 * LANES] = place_extra(1.0, some + more)

    pipelined([(b, p, h) for b in range(len(locals_)) for p in range(pairs) for h in range(2)], scores_of, mix)


def attend_forward(scalars, mine, others, w_query, w_key, w_value, b_query, b_value):
    locals_ = tuple(part.shape[1] for part in mine)
    rows = sum(locals_)
    width = w_query.shape[0]
    steps = 3
    wide = width // steps
    low = jnp.bfloat16
    column = pl.BlockSpec((width, wide), lambda g: (0, g))
    bias = pl.BlockSpec((wide,), lambda g: (g,))
    return pl.pallas_call(
        partial(forward_kernel, locals_),
        grid=(steps,),
        in_specs=[pl.BlockSpec(memory_space=pltpu.SMEM)] + [ANY] * 6 + [column] * 3 + [bias] * 2,
        out_specs=[
            pl.BlockSpec((rows, 2 * wide), lambda g: (0, g)),
            pl.BlockSpec((2 * rows, wide), lambda g: (0, g)),
            pl.BlockSpec((2 * rows, wide), lambda g: (0, g)),
            pl.BlockSpec((rows, wide), lambda g: (0, g)),
            pl.BlockSpec((width, 2 * rows // steps), lambda g: (0, g)),
            pl.BlockSpec((2 * rows, LANES), lambda g: (0, 0)),
        ],
        out_shape=shapes(
            ((rows, 2 * width), low), ((2 * rows, width), low), ((2 * rows, width), low), ((rows, width), low),
            ((width, 2 * rows), low), ((2 * rows, LANES), low),
        ),
        scratch_shapes=[pltpu.VMEM((2 * rows, width), low), pltpu.SemaphoreType.DMA((6,))],
        compiler_params=pltpu.CompilerParams(vmem_limit_bytes=LIMIT),
        cost_estimate=cost(26),
        name="attend_forward",
    )(scalars, *mine, *others, w_query, w_key, w_value, b_query, b_value)


def backward_kernel(locals_, group, scalars, qa, keys, values, mixed, grad_mixed, turned_h, extra, vectors_in, *refs):
    if group % 2:
        earlier, *refs = refs
    grad_query, grad_keys, grad_values, vectors, *grad_w_refs, turned, sems = refs
    copies = Copies(sems)
    copies.start("turned", turned_h, turned)
    vectors[...] = vectors_in[...]
    spans = spans_of(locals_)
    joint = lambda ref, bucket: jnp.concatenate([ref[span, :] for span in spans[bucket]], 0)
    held = {}

    def prepare(bucket):
        own = spans[bucket][0]
        local = locals_[bucket]
        cot = grad_mixed[own, :]
        product = cot.astype(jnp.float32) * mixed[own, :].astype(jnp.float32)
        lanes = lane_ids(local)
        pieces = []
        for head in range(2):
            keep = (lanes < 64) if head == 0 else (lanes >= 64)
            delta = jnp.sum(jnp.where(keep, product, 0.0), axis=-1, keepdims=True)
            pieces.extend(split_low(-jnp.broadcast_to(delta, (local, LANES))))
        marks = joint(extra, bucket)
        key = joint(keys, bucket)
        return (
            qa[own, :LANES], qa[own, LANES:], cot, place_extra(0.0, pieces), key,
            jnp.concatenate([key, marks], 1), jnp.concatenate([joint(values, bucket), marks], 1),
        )

    def scores_of(item):
        bucket, head = item
        if head == 0:
            held[bucket] = prepare(bucket)
        query, more, cot, cot_more, _, key_block, value_block = held[bucket]
        query_one, cot_one = pick_head(query, head), pick_head(cot, head)
        return (
            dot(key_block, jnp.concatenate([query_one, pick_extra(more, head)], 1), NT),
            dot(value_block, jnp.concatenate([cot_one, pick_extra(cot_more, head)], 1), NT),
            query_one, cot_one,
        )

    sums = {}

    def spread(item, ready):
        bucket, head = item
        scores, change, query_one, cot_one = ready
        probs = jnp.exp2(scores)
        grad_scores = (probs * change).astype(jnp.bfloat16)
        terms = (
            dot(probs.astype(jnp.bfloat16), cot_one),
            dot(grad_scores, query_one),
            dot(grad_scores, pick_head(held[bucket][4], head), TN),
        )
        if head == 0:
            sums[bucket] = terms
            return
        value, key, query = (old + term for old, term in zip(sums.pop(bucket), terms))
        own, other = spans[bucket]
        local = locals_[bucket]
        grad_query[own, :] = (query * 0.125).astype(jnp.bfloat16)
        key = (key * (1.0 / LOG2E)).astype(jnp.bfloat16)
        value = value.astype(jnp.bfloat16)
        grad_keys[own, :], grad_keys[other, :] = key[:local], key[local:]
        grad_values[own, :], grad_values[other, :] = value[:local], value[local:]

    pipelined([(bucket, head) for bucket in range(len(locals_)) for head in range(2)], scores_of, spread)
    copies.wait_all()
    both = dot(turned[...], jnp.concatenate([grad_keys[...], grad_values[...]], 1))
    query = dot(turned[:, : sum(locals_)], grad_query[...])
    grad_w = [part.astype(jnp.bfloat16) for part in (query, both[:, :LANES], both[:, LANES:])]
    for i in range(3):
        if group % 2:
            store_halves(scalars[3], grad_w_refs[0].at[i], grad_w_refs[1].at[i], earlier[i], grad_w[i])
        else:
            grad_w_refs[0][i] = grad_w[i]
    cs = pl.ds(group * LANES, LANES)
    vectors[6:7, cs] = sum_rows(grad_query[...].astype(jnp.float32))
    vectors[7:8, cs] = sum_rows(grad_values[...].astype(jnp.float32))


def attend_backward(scalars, locals_, qa, keys, values, mixed, grad_mixed, turned, extra, vectors, group, earlier):
    rows = sum(locals_)
    width = turned.shape[0]
    low = jnp.bfloat16

    def col(n, w=LANES):
        return pl.BlockSpec((n, w), lambda g: (0, group))

    def whole(shape):
        return pl.BlockSpec(shape, lambda g: (0,) * len(shape))

    weights = (3, width, LANES)
    last = group % 2
    return pl.pallas_call(
        partial(backward_kernel, locals_, group),
        grid=(1,),
        in_specs=[pl.BlockSpec(memory_space=pltpu.SMEM), col(rows, 2 * LANES), col(2 * rows), col(2 * rows), col(rows), col(rows),
                  ANY, whole(extra.shape), whole(vectors.shape)] + [whole(weights)] * last,
        out_specs=[whole((rows, LANES)), whole((2 * rows, LANES)), whole((2 * rows, LANES)), whole(vectors.shape)]
        + [whole(weights)] * (1 + last),
        out_shape=shapes(
            ((rows, LANES), low), ((2 * rows, LANES), low), ((2 * rows, LANES), low), (vectors.shape, jnp.float32),
            *[(weights, low)] * (1 + last),
        ),
        scratch_shapes=[pltpu.VMEM(turned.shape, low), pltpu.SemaphoreType.DMA((1,))],
        compiler_params=pltpu.CompilerParams(vmem_limit_bytes=MIDDLE),
        cost_estimate=cost(9),
        name="attend_backward",
    )(scalars, qa, keys, values, mixed, grad_mixed, turned, extra, vectors, *([earlier] if last else []))


def gelu_and_slope(inner):
    share = 0.5 + 0.5 * lax.erf(inner * 0.7071067811865476)
    bell = jnp.exp2(inner * inner * (-0.5 * LOG2E))
    return inner * share, share + inner * bell * 0.3989422804014327


def mean_of(field):
    return jnp.sum(field, axis=-1, keepdims=True) * (1.0 / field.shape[-1])


def normalize(field):
    centered = field - mean_of(field)
    inverse = lax.rsqrt(mean_of(centered * centered) + 1e-12)
    return centered * inverse, inverse


def norm_back(grad, normed, inverse):
    return inverse * (grad - mean_of(grad) - normed * mean_of(grad * normed))


def store_halves(core, keep, send, low, high):
    first = core == 0
    keep[...] = jnp.where(first, low, high).astype(keep.dtype)
    send[...] = jnp.where(first, high, low).astype(send.dtype)


def ffn_kernel(blocks, scalars, mixed_h, tok_long, tok_mid, tok_short, cot_long, cot_mid, cot_short,
               w_out_h, b_out, gain_attn, beta_attn, w_inner_h, b_inner, w_outer_h, b_outer, gain_ffn, beta_ffn,
               out_long, out_mid, out_short, grad_sum_h, grad_mixed_h, vectors, keep_outer_h, send_outer_h, keep_inner_h, send_inner_h,
               mixed, toks, cots, w_out, w_inner, w_outer, hidden_s, slope_s, normed_s, second_s, first_s, outer_s, branch_s,
               out_s, grad_mixed, keep_outer, send_outer, keep_inner, send_inner, sems):
    width, inner_width = w_inner.shape
    chunks = inner_width // CHUNK
    copies = Copies(sems)
    copies.start("mixed", mixed_h, mixed)
    copies.start("w_out", w_out_h, w_out)
    places = []
    at = 0
    for i, ref in enumerate((tok_long, tok_mid, tok_short)):
        places.append(pl.ds(at, ref.shape[1]))
        copies.start(("tok", i), ref.at[0], toks.at[places[i]])
        at += ref.shape[1]
    columns = [pl.ds(j * CHUNK, CHUNK) for j in range(chunks)]
    for j, cs in enumerate(columns):
        copies.start(("inner", j), w_inner_h.at[:, cs], w_inner.at[:, cs])
        copies.start(("outer", j), w_outer_h.at[cs, :], w_outer.at[cs, :])
    for i, ref in enumerate((cot_long, cot_mid, cot_short)):
        copies.start(("cot", i), ref.at[0], cots.at[places[i]])

    full = jnp.float32
    low = jnp.bfloat16
    spans = [pl.ds(0, blocks[0]), pl.ds(blocks[0], blocks[1])]
    inverses, sums = [None] * 2, {}

    def add(name, value):
        sums[name] = value if name not in sums else sums[name] + value

    def enter(b):
        rs = spans[b]
        field = toks[rs, :].astype(full) + dot(mixed[rs, :], w_out[...]) + b_out[...][None, :]
        normed, inverses[b] = normalize(field)
        normed_s[rs, :] = normed
        first = normed * gain_attn[...][None, :] + beta_attn[...][None, :]
        first_s[rs, :] = first.astype(low)
        second_s[rs, :] = first + b_outer[...][None, :]

    def forward(b, between):
        rs = spans[b]
        copies.wait(("inner", 0))
        work = {0: dot(first_s[rs, :], w_inner[:, columns[0]])}
        for j, cs in enumerate(columns):
            if j + 1 < chunks:
                copies.wait(("inner", j + 1))
                work[j + 1] = dot(first_s[rs, :], w_inner[:, columns[j + 1]])
            value, rate = gelu_and_slope(work.pop(j) + b_inner[cs][None, :])
            hidden = value.astype(low)
            hidden_s[rs, cs] = hidden
            slope_s[rs, cs] = rate.astype(low)
            copies.wait(("outer", j))
            second_s[rs, :] += dot(hidden_s[rs, cs], w_outer[cs, :])
            if j == 0:
                between()

    def leave(b):
        rs = spans[b]
        normed, inverse = normalize(second_s[rs, :])
        out_s[rs, :] = (normed * gain_ffn[...][None, :] + beta_ffn[...][None, :]).astype(low)
        cot = cots[rs, :].astype(full)
        back = norm_back(cot * gain_ffn[...][None, :], normed, inverse)
        second_s[rs, :] = back
        rounded = back.astype(low)
        outer_s[rs, :] = rounded
        add("gain_ffn", sum_rows(cot * normed))
        add("beta_ffn", sum_rows(cot))
        add("b_outer", sum_rows(rounded.astype(full)))

    def backward(b, between):
        rs = spans[b]
        work = {0: dot(outer_s[rs, :], w_outer[columns[0], :], NT)}
        for j, cs in enumerate(columns):
            if j + 1 < chunks:
                work[j + 1] = dot(outer_s[rs, :], w_outer[columns[j + 1], :], NT)
            rounded = (work.pop(j) * slope_s[rs, cs].astype(full)).astype(low)
            slope_s[rs, cs] = rounded
            add(("b_inner", j), sum_rows(rounded.astype(full)))
            second_s[rs, :] += dot(slope_s[rs, cs], w_inner[:, cs], NT)
            if j == 0:
                between()

    def finish(b):
        rs = spans[b]
        total = second_s[rs, :]
        normed = normed_s[rs, :]
        back = norm_back(total * gain_attn[...][None, :], normed, inverses[b])
        add("gain_attn", sum_rows(total * normed))
        add("beta_attn", sum_rows(total))
        normed_s[rs, :] = back
        rounded = back.astype(low)
        branch_s[rs, :] = rounded
        add("b_out", sum_rows(rounded.astype(full)))
        grad_mixed[rs, :] = dot(rounded, w_out[...], NT).astype(low)

    core = scalars[3]
    half = width // 2

    def outer_weights(chosen):
        for j in chosen:
            cs = columns[j]
            whole = dot(hidden_s[:, cs], outer_s[...], TN)
            for p in range(3):
                near, far = whole[:, p * LANES : (p + 1) * LANES], whole[:, half + p * LANES : half + (p + 1) * LANES]
                store_halves(core, keep_outer.at[p, cs, :], send_outer.at[p, cs, :], near, far)

    copies.wait("mixed")
    copies.wait("w_out")
    for i in range(3):
        copies.wait(("tok", i))
    enter(0)
    enter(1)
    forward(0, lambda: None)
    for i in range(3):
        copies.wait(("cot", i))
    forward(1, lambda: leave(0))
    backward(0, lambda: leave(1))
    for i, ref in enumerate((out_long, out_mid, out_short)):
        copies.start(("out", i), out_s.at[places[i]], ref.at[0])
    outer_weights(range(chunks // 3))
    backward(1, lambda: finish(0))
    outer_weights(range(chunks // 3, chunks - 1))
    finish(1)
    outer_weights(range(chunks - 1, chunks))
    for p in range(3):
        copies.start(("send_outer", p), send_outer.at[p], send_outer_h.at[p])
        copies.start(("keep_outer", p), keep_outer.at[p], keep_outer_h.at[p])
    copies.start("grad_mixed", grad_mixed, grad_mixed_h)
    copies.start("grad_sum", normed_s, grad_sum_h)
    part = inner_width // 6
    turned = first_s[...].T
    for p in range(3):
        near = dot(turned, slope_s[:, pl.ds(p * part, part)])
        far = dot(turned, slope_s[:, pl.ds(inner_width // 2 + p * part, part)])
        cs = pl.ds(0, part)
        store_halves(core, keep_inner.at[p, :, cs], send_inner.at[p, :, cs], near, far)
    whole = dot(mixed[...], branch_s[...], TN)
    for p in range(3):
        near, far = whole[:, p * LANES : (p + 1) * LANES], whole[:, half + p * LANES : half + (p + 1) * LANES]
        cs = pl.ds(part, LANES)
        store_halves(core, keep_inner.at[p, :, cs], send_inner.at[p, :, cs], near, far)
        copies.start(("send_inner", p), send_inner.at[p], send_inner_h.at[p])
        copies.start(("keep_inner", p), keep_inner.at[p], keep_inner_h.at[p])
    for i, name in enumerate(("gain_ffn", "beta_ffn", "b_outer", "gain_attn", "beta_attn", "b_out")):
        vectors[pl.ds(i, 1), :] = sums[name]
    vectors[6:16, :] = jnp.zeros((10, width), full)
    line = jnp.concatenate([sums["b_inner", j] for j in range(chunks)], 1)
    for i in range(inner_width // width):
        vectors[pl.ds(16 + i, 1), :] = line[:, i * width : (i + 1) * width]
    copies.wait_all()


def ffn(scalars, mixed, toks, cots, w_out, b_out, gain_attn, beta_attn, w_inner, b_inner, w_outer, b_outer, gain_ffn, beta_ffn):
    rows, width = mixed.shape
    inner_width = w_inner.shape[1]
    low, full = jnp.bfloat16, jnp.float32
    blocks = (toks[0].shape[1], toks[1].shape[1] + toks[2].shape[1])
    vm = pl.BlockSpec(memory_space=pltpu.VMEM)
    outer = (3, inner_width, LANES)
    inner = (3, width, inner_width // 6 + LANES)
    square = (rows, width)
    wide = (rows, inner_width)
    vectors = (16 + inner_width // width, width)
    scratch = [
        (square, low), (square, low), (square, low), (w_out.shape, low), (w_inner.shape, low), (w_outer.shape, low),
        (wide, low), (wide, low), (square, full), (square, full), (square, low), (square, low), (square, low),
        (square, low), (square, low), (outer, low), (outer, low), (inner, low), (inner, low),
    ]
    return pl.pallas_call(
        partial(ffn_kernel, blocks),
        in_specs=[pl.BlockSpec(memory_space=pltpu.SMEM)] + [ANY] * 7 + [ANY, vm, vm, vm, ANY, vm, ANY, vm, vm, vm],
        out_specs=[ANY] * 5 + [vm] + [ANY] * 4,
        out_shape=shapes(
            *[(tok.shape, low) for tok in toks], (square, full), (square, low), (vectors, full),
            (outer, low), (outer, low), (inner, low), (inner, low),
        ),
        scratch_shapes=[pltpu.VMEM(shape, dtype) for shape, dtype in scratch]
        + [pltpu.SemaphoreType.DMA((8 + 2 * (inner_width // CHUNK) + 17,))],
        compiler_params=pltpu.CompilerParams(vmem_limit_bytes=FFN_LIMIT),
        cost_estimate=cost(50),
        name="ffn_all",
    )(scalars, mixed, *toks, *cots, w_out, b_out, gain_attn, beta_attn, w_inner, b_inner, w_outer, b_outer, gain_ffn, beta_ffn)


def input_kernel(half, *refs):
    out = refs[-1]
    if half == 0:
        grad_sum, w_query, *refs = refs
    w_key, w_value, *parts = refs[:-1]
    count = len(parts) // (3 - half)
    keys, values, queries = parts[:count], parts[count : 2 * count], parts[2 * count :]
    rows = out.shape[0]
    span = slice(half * rows, (half + 1) * rows)
    beside = lambda blocks, rows: jnp.concatenate([block[rows, :] for block in blocks], 1)
    total = dot(beside(keys, span), w_key[...], NT) + dot(beside(values, span), w_value[...], NT)
    if half == 0:
        total = total + grad_sum[...] + dot(beside(queries, span), w_query[...], NT)
    out[...] = total.astype(out.dtype)


def input_grads(locals_, half, dtype, operands):
    vm = pl.BlockSpec(memory_space=pltpu.VMEM)
    rows, width = sum(locals_), operands[0].shape[1]
    return pl.pallas_call(
        partial(input_kernel, half),
        in_specs=[vm] * len(operands),
        out_specs=vm,
        out_shape=jax.ShapeDtypeStruct((rows, width), dtype),
        compiler_params=pltpu.CompilerParams(vmem_limit_bytes=MIDDLE),
        cost_estimate=cost(8 - 2 * half),
        name="input_grads",
    )(*operands)


def swap(value, axis, bit):
    return lax.ppermute(value, axis, [(i, i ^ bit) for i in range(lax.axis_size(axis))])


def up16(rows):
    return -(-rows // 16) * 16


def halves_of(shards, left, bit):
    place = left.index(bit)
    return 2**place, shards // 2 ** (place + 1)


def steps_of(pairs):
    steps = min(pairs, STEPS)
    return steps, pairs // steps


def half_spec(array, above, below, lead=None):
    _, many = steps_of(above * below)
    if below >= many:
        block = (1, 2, many)
        index = lambda k: (k * many // below, 0, k * many % below // many)
    else:
        block = (many // below, 2, below)
        index = lambda k: (k, 0, 0)
    shape = block + array.shape[-2:]
    if lead is None:
        return pl.BlockSpec(shape, lambda k, s: index(k) + (0, 0))
    return pl.BlockSpec((None,) + shape, lambda k, s: (lead,) + index(k) + (0, 0))


def pairs_in(ref):
    above, below = ref.shape[0], ref.shape[2]
    return [(a * below + b, a, b) for a in range(above) for b in range(below)]


def call_halving(body, name, scalars, pairs, operands, specs, outs):
    steps, many = steps_of(pairs)
    blocks = [(many,) + tuple(out) for out in outs for _ in range(2)]
    return pl.pallas_call(
        body,
        grid_spec=pltpu.PrefetchScalarGridSpec(
            num_scalar_prefetch=1,
            grid=(steps,),
            in_specs=specs,
            out_specs=[pl.BlockSpec(block, lambda k, s: (k, 0, 0)) for block in blocks],
        ),
        out_shape=shapes(*[((pairs,) + block[1:], jnp.bfloat16) for block in blocks]),
        compiler_params=pltpu.CompilerParams(vmem_limit_bytes=SMALL),
        cost_estimate=cost(2),
        name=name,
    )(scalars, *operands)


def bit_of(scalars, bit):
    return (scalars[4] >> bit) & 1


def ffn_merge_kernel(bits, scalars, *refs):
    ins, outs = refs[:12], refs[12:]
    for p in range(3):
        keep_outer, came_outer, keep_inner, came_inner = ins[4 * p : 4 * p + 4]
        mine = bit_of(scalars, bits[p])
        for out, which in zip(outs[2 * p : 2 * p + 2], (1 - mine, mine)):
            for k, a, b in pairs_in(keep_outer):
                first = keep_outer[a, which, b] + came_outer[a, which, b]
                rows = first.shape[0]
                out[k, pl.ds(0, rows), :] = first
                second = keep_inner[a, which, b] + came_inner[a, which, b]
                at = up16(rows)
                rows = second.shape[0]
                for q in range(second.shape[1] // LANES):
                    out[k, pl.ds(at, rows), :] = second[:, q * LANES : (q + 1) * LANES]
                    at += up16(rows)


def ffn_merge(n, bits, scalars, keep_outer, came_outer, keep_inner, came_inner):
    operands, specs = [], []
    left = list(range(n.bit_length() - 1))[::-1]
    for p in range(3):
        above, below = halves_of(n, left, bits[p])
        for array in (keep_outer, came_outer, keep_inner, came_inner):
            view = array.reshape(3, above, 2, below, array.shape[1] // n, array.shape[2])
            operands.append(view)
            specs.append(half_spec(view, above, below, p))
    height = up16(keep_outer.shape[1] // n) + keep_inner.shape[2] // LANES * up16(keep_inner.shape[1] // n)
    return call_halving(
        partial(ffn_merge_kernel, bits), "ffn_merge", scalars, n // 2, operands, specs, [(height, LANES)] * 3
    )


def own_columns(line, start, size):
    width = line.shape[1]
    lanes = -(-size // LANES) * LANES
    from_ = lax.broadcasted_iota(jnp.int32, (width, lanes), 0)
    to = lax.broadcasted_iota(jnp.int32, (width, lanes), 1)
    chosen = jnp.where((from_ == start + to) & (to < size), 1.0, 0.0).astype(jnp.bfloat16)
    return dot(line.astype(jnp.bfloat16), chosen)


def attend_merge_kernel(n, bits, scalars, vectors, vectors_came, *refs):
    count = (len(refs) - 6) // 6
    ins, outs = refs[: 6 * count], refs[6 * count :]
    many = outs[0].shape[0]
    for p in range(3):
        mine = bit_of(scalars, bits[p])
        for out, which in zip(outs[2 * p : 2 * p + 2], (1 - mine, mine)):
            at = 0
            for t in range(count):
                keep, came = ins[2 * (p * count + t) : 2 * (p * count + t) + 2]
                for k, a, b in pairs_in(keep):
                    total = keep[a, which, b] + came[a, which, b]
                    rows = total.shape[0]
                    out[k, pl.ds(at, rows), :] = total
                at += up16(rows)
            if p > 0:
                continue
            below = 2 ** bits[0]
            for k in range(many):
                pair = pl.program_id(0) * many + k
                shard = (pair // below * 2 + which) * below + pair % below
                small = vectors[...] + vectors_came[...]
                width = small.shape[1]
                found = own_columns(small, shard * (width // n), width // n)
                inner = small.shape[0] - 16
                per = inner * width // n
                span = n // inner
                line = jnp.zeros((1, width), jnp.float32)
                for i in range(inner):
                    line = jnp.where(shard // span == i, small[16 + i : 17 + i], line)
                wide = own_columns(jnp.broadcast_to(line, (8, width)), shard % span * per, per)
                groups = [wide[:1, g * LANES : (g + 1) * LANES] for g in range(wide.shape[1] // LANES)]
                block = jnp.concatenate([found[: 16 - len(groups)]] + groups, 0)
                out[k, pl.ds(at, 16), :] = block.astype(out.dtype)


def attend_merge(n, bits, scalars, vectors, vectors_came, keeps, cames):
    whole = pl.BlockSpec(vectors.shape, lambda k, s: (0, 0))
    operands, specs = [vectors, vectors_came], [whole, whole]
    left = list(range(n.bit_length() - 1))[::-1]
    for p in range(3):
        above, below = halves_of(n, left, bits[p])
        for pair in zip(keeps, cames):
            for array in pair:
                view = array.reshape(3, above, 2, below, array.shape[1] // n, array.shape[2])
                operands.append(view)
                specs.append(half_spec(view, above, below, p))
    height = len(keeps) * up16(keeps[0].shape[1] // n)
    return call_halving(
        partial(attend_merge_kernel, n, bits), "attend_merge", scalars, n // 2, operands, specs,
        [(height + 16, LANES), (height, LANES), (height, LANES)],
    )


def advance_kernel(bits, scalars, *refs):
    count = len(bits)
    for p, bit in enumerate(bits):
        keep, came = refs[2 * p : 2 * p + 2]
        mine = bit_of(scalars, bit)
        for out, which in zip(refs[2 * (count + p) : 2 * (count + p) + 2], (1 - mine, mine)):
            for k, a, b in pairs_in(keep):
                out[k] = keep[a, which, b] + came[a, which, b]


def advance(name, scalars, lefts, bits, keeps, cames):
    operands, specs = [], []
    shards = keeps[0].shape[0]
    for left, bit, keep, came in zip(lefts, bits, keeps, cames):
        above, below = halves_of(shards, left, bit)
        for array in (keep, came):
            view = array.reshape(above, 2, below, *array.shape[1:])
            operands.append(view)
            specs.append(half_spec(view, above, below))
    return call_halving(
        partial(advance_kernel, bits), name, scalars, shards // 2, operands, specs, [keep.shape[1:] for keep in keeps]
    )


def join_kernel(bit, count, scalars, *refs):
    send, kept = refs[2 * count :]
    mine = bit_of(scalars, bit)
    at = 0
    for p in range(count):
        keep, came = refs[2 * p : 2 * p + 2]
        rows = keep.shape[-2]
        for out, which in ((send, 1 - mine), (kept, mine)):
            for k, a, b in pairs_in(keep):
                out[k, pl.ds(at, rows), :] = keep[a, which, b] + came[a, which, b]
        at += rows


def join(scalars, left, bit, keeps, cames):
    operands, specs = [], []
    shards = keeps[0].shape[0]
    above, below = halves_of(shards, left, bit)
    for keep, came in zip(keeps, cames):
        for array in (keep, came):
            view = array.reshape(above, 2, below, *array.shape[1:])
            operands.append(view)
            specs.append(half_spec(view, above, below))
    height = sum(keep.shape[1] for keep in keeps)
    return call_halving(
        partial(join_kernel, bit, len(keeps)), "join_portions", scalars, shards // 2, operands, specs, [(height, LANES)]
    )


def last_kernel(keep, came, out):
    out[...] = keep[0] + came[0]


def last_sum(keep, came):
    vm = pl.BlockSpec(memory_space=pltpu.VMEM)
    return pl.pallas_call(
        last_kernel,
        in_specs=[vm] * 2,
        out_specs=vm,
        out_shape=jax.ShapeDtypeStruct(keep.shape[1:], keep.dtype),
        cost_estimate=cost(2),
        name="last_sum",
    )(keep, came)


def placer(scalars, mine, other):
    first = scalars[3] == 0
    at = 0

    def place(ref, left, right, size):
        nonlocal at
        a = mine[pl.ds(at, size), :].astype(jnp.float32)
        b = other[pl.ds(at, size), :].astype(jnp.float32)
        ref[:, pl.ds(left, LANES)] = jnp.where(first, a, b)
        ref[:, pl.ds(right, LANES)] = jnp.where(first, b, a)
        at += up16(size)

    def skip(size):
        nonlocal at
        at += size
        return at - size

    return place, skip


def ffn_result_kernel(scalars, mine, other, w_outer, w_inner, w_out):
    place, _ = placer(scalars, mine, other)
    rows, width = w_out.shape
    half = width // 2
    inner_half = w_inner.shape[1] // 2
    for p in range(3):
        place(w_outer, p * LANES, half + p * LANES, w_outer.shape[0])
        for q in range(inner_half // 3 // LANES):
            column = p * (inner_half // 3) + q * LANES
            place(w_inner, column, inner_half + column, rows)
        place(w_out, p * LANES, half + p * LANES, rows)


def attend_result_kernel(count, scalars, mine, other, w_query, w_key, w_value, b_inner, *lines):
    place, skip = placer(scalars, mine, other)
    rows = w_query.shape[0]
    for ref in (w_query, w_key, w_value):
        for t in range(count):
            place(ref, 2 * t * LANES, (2 * t + 1) * LANES, rows)
        if ref is w_query:
            small = mine[pl.ds(skip(16), 16), :].astype(jnp.float32)
    for i, ref in enumerate(lines):
        ref[...] = small[i, :rows]
    size = b_inner.shape[0]
    groups = -(-size // LANES)
    for g in range(groups):
        part = min(LANES, size - g * LANES)
        b_inner[pl.ds(g * LANES, part)] = small[16 - groups + g, :part]


def results(body, name, scalars, mine, outs):
    vm = pl.BlockSpec(memory_space=pltpu.VMEM)
    return pl.pallas_call(
        body,
        in_specs=[pl.BlockSpec(memory_space=pltpu.SMEM), vm, vm],
        out_specs=[vm] * len(outs),
        out_shape=shapes(*[(out, jnp.float32) for out in outs]),
        compiler_params=pltpu.CompilerParams(vmem_limit_bytes=SMALL),
        cost_estimate=cost(2),
        name=name,
    )(scalars, mine, swap(mine, "blk", 1))


def finish_kernel(own, came, *outs):
    start = 0
    for out in outs:
        rs = pl.ds(start, out.shape[1])
        out[0] = (own[rs, :] + came[rs, :].astype(jnp.float32)).astype(out.dtype)
        start += out.shape[1]


def finish_grads(toks, own, came):
    vm = pl.BlockSpec(memory_space=pltpu.VMEM)
    return pl.pallas_call(
        finish_kernel,
        in_specs=[vm] * 2,
        out_specs=[vm] * len(toks),
        out_shape=shapes(*[(tok.shape, tok.dtype) for tok in toks]),
        compiler_params=pltpu.CompilerParams(vmem_limit_bytes=SMALL),
        cost_estimate=cost(2),
        name="finish_grads",
    )(own, came)


def tie(*groups):
    flat, tree = jax.tree.flatten(groups)
    return jax.tree.unflatten(tree, lax.optimization_barrier(flat))


class Chain:
    def __init__(self, name, scalars, orders, arrays):
        self.name, self.scalars, self.orders = name, scalars, orders
        bits = len(orders[0])
        self.lefts = [[bit for bit in range(bits)[::-1] if bit != order[0]] for order in orders]
        self.step = 0
        self.hold(arrays)

    def hold(self, arrays):
        self.sends, self.keeps = list(arrays[0::2]), list(arrays[1::2])

    def send(self):
        self.cames = [swap(value, "batch", 1 << order[self.step]) for value, order in zip(self.sends, self.orders)]
        self.step += 1

    def advance(self):
        bits = [order[self.step] for order in self.orders]
        if any(left != self.lefts[0] for left in self.lefts):
            self.hold(advance(self.name, self.scalars, self.lefts, bits, self.keeps, self.cames))
        else:
            self.hold(join(self.scalars, self.lefts[0], bits[0], self.keeps, self.cames))
            self.lefts, self.orders = self.lefts[:1], self.orders[:1]
        for left, bit in zip(self.lefts, bits):
            left.remove(bit)

    def more(self):
        return self.step < len(self.orders[0])


def per_device(
    tokens_long, tokens_mid, tokens_short, lengths_long, lengths_mid, lengths_short,
    w_query, b_query, w_key, w_value, b_value, w_out, b_out, gain_attn, beta_attn,
    w_inner, b_inner, w_outer, b_outer, gain_ffn, beta_ffn,
    cotangent_long, cotangent_mid, cotangent_short,
):
    toks = (tokens_long, tokens_mid, tokens_short)
    cots = (cotangent_long, cotangent_mid, cotangent_short)
    locals_ = tuple(tok.shape[1] for tok in toks)
    width = w_query.shape[0]
    inner_width = w_inner.shape[1]
    n = lax.axis_size("batch")
    bits = n.bit_length() - 1
    later = list(range(3, bits))
    orders = [[0, 1, 2] + later, [1, 2, 0] + later, [2, 0, 1] + later]
    firsts = [order[0] for order in orders]
    core = lax.axis_index("blk")
    place = lax.axis_index("batch")
    scalars = jnp.concatenate(
        [lengths_long, lengths_mid, lengths_short, jnp.stack([core, place]).astype(jnp.int32)]
    )
    others = [swap(tok, "blk", 1) for tok in toks]
    qa, keys, values, mixed, turned, extra = attend_forward(scalars, toks, others, w_query, w_key, w_value, b_query, b_value)
    out_long, out_mid, out_short, grad_sum, grad_mixed, vectors, keep_outer, send_outer, keep_inner, send_inner = ffn(
        scalars, mixed, toks, cots, w_out, b_out, gain_attn, beta_attn, w_inner, b_inner, w_outer, b_outer, gain_ffn, beta_ffn
    )
    came_outer = swap(send_outer, "blk", 1)
    came_inner = swap(send_inner, "blk", 1)
    pieces = []
    keeps, cames = [], []
    groups = width // LANES
    chain = None
    earlier = None
    for group in range(groups):
        if group == 1:
            vectors, keep_outer, keep_inner = tie(vectors, keep_outer, keep_inner)
            merged = ffn_merge(n, firsts, scalars, keep_outer, came_outer, keep_inner, came_inner)
            chain = Chain("ffn_step", scalars, orders, merged)
        if group > 2:
            done = (group - 1) // 2
            vectors, chain.keeps, cames[:done] = tie(vectors, chain.keeps, cames[:done])
            chain.advance()
        if group == 1 or group > 2:
            vectors, chain.sends = tie(vectors, chain.sends)
            chain.send()
        found = attend_backward(scalars, locals_, qa, keys, values, mixed, grad_mixed, turned, extra, vectors, group, earlier)
        pieces.append(found[:3])
        vectors = found[3]
        earlier = found[4]
        if group % 2:
            keeps.append(found[4])
            cames.append(swap(found[5], "blk", 1))
    vectors_came = swap(vectors, "blk", 1)
    grad_queries, grad_keys, grad_values = zip(*pieces)
    send = input_grads(locals_, 1, jnp.bfloat16, (w_key, w_value, *grad_keys, *grad_values))
    chain.cames, send = tie(chain.cames, send)
    while chain.more():
        chain.advance()
        chain.send()
    keeps, send = tie(keeps, send)
    tail = Chain("attend_step", scalars, orders, attend_merge(n, firsts, scalars, vectors, vectors_came, keeps, cames))
    grad_sum, tail.sends = tie(grad_sum, tail.sends)
    tail.send()
    came = swap(send, "blk", 1)
    own = input_grads(
        locals_, 0, jnp.float32, (grad_sum, w_query, w_key, w_value, *grad_keys, *grad_values, *grad_queries)
    )
    own, tail.keeps = tie(own, tail.keeps)
    tail.advance()
    chain.keeps, own, tail.sends = tie(chain.keeps, own, tail.sends)
    tail.send()
    whole = last_sum(chain.keeps[0], chain.cames[0])
    grad_parts = list(finish_grads(toks, own, came))
    square = (width // n, width)
    grad_w_outer, grad_w_inner, grad_w_out = results(
        ffn_result_kernel, "ffn_results", scalars, whole, [(inner_width // n, width), (width // n, inner_width), square]
    )
    grad_parts, tail.keeps = tie(grad_parts, tail.keeps)
    tail.advance()
    tail.send()
    while tail.more():
        tail.advance()
        tail.send()
    (
        grad_w_query, grad_w_key, grad_w_value, grad_b_inner, grad_gain_ffn, grad_beta_ffn, grad_b_outer,
        grad_gain_attn, grad_beta_attn, grad_b_out, grad_b_query, grad_b_value,
    ) = results(
        partial(attend_result_kernel, groups // 2), "attend_results", scalars, last_sum(tail.keeps[0], tail.cames[0]),
        [square] * 3 + [(inner_width // n,)] + [(width // n,)] * 8,
    )
    return (
        out_long, out_mid, out_short, *grad_parts, grad_w_query, grad_b_query, grad_w_key, grad_w_value, grad_b_value,
        grad_w_out, grad_b_out, grad_gain_attn, grad_beta_attn, grad_w_inner, grad_b_inner, grad_w_outer, grad_b_outer,
        grad_gain_ffn, grad_beta_ffn,
    )


def solution(mesh):
    in_specs = (
        P("batch", "blk", None),
        P("batch", "blk", None),
        P("batch", "blk", None),
        P("batch"),
        P("batch"),
        P("batch"),
        P(),
        P(),
        P(),
        P(),
        P(),
        P(),
        P(),
        P(),
        P(),
        P(),
        P(),
        P(),
        P(),
        P(),
        P(),
        P("batch", "blk", None),
        P("batch", "blk", None),
        P("batch", "blk", None),
    )
    out_specs = (
        P("batch", "blk", None),
        P("batch", "blk", None),
        P("batch", "blk", None),
        P("batch", "blk", None),
        P("batch", "blk", None),
        P("batch", "blk", None),
        P("batch", None),
        P("batch"),
        P("batch", None),
        P("batch", None),
        P("batch"),
        P("batch", None),
        P("batch"),
        P("batch"),
        P("batch"),
        P("batch", None),
        P("batch"),
        P("batch", None),
        P("batch"),
        P("batch"),
        P("batch"),
    )
    return jax.shard_map(
        per_device, mesh=mesh, in_specs=in_specs, out_specs=out_specs, check_vma=False
    )
```

```python
import math
from functools import partial

import jax
import jax.numpy as jnp
from jax import lax
from jax.experimental import pallas as pl
from jax.experimental.pallas import tpu as pltpu
from jax.sharding import PartitionSpec as P

HEADS = 12
LANES = 128
NT = (((1,), (1,)), ((), ()))
TN = (((0,), (0,)), ((), ()))
LOG2E = 1.4426950408889634
CHUNK = 1024
LIMIT = 58 * 1024 * 1024
MIDDLE = 32 * 1024 * 1024
FFN_LIMIT = 60 * 1024 * 1024
SMALL = 24 * 1024 * 1024
STEPS = 2
ANY = pl.BlockSpec(memory_space=pl.ANY)


def cost(microseconds):
    return pl.CostEstimate(flops=microseconds * 1_100_000_000, bytes_accessed=1_000_000, transcendentals=0)


def shapes(*items):
    return [jax.ShapeDtypeStruct(shape, dtype) for shape, dtype in items]


def sum_rows(field):
    return jnp.sum(field, axis=0, keepdims=True)


def dot(left, right, dims=(((1,), (0,)), ((), ()))):
    return lax.dot_general(left, right, dims, preferred_element_type=jnp.float32)


def split_low(value):
    high = value.astype(jnp.bfloat16).astype(jnp.float32)
    rest = value - high
    middle = rest.astype(jnp.bfloat16).astype(jnp.float32)
    return high, middle, rest - middle


def lane_ids(rows):
    return lax.broadcasted_iota(jnp.int32, (rows, LANES), 1)


def pick_head(block, head):
    lanes = lane_ids(block.shape[0])
    half = LANES // 2
    keep = (lanes < half) if head == 0 else (lanes >= half)
    return jnp.where(keep, block.astype(jnp.float32), 0.0).astype(jnp.bfloat16)


def pick_extra(block, head):
    lanes = lane_ids(block.shape[0])
    keep = (lanes == 0) | ((lanes >= 1 + 3 * head) & (lanes < 4 + 3 * head))
    return jnp.where(keep, block.astype(jnp.float32), 0.0).astype(jnp.bfloat16)


def place_extra(first, pieces):
    lanes = lane_ids(pieces[0].shape[0])
    block = jnp.where(lanes == 0, first, 0.0)
    for place, piece in enumerate(pieces):
        block = jnp.where(lanes == 1 + place, piece, block)
    return block.astype(jnp.bfloat16)


class Copies:
    def __init__(self, sems):
        self.sems, self.used, self.waiting = sems, 0, {}

    def start(self, name, source, target):
        copy = pltpu.make_async_copy(source, target, self.sems.at[self.used])
        copy.start()
        self.used += 1
        self.waiting[name] = copy

    def wait(self, name):
        copy = self.waiting.pop(name, None)
        if copy is not None:
            copy.wait()

    def wait_all(self):
        for name in list(self.waiting):
            self.wait(name)


def fill_extra(locals_, scalars, extra):
    core = scalars[3]
    offset = 0
    for half in range(2):
        for bucket, local in enumerate(locals_):
            owner = core if half == 0 else 1 - core
            lanes = lane_ids(local)
            places = lax.broadcasted_iota(jnp.int32, (local, LANES), 0) + owner * local
            bias = jnp.where(places < scalars[bucket], 0.0, -1e9)
            block = jnp.where(lanes == 0, bias, jnp.where(lanes < 7, 1.0, 0.0))
            extra[pl.ds(offset, local), :] = block.astype(jnp.bfloat16)
            offset += local


def spans_of(locals_):
    spans = []
    start = 0
    for local in locals_:
        spans.append((slice(start, start + local), slice(sum(locals_) + start, sum(locals_) + start + local)))
        start += local
    return spans


def pipelined(items, first, rest):
    ready = first(items[0])
    for place, item in enumerate(items):
        following = first(items[place + 1]) if place + 1 < len(items) else None
        rest(item, ready)
        ready = following


def forward_kernel(locals_, scalars, x_long, x_mid, x_short, y_long, y_mid, y_short,
                   w_query, w_key, w_value, b_query, b_value,
                   qa_out, keys_out, values_out, mixed_out, paired_out, turned_out, extra, x, sems):
    step = pl.program_id(0)
    rows = sum(locals_)

    @pl.when(step == 0)
    def _():
        copies = Copies(sems)
        offset = 0
        for i, ref in enumerate((x_long, x_mid, x_short, y_long, y_mid, y_short)):
            copies.start(i, ref.at[0], x.at[pl.ds(offset, ref.shape[1])])
            offset += ref.shape[1]
        fill_extra(locals_, scalars, extra)
        copies.wait_all()

    wide = w_query.shape[1]
    pairs = wide // LANES
    both = dot(x[...], jnp.concatenate([w_key[...], w_value[...]], 1))
    keys = both[:, :wide].astype(jnp.bfloat16)
    values = (both[:, wide:] + b_value[...][None, :]).astype(jnp.bfloat16)
    for pair in range(pairs):
        keys_out[pair] = keys[:, pair * LANES : (pair + 1) * LANES]
        values_out[pair] = values[:, pair * LANES : (pair + 1) * LANES]
    queries = ((dot(x[pl.ds(0, rows), :], w_query[...]) + b_query[...][None, :]) * (0.125 * LOG2E)).astype(jnp.bfloat16)
    chunk = turned_out.shape[1]
    for i in range(chunk // LANES):
        start = pl.multiple_of(step * chunk + i * LANES, LANES)
        turned_out[:, pl.ds(i * LANES, LANES)] = x[pl.ds(start, LANES), :].T

    spans = spans_of(locals_)
    joint = lambda value, bucket: jnp.concatenate([value[span] for span in spans[bucket]], 0)
    cols = [slice(pair * LANES, (pair + 1) * LANES) for pair in range(pairs)]
    key_blocks = {}
    found = {}

    def scores_of(item):
        bucket, pair, head = item
        local = locals_[bucket]
        if head == 0:
            marks = jnp.concatenate([extra[span, :] for span in spans[bucket]], 0)
            key_blocks[bucket, pair] = jnp.concatenate([joint(keys[:, cols[pair]], bucket), marks], 1)
        one = jnp.where(lane_ids(local) == 0, 1.0, 0.0).astype(jnp.bfloat16)
        query = pick_head(queries[spans[bucket][0], cols[pair]], head)
        return dot(jnp.concatenate([query, one], 1), key_blocks[bucket, pair], NT)

    def mix(item, scores):
        bucket, pair, head = item
        top = jnp.max(scores, axis=-1, keepdims=True)
        weights = jnp.exp2(scores - top).astype(jnp.bfloat16)
        value = pick_head(joint(values[:, cols[pair]], bucket), head)
        result = dot(weights, jnp.concatenate([value, jnp.ones(value.shape, jnp.bfloat16)], 1))
        bulk = result[:, LANES:]
        found[item] = result[:, :LANES] / bulk, split_low(-(top + jnp.log2(bulk)))
        if head == 1:
            (left, some), (right, more) = found.pop((bucket, pair, 0)), found.pop(item)
            own = spans[bucket][0]
            mixed = (left + right).astype(jnp.bfloat16)
            mixed_out[own, cols[pair]] = mixed
            paired_out[pair, own, :] = mixed
            qa_out[pair, own, :LANES] = queries[own, cols[pair]]
            qa_out[pair, own, LANES:] = place_extra(1.0, some + more)

    pipelined([(b, p, h) for b in range(len(locals_)) for p in range(pairs) for h in range(2)], scores_of, mix)


def attend_forward(scalars, mine, others, w_query, w_key, w_value, b_query, b_value):
    locals_ = tuple(part.shape[1] for part in mine)
    rows = sum(locals_)
    width = w_query.shape[0]
    steps = 3
    near = [pl.BlockSpec(part.shape, lambda g: (0, 0, 0)) for part in others]
    wide = width // steps
    low = jnp.bfloat16
    pairs = width // LANES
    by_pair = lambda count, lanes: pl.BlockSpec((pairs // steps, count, lanes), lambda g: (g, 0, 0))
    column = pl.BlockSpec((width, wide), lambda g: (0, g))
    bias = pl.BlockSpec((wide,), lambda g: (g,))
    return pl.pallas_call(
        partial(forward_kernel, locals_),
        grid=(steps,),
        in_specs=[pl.BlockSpec(memory_space=pltpu.SMEM)] + [ANY] * 3 + near + [column] * 3 + [bias] * 2,
        out_specs=[
            by_pair(rows, 2 * LANES),
            by_pair(2 * rows, LANES),
            by_pair(2 * rows, LANES),
            pl.BlockSpec((rows, wide), lambda g: (0, g)),
            by_pair(rows, LANES),
            pl.BlockSpec((width, 2 * rows // steps), lambda g: (0, g)),
            pl.BlockSpec((2 * rows, LANES), lambda g: (0, 0)),
        ],
        out_shape=shapes(
            ((pairs, rows, 2 * LANES), low), ((pairs, 2 * rows, LANES), low), ((pairs, 2 * rows, LANES), low),
            ((rows, width), low), ((pairs, rows, LANES), low), ((width, 2 * rows), low), ((2 * rows, LANES), low),
        ),
        scratch_shapes=[pltpu.VMEM((2 * rows, width), low), pltpu.SemaphoreType.DMA((6,))],
        compiler_params=pltpu.CompilerParams(vmem_limit_bytes=LIMIT),
        cost_estimate=cost(26),
        name="attend_forward",
    )(scalars, *mine, *others, w_query, w_key, w_value, b_query, b_value)


def backward_kernel(locals_, group, scalars, qa, keys, values, mixed, grad_mixed, turned_h, extra, vectors_in, *refs):
    if group % 2:
        earlier, *refs = refs
    grad_query, grad_keys, grad_values, vectors, *grad_w_refs, turned, sems = refs
    copies = Copies(sems)
    copies.start("turned", turned_h, turned)
    vectors[...] = vectors_in[...]
    spans = spans_of(locals_)
    joint = lambda ref, bucket: jnp.concatenate([ref[span, :] for span in spans[bucket]], 0)
    held = {}

    def prepare(bucket):
        own = spans[bucket][0]
        local = locals_[bucket]
        cot = grad_mixed[own, :]
        product = cot.astype(jnp.float32) * mixed[own, :].astype(jnp.float32)
        lanes = lane_ids(local)
        pieces = []
        for head in range(2):
            keep = (lanes < 64) if head == 0 else (lanes >= 64)
            delta = jnp.sum(jnp.where(keep, product, 0.0), axis=-1, keepdims=True)
            pieces.extend(split_low(-jnp.broadcast_to(delta, (local, LANES))))
        marks = joint(extra, bucket)
        key = joint(keys, bucket)
        return (
            qa[own, :LANES], qa[own, LANES:], cot, place_extra(0.0, pieces), key,
            jnp.concatenate([key, marks], 1), jnp.concatenate([joint(values, bucket), marks], 1),
        )

    def scores_of(item):
        bucket, head = item
        if head == 0:
            held[bucket] = prepare(bucket)
        query, more, cot, cot_more, _, key_block, value_block = held[bucket]
        query_one, cot_one = pick_head(query, head), pick_head(cot, head)
        return (
            dot(key_block, jnp.concatenate([query_one, pick_extra(more, head)], 1), NT),
            dot(value_block, jnp.concatenate([cot_one, pick_extra(cot_more, head)], 1), NT),
            query_one, cot_one,
        )

    sums = {}

    def spread(item, ready):
        bucket, head = item
        scores, change, query_one, cot_one = ready
        probs = jnp.exp2(scores)
        grad_scores = (probs * change).astype(jnp.bfloat16)
        terms = (
            dot(probs.astype(jnp.bfloat16), cot_one),
            dot(grad_scores, query_one),
            dot(grad_scores, pick_head(held[bucket][4], head), TN),
        )
        if head == 0:
            sums[bucket] = terms
            return
        value, key, query = (old + term for old, term in zip(sums.pop(bucket), terms))
        own, other = spans[bucket]
        local = locals_[bucket]
        grad_query[own, :] = (query * 0.125).astype(jnp.bfloat16)
        key = (key * (1.0 / LOG2E)).astype(jnp.bfloat16)
        value = value.astype(jnp.bfloat16)
        grad_keys[own, :], grad_keys[other, :] = key[:local], key[local:]
        grad_values[own, :], grad_values[other, :] = value[:local], value[local:]

    pipelined([(bucket, head) for bucket in range(len(locals_)) for head in range(2)], scores_of, spread)
    copies.wait_all()
    both = dot(turned[...], jnp.concatenate([grad_keys[...], grad_values[...]], 1))
    query = dot(turned[:, : sum(locals_)], grad_query[...])
    grad_w = [part.astype(jnp.bfloat16) for part in (query, both[:, :LANES], both[:, LANES:])]
    for i in range(3):
        if group % 2:
            store_halves(scalars[3], grad_w_refs[0].at[i], grad_w_refs[1].at[i], earlier[i], grad_w[i])
        else:
            grad_w_refs[0][i] = grad_w[i]
    cs = pl.ds(group * LANES, LANES)
    vectors[6:7, cs] = sum_rows(grad_query[...].astype(jnp.float32))
    vectors[7:8, cs] = sum_rows(grad_values[...].astype(jnp.float32))


def attend_backward(scalars, locals_, qa, keys, values, mixed, grad_mixed, turned, extra, vectors, group, earlier):
    rows = sum(locals_)
    width = turned.shape[0]
    low = jnp.bfloat16

    def col(n, w=LANES):
        return pl.BlockSpec((None, n, w), lambda g: (group, 0, 0))

    def whole(shape):
        return pl.BlockSpec(shape, lambda g: (0,) * len(shape))

    weights = (3, width, LANES)
    last = group % 2
    qa, keys, values, mixed, grad_mixed = (
        pltpu.with_memory_space_constraint(value, pltpu.HBM) for value in (qa, keys, values, mixed, grad_mixed)
    )
    return pl.pallas_call(
        partial(backward_kernel, locals_, group),
        grid=(1,),
        in_specs=[pl.BlockSpec(memory_space=pltpu.SMEM), col(rows, 2 * LANES), col(2 * rows), col(2 * rows), col(rows), col(rows),
                  ANY, whole(extra.shape), whole(vectors.shape)] + [whole(weights)] * last,
        out_specs=[whole((rows, LANES)), whole((2 * rows, LANES)), whole((2 * rows, LANES)), whole(vectors.shape)]
        + [whole(weights)] * (1 + last),
        out_shape=[pltpu.HBM((rows, LANES), low), pltpu.HBM((2 * rows, LANES), low), pltpu.HBM((2 * rows, LANES), low),
                   jax.ShapeDtypeStruct(vectors.shape, jnp.float32)] + [pltpu.HBM(weights, low)] * (1 + last),
        scratch_shapes=[pltpu.VMEM(turned.shape, low), pltpu.SemaphoreType.DMA((1,))],
        compiler_params=pltpu.CompilerParams(vmem_limit_bytes=MIDDLE),
        cost_estimate=cost(9),
        name="attend_backward",
    )(scalars, qa, keys, values, mixed, grad_mixed, turned, extra, vectors, *([earlier] if last else []))


def gelu_and_slope(inner):
    share = 0.5 + 0.5 * lax.erf(inner * 0.7071067811865476)
    bell = jnp.exp2(inner * inner * (-0.5 * LOG2E))
    return inner * share, share + inner * bell * 0.3989422804014327


def mean_of(field):
    return jnp.sum(field, axis=-1, keepdims=True) * (1.0 / field.shape[-1])


def normalize(field):
    centered = field - mean_of(field)
    inverse = lax.rsqrt(mean_of(centered * centered) + 1e-12)
    return centered * inverse, inverse


def norm_back(grad, normed, inverse):
    return inverse * (grad - mean_of(grad) - normed * mean_of(grad * normed))


def store_halves(core, keep, send, low, high):
    first = core == 0
    keep[...] = jnp.where(first, low, high).astype(keep.dtype)
    send[...] = jnp.where(first, high, low).astype(send.dtype)


def ffn_kernel(blocks, scalars, mixed_h, tok_long, tok_mid, tok_short, cot_long, cot_mid, cot_short,
               w_out_h, b_out, gain_attn, beta_attn, w_inner_h, b_inner, w_outer_h, b_outer, gain_ffn, beta_ffn,
               out_long, out_mid, out_short, grad_sum_h, grad_mixed_h, vectors, keep_outer_h, send_outer_h, keep_inner_h, send_inner_h,
               mixed, toks, cots, w_out, w_inner, w_outer, hidden_s, slope_s, normed_s, second_s, first_s, outer_s, branch_s,
               out_s, grad_mixed, keep_outer, send_outer, keep_inner, send_inner, sems):
    width, inner_width = w_inner.shape
    chunks = inner_width // CHUNK
    copies = Copies(sems)
    copies.start("mixed", mixed_h, mixed)
    copies.start("w_out", w_out_h, w_out)
    places = []
    at = 0
    for i, ref in enumerate((tok_long, tok_mid, tok_short)):
        places.append(pl.ds(at, ref.shape[1]))
        copies.start(("tok", i), ref.at[0], toks.at[places[i]])
        at += ref.shape[1]
    columns = [pl.ds(j * CHUNK, CHUNK) for j in range(chunks)]
    for j, cs in enumerate(columns):
        copies.start(("inner", j), w_inner_h.at[:, cs], w_inner.at[:, cs])
        copies.start(("outer", j), w_outer_h.at[cs, :], w_outer.at[cs, :])
    for i, ref in enumerate((cot_long, cot_mid, cot_short)):
        copies.start(("cot", i), ref.at[0], cots.at[places[i]])

    full = jnp.float32
    low = jnp.bfloat16
    spans = [pl.ds(0, blocks[0]), pl.ds(blocks[0], blocks[1])]
    inverses, sums = [None] * 2, {}

    def add(name, value):
        sums[name] = value if name not in sums else sums[name] + value

    def enter(b):
        rs = spans[b]
        field = toks[rs, :].astype(full) + dot(mixed[rs, :], w_out[...]) + b_out[...][None, :]
        normed, inverses[b] = normalize(field)
        normed_s[rs, :] = normed
        first = normed * gain_attn[...][None, :] + beta_attn[...][None, :]
        first_s[rs, :] = first.astype(low)
        second_s[rs, :] = first + b_outer[...][None, :]

    def forward(b, between):
        rs = spans[b]
        copies.wait(("inner", 0))
        work = {0: dot(first_s[rs, :], w_inner[:, columns[0]])}
        for j, cs in enumerate(columns):
            if j + 1 < chunks:
                copies.wait(("inner", j + 1))
                work[j + 1] = dot(first_s[rs, :], w_inner[:, columns[j + 1]])
            value, rate = gelu_and_slope(work.pop(j) + b_inner[cs][None, :])
            hidden = value.astype(low)
            hidden_s[rs, cs] = hidden
            slope_s[rs, cs] = rate.astype(low)
            copies.wait(("outer", j))
            second_s[rs, :] += dot(hidden_s[rs, cs], w_outer[cs, :])
            if j == 0:
                between()

    def leave(b):
        rs = spans[b]
        normed, inverse = normalize(second_s[rs, :])
        out_s[rs, :] = (normed * gain_ffn[...][None, :] + beta_ffn[...][None, :]).astype(low)
        cot = cots[rs, :].astype(full)
        back = norm_back(cot * gain_ffn[...][None, :], normed, inverse)
        second_s[rs, :] = back
        rounded = back.astype(low)
        outer_s[rs, :] = rounded
        add("gain_ffn", sum_rows(cot * normed))
        add("beta_ffn", sum_rows(cot))
        add("b_outer", sum_rows(rounded.astype(full)))

    def backward(b, between):
        rs = spans[b]
        work = {0: dot(outer_s[rs, :], w_outer[columns[0], :], NT)}
        for j, cs in enumerate(columns):
            if j + 1 < chunks:
                work[j + 1] = dot(outer_s[rs, :], w_outer[columns[j + 1], :], NT)
            rounded = (work.pop(j) * slope_s[rs, cs].astype(full)).astype(low)
            slope_s[rs, cs] = rounded
            add(("b_inner", j), sum_rows(rounded.astype(full)))
            second_s[rs, :] += dot(slope_s[rs, cs], w_inner[:, cs], NT)
            if j == 0:
                between()

    def finish(b):
        rs = spans[b]
        total = second_s[rs, :]
        normed = normed_s[rs, :]
        back = norm_back(total * gain_attn[...][None, :], normed, inverses[b])
        add("gain_attn", sum_rows(total * normed))
        add("beta_attn", sum_rows(total))
        normed_s[rs, :] = back
        rounded = back.astype(low)
        branch_s[rs, :] = rounded
        add("b_out", sum_rows(rounded.astype(full)))
        change = dot(rounded, w_out[...], NT).astype(low)
        for pair in range(width // LANES):
            grad_mixed[pair, rs, :] = change[:, pair * LANES : (pair + 1) * LANES]

    core = scalars[3]
    half = width // 2

    def outer_weights(chosen):
        for j in chosen:
            cs = columns[j]
            whole = dot(hidden_s[:, cs], outer_s[...], TN)
            for p in range(3):
                near, far = whole[:, p * LANES : (p + 1) * LANES], whole[:, half + p * LANES : half + (p + 1) * LANES]
                store_halves(core, keep_outer.at[p, cs, :], send_outer.at[p, cs, :], near, far)

    copies.wait("mixed")
    copies.wait("w_out")
    for i in range(3):
        copies.wait(("tok", i))
    enter(0)
    forward(0, lambda: enter(1))
    for i in range(3):
        copies.wait(("cot", i))
    forward(1, lambda: leave(0))
    backward(0, lambda: leave(1))
    for i, ref in enumerate((out_long, out_mid, out_short)):
        copies.start(("out", i), out_s.at[places[i]], ref.at[0])
    outer_weights(range(chunks // 3))
    backward(1, lambda: finish(0))
    outer_weights(range(chunks // 3, chunks - 1))
    finish(1)
    outer_weights(range(chunks - 1, chunks))
    for p in range(3):
        copies.start(("send_outer", p), send_outer.at[p], send_outer_h.at[p])
        copies.start(("keep_outer", p), keep_outer.at[p], keep_outer_h.at[p])
    copies.start("grad_mixed", grad_mixed, grad_mixed_h)
    copies.start("grad_sum", normed_s, grad_sum_h)
    part = inner_width // 6
    whole = dot(mixed[...], branch_s[...], TN)
    for p in range(3):
        near, far = whole[:, p * LANES : (p + 1) * LANES], whole[:, half + p * LANES : half + (p + 1) * LANES]
        cs = pl.ds(part, LANES)
        store_halves(core, keep_inner.at[p, :, cs], send_inner.at[p, :, cs], near, far)
    turned = first_s[...].T
    for p in range(3):
        near = dot(turned, slope_s[:, pl.ds(p * part, part)])
        far = dot(turned, slope_s[:, pl.ds(inner_width // 2 + p * part, part)])
        cs = pl.ds(0, part)
        store_halves(core, keep_inner.at[p, :, cs], send_inner.at[p, :, cs], near, far)
        copies.start(("send_inner", p), send_inner.at[p], send_inner_h.at[p])
        copies.start(("keep_inner", p), keep_inner.at[p], keep_inner_h.at[p])
    for i, name in enumerate(("gain_ffn", "beta_ffn", "b_outer", "gain_attn", "beta_attn", "b_out")):
        vectors[pl.ds(i, 1), :] = sums[name]
    vectors[6:16, :] = jnp.zeros((10, width), full)
    line = jnp.concatenate([sums["b_inner", j] for j in range(chunks)], 1)
    for i in range(inner_width // width):
        vectors[pl.ds(16 + i, 1), :] = line[:, i * width : (i + 1) * width]
    copies.wait_all()


def ffn(scalars, mixed, toks, cots, w_out, b_out, gain_attn, beta_attn, w_inner, b_inner, w_outer, b_outer, gain_ffn, beta_ffn):
    rows, width = mixed.shape
    inner_width = w_inner.shape[1]
    low, full = jnp.bfloat16, jnp.float32
    blocks = (toks[0].shape[1], toks[1].shape[1] + toks[2].shape[1])
    vm = pl.BlockSpec(memory_space=pltpu.VMEM)
    outer = (3, inner_width, LANES)
    inner = (3, width, inner_width // 6 + LANES)
    square = (rows, width)
    wide = (rows, inner_width)
    by_pair = (width // LANES, rows, LANES)
    vectors = (16 + inner_width // width, width)
    scratch = [
        (square, low), (square, low), (square, low), (w_out.shape, low), (w_inner.shape, low), (w_outer.shape, low),
        (wide, low), (wide, low), (square, full), (square, full), (square, low), (square, low), (square, low),
        (square, low), (by_pair, low), (outer, low), (outer, low), (inner, low), (inner, low),
    ]
    return pl.pallas_call(
        partial(ffn_kernel, blocks),
        in_specs=[pl.BlockSpec(memory_space=pltpu.SMEM)] + [ANY] * 7 + [ANY, vm, vm, vm, ANY, vm, ANY, vm, vm, vm],
        out_specs=[ANY] * 5 + [vm] + [ANY] * 4,
        out_shape=shapes(
            *[(tok.shape, low) for tok in toks], (square, full), (by_pair, low), (vectors, full),
            (outer, low), (outer, low), (inner, low), (inner, low),
        ),
        scratch_shapes=[pltpu.VMEM(shape, dtype) for shape, dtype in scratch]
        + [pltpu.SemaphoreType.DMA((8 + 2 * (inner_width // CHUNK) + 17,))],
        compiler_params=pltpu.CompilerParams(vmem_limit_bytes=FFN_LIMIT),
        cost_estimate=cost(50),
        name="ffn_all",
    )(scalars, mixed, *toks, *cots, w_out, b_out, gain_attn, beta_attn, w_inner, b_inner, w_outer, b_outer, gain_ffn, beta_ffn)


def input_kernel(half, count, *refs):
    out = refs[-1]
    w_key, w_value, *parts = refs[:-1]
    keys, values, parts = parts[:count], parts[count : 2 * count], parts[2 * count :]
    beside = lambda blocks: jnp.concatenate([block[...] for block in blocks], 1)
    total = dot(beside(keys), w_key[...], NT) + dot(beside(values), w_value[...], NT)
    if half == 0:
        w_query, grad_sum, *queries = parts
        total = total + dot(beside(queries), w_query[...], NT) + grad_sum[...]
    out[...] = total.astype(out.dtype)


def input_grads(half, dtype, w_key, w_value, keys, values, *more):
    width = w_key.shape[0]
    rows = keys[0].shape[0] // 2
    steps = 3
    size = rows // steps
    square = pl.BlockSpec(w_key.shape, lambda k: (0, 0))
    row = lambda cols, shift=0: pl.BlockSpec((size, cols), lambda k: (k + shift, 0))
    operands = [w_key, w_value, *keys, *values]
    specs = [square] * 2 + [row(LANES, half * steps)] * (2 * len(keys))
    if half == 0:
        w_query, grad_sum, queries = more
        operands += [w_query, grad_sum, *queries]
        specs += [square, row(width)] + [row(LANES)] * len(queries)
    return pl.pallas_call(
        partial(input_kernel, half, len(keys)),
        grid=(steps,),
        in_specs=specs,
        out_specs=row(width),
        out_shape=jax.ShapeDtypeStruct((rows, width), dtype),
        compiler_params=pltpu.CompilerParams(vmem_limit_bytes=MIDDLE),
        cost_estimate=cost(7 - 2 * half),
        name="input_grads",
    )(*operands)


def swap(value, axis, bit):
    return lax.ppermute(value, axis, [(i, i ^ bit) for i in range(lax.axis_size(axis))])


def up16(rows):
    return -(-rows // 16) * 16


def halves_of(shards, left, bit):
    place = left.index(bit)
    return 2**place, shards // 2 ** (place + 1)


def steps_of(pairs):
    steps = min(pairs, STEPS)
    return steps, pairs // steps


def half_spec(array, above, below, lead=None):
    _, many = steps_of(above * below)
    if below >= many:
        block = (1, 2, many)
        index = lambda k: (k * many // below, 0, k * many % below // many)
    else:
        block = (many // below, 2, below)
        index = lambda k: (k, 0, 0)
    shape = block + array.shape[-2:]
    if lead is None:
        return pl.BlockSpec(shape, lambda k, s: index(k) + (0, 0))
    return pl.BlockSpec((None,) + shape, lambda k, s: (lead,) + index(k) + (0, 0))


def pairs_in(ref):
    above, below = ref.shape[0], ref.shape[2]
    return [(a * below + b, a, b) for a in range(above) for b in range(below)]


def call_halving(body, name, scalars, pairs, operands, specs, outs):
    steps, many = steps_of(pairs)
    blocks = [(many,) + tuple(out) for out in outs for _ in range(2)]
    large = 2 * pairs * sum(math.prod(out) for out in outs) > 1000000
    kind = pltpu.HBM if large else jax.ShapeDtypeStruct
    return pl.pallas_call(
        body,
        grid_spec=pltpu.PrefetchScalarGridSpec(
            num_scalar_prefetch=1,
            grid=(steps,),
            in_specs=specs,
            out_specs=[pl.BlockSpec(block, lambda k, s: (k, 0, 0)) for block in blocks],
        ),
        out_shape=[kind((pairs,) + block[1:], jnp.bfloat16) for block in blocks],
        compiler_params=pltpu.CompilerParams(vmem_limit_bytes=SMALL),
        cost_estimate=cost(2),
        name=name,
    )(scalars, *operands)


def bit_of(scalars, bit):
    return (scalars[4] >> bit) & 1


def ffn_merge_kernel(bits, scalars, *refs):
    ins, outs = refs[:12], refs[12:]
    for p in range(3):
        keep_outer, came_outer, keep_inner, came_inner = ins[4 * p : 4 * p + 4]
        mine = bit_of(scalars, bits[p])
        for out, which in zip(outs[2 * p : 2 * p + 2], (1 - mine, mine)):
            for k, a, b in pairs_in(keep_outer):
                first = keep_outer[a, which, b] + came_outer[a, which, b]
                rows = first.shape[0]
                out[k, pl.ds(0, rows), :] = first
                second = keep_inner[a, which, b] + came_inner[a, which, b]
                at = up16(rows)
                rows = second.shape[0]
                for q in range(second.shape[1] // LANES):
                    out[k, pl.ds(at, rows), :] = second[:, q * LANES : (q + 1) * LANES]
                    at += up16(rows)


def ffn_merge(n, bits, scalars, keep_outer, came_outer, keep_inner, came_inner):
    operands, specs = [], []
    left = list(range(n.bit_length() - 1))[::-1]
    for p in range(3):
        above, below = halves_of(n, left, bits[p])
        for array in (keep_outer, came_outer, keep_inner, came_inner):
            view = array.reshape(3, above, 2, below, array.shape[1] // n, array.shape[2])
            operands.append(view)
            specs.append(half_spec(view, above, below, p))
    height = up16(keep_outer.shape[1] // n) + keep_inner.shape[2] // LANES * up16(keep_inner.shape[1] // n)
    return call_halving(
        partial(ffn_merge_kernel, bits), "ffn_merge", scalars, n // 2, operands, specs, [(height, LANES)] * 3
    )


def own_columns(line, start, size):
    width = line.shape[1]
    lanes = -(-size // LANES) * LANES
    from_ = lax.broadcasted_iota(jnp.int32, (width, lanes), 0)
    to = lax.broadcasted_iota(jnp.int32, (width, lanes), 1)
    chosen = jnp.where((from_ == start + to) & (to < size), 1.0, 0.0).astype(jnp.bfloat16)
    return dot(line.astype(jnp.bfloat16), chosen)


def attend_merge_kernel(n, bits, scalars, vectors, *refs):
    count = (len(refs) - 6) // 6
    ins, outs = refs[: 6 * count], refs[6 * count :]
    many = outs[0].shape[0]
    for p in range(3):
        mine = bit_of(scalars, bits[p])
        for out, which in zip(outs[2 * p : 2 * p + 2], (1 - mine, mine)):
            at = 0
            for t in range(count):
                keep, came = ins[2 * (p * count + t) : 2 * (p * count + t) + 2]
                for k, a, b in pairs_in(keep):
                    total = keep[a, which, b] + came[a, which, b]
                    rows = total.shape[0]
                    out[k, pl.ds(at, rows), :] = total
                at += up16(rows)
            if p > 0:
                continue
            below = 2 ** bits[0]
            for k in range(many):
                pair = pl.program_id(0) * many + k
                shard = (pair // below * 2 + which) * below + pair % below
                small = vectors[...]
                width = small.shape[1]
                found = own_columns(small, shard * (width // n), width // n)
                inner = small.shape[0] - 16
                per = inner * width // n
                span = n // inner
                line = jnp.zeros((1, width), jnp.float32)
                for i in range(inner):
                    line = jnp.where(shard // span == i, small[16 + i : 17 + i], line)
                wide = own_columns(jnp.broadcast_to(line, (8, width)), shard % span * per, per)
                groups = [wide[:1, g * LANES : (g + 1) * LANES] for g in range(wide.shape[1] // LANES)]
                block = jnp.concatenate([found[: 16 - len(groups)]] + groups, 0)
                out[k, pl.ds(at, 16), :] = block.astype(out.dtype)


def attend_merge(n, bits, scalars, vectors, keeps, cames):
    whole = pl.BlockSpec(vectors.shape, lambda k, s: (0, 0))
    operands, specs = [vectors], [whole]
    left = list(range(n.bit_length() - 1))[::-1]
    for p in range(3):
        above, below = halves_of(n, left, bits[p])
        for pair in zip(keeps, cames):
            for array in pair:
                view = array.reshape(3, above, 2, below, array.shape[1] // n, array.shape[2])
                operands.append(view)
                specs.append(half_spec(view, above, below, p))
    height = len(keeps) * up16(keeps[0].shape[1] // n)
    return call_halving(
        partial(attend_merge_kernel, n, bits), "attend_merge", scalars, n // 2, operands, specs,
        [(height + 16, LANES), (height, LANES), (height, LANES)],
    )


def advance_kernel(bits, scalars, *refs):
    count = len(bits)
    for p, bit in enumerate(bits):
        keep, came = refs[2 * p : 2 * p + 2]
        mine = bit_of(scalars, bit)
        for out, which in zip(refs[2 * (count + p) : 2 * (count + p) + 2], (1 - mine, mine)):
            for k, a, b in pairs_in(keep):
                out[k] = keep[a, which, b] + came[a, which, b]


def advance(name, scalars, lefts, bits, keeps, cames):
    operands, specs = [], []
    shards = keeps[0].shape[0]
    for left, bit, keep, came in zip(lefts, bits, keeps, cames):
        above, below = halves_of(shards, left, bit)
        for array in (keep, came):
            view = array.reshape(above, 2, below, *array.shape[1:])
            operands.append(view)
            specs.append(half_spec(view, above, below))
    return call_halving(
        partial(advance_kernel, bits), name, scalars, shards // 2, operands, specs, [keep.shape[1:] for keep in keeps]
    )


def join_kernel(bit, count, scalars, *refs):
    send, kept = refs[2 * count :]
    mine = bit_of(scalars, bit)
    at = 0
    for p in range(count):
        keep, came = refs[2 * p : 2 * p + 2]
        rows = keep.shape[-2]
        for out, which in ((send, 1 - mine), (kept, mine)):
            for k, a, b in pairs_in(keep):
                out[k, pl.ds(at, rows), :] = keep[a, which, b] + came[a, which, b]
        at += rows


def join(scalars, left, bit, keeps, cames):
    operands, specs = [], []
    shards = keeps[0].shape[0]
    above, below = halves_of(shards, left, bit)
    for keep, came in zip(keeps, cames):
        for array in (keep, came):
            view = array.reshape(above, 2, below, *array.shape[1:])
            operands.append(view)
            specs.append(half_spec(view, above, below))
    height = sum(keep.shape[1] for keep in keeps)
    return call_halving(
        partial(join_kernel, bit, len(keeps)), "join_portions", scalars, shards // 2, operands, specs, [(height, LANES)]
    )


def last_kernel(keep, came, out):
    out[...] = keep[0] + came[0]


def last_sum(keep, came):
    vm = pl.BlockSpec(memory_space=pltpu.VMEM)
    return pl.pallas_call(
        last_kernel,
        in_specs=[vm] * 2,
        out_specs=vm,
        out_shape=jax.ShapeDtypeStruct(keep.shape[1:], keep.dtype),
        cost_estimate=cost(2),
        name="last_sum",
    )(keep, came)


def placer(scalars, mine, other):
    first = scalars[3] == 0
    at = 0

    def place(ref, left, right, size):
        nonlocal at
        a = mine[pl.ds(at, size), :].astype(jnp.float32)
        b = other[pl.ds(at, size), :].astype(jnp.float32)
        ref[:, pl.ds(left, LANES)] = jnp.where(first, a, b)
        ref[:, pl.ds(right, LANES)] = jnp.where(first, b, a)
        at += up16(size)

    def skip(size):
        nonlocal at
        at += size
        return at - size

    return place, skip


def ffn_result_kernel(scalars, mine, other, w_outer, w_inner, w_out):
    place, _ = placer(scalars, mine, other)
    rows, width = w_out.shape
    half = width // 2
    inner_half = w_inner.shape[1] // 2
    for p in range(3):
        place(w_outer, p * LANES, half + p * LANES, w_outer.shape[0])
        for q in range(inner_half // 3 // LANES):
            column = p * (inner_half // 3) + q * LANES
            place(w_inner, column, inner_half + column, rows)
        place(w_out, p * LANES, half + p * LANES, rows)


def attend_result_kernel(count, scalars, mine, other, w_query, w_key, w_value, b_inner, *lines):
    place, skip = placer(scalars, mine, other)
    rows = w_query.shape[0]
    for ref in (w_query, w_key, w_value):
        for t in range(count):
            place(ref, 2 * t * LANES, (2 * t + 1) * LANES, rows)
        if ref is w_query:
            rs = pl.ds(skip(16), 16)
            small = mine[rs, :].astype(jnp.float32) + other[rs, :].astype(jnp.float32)
    for i, ref in enumerate(lines):
        ref[...] = small[i, :rows]
    size = b_inner.shape[0]
    groups = -(-size // LANES)
    for g in range(groups):
        part = min(LANES, size - g * LANES)
        b_inner[pl.ds(g * LANES, part)] = small[16 - groups + g, :part]


def results(body, name, scalars, mine, outs):
    vm = pl.BlockSpec(memory_space=pltpu.VMEM)
    return pl.pallas_call(
        body,
        in_specs=[pl.BlockSpec(memory_space=pltpu.SMEM), vm, vm],
        out_specs=[vm] * len(outs),
        out_shape=shapes(*[(out, jnp.float32) for out in outs]),
        compiler_params=pltpu.CompilerParams(vmem_limit_bytes=SMALL),
        cost_estimate=cost(2),
        name=name,
    )(scalars, mine, swap(mine, "blk", 1))


def finish_kernel(own, came, *outs):
    start = 0
    for out in outs:
        rs = pl.ds(start, out.shape[1])
        out[0] = (own[rs, :] + came[rs, :].astype(jnp.float32)).astype(out.dtype)
        start += out.shape[1]


def finish_grads(toks, own, came):
    vm = pl.BlockSpec(memory_space=pltpu.VMEM)
    return pl.pallas_call(
        finish_kernel,
        in_specs=[vm] * 2,
        out_specs=[vm] * len(toks),
        out_shape=shapes(*[(tok.shape, tok.dtype) for tok in toks]),
        compiler_params=pltpu.CompilerParams(vmem_limit_bytes=SMALL),
        cost_estimate=cost(2),
        name="finish_grads",
    )(own, came)


def tie(*groups):
    flat, tree = jax.tree.flatten(groups)
    return jax.tree.unflatten(tree, lax.optimization_barrier(flat))


class Chain:
    def __init__(self, name, scalars, orders, arrays):
        self.name, self.scalars, self.orders = name, scalars, orders
        bits = len(orders[0])
        self.lefts = [[bit for bit in range(bits)[::-1] if bit != order[0]] for order in orders]
        self.step = 0
        self.hold(arrays)

    def hold(self, arrays):
        self.sends, self.keeps = list(arrays[0::2]), list(arrays[1::2])

    def send(self):
        self.cames = [swap(value, "batch", 1 << order[self.step]) for value, order in zip(self.sends, self.orders)]
        self.step += 1

    def advance(self):
        bits = [order[self.step] for order in self.orders]
        if any(left != self.lefts[0] for left in self.lefts):
            self.hold(advance(self.name, self.scalars, self.lefts, bits, self.keeps, self.cames))
        else:
            self.hold(join(self.scalars, self.lefts[0], bits[0], self.keeps, self.cames))
            self.lefts, self.orders = self.lefts[:1], self.orders[:1]
        for left, bit in zip(self.lefts, bits):
            left.remove(bit)

    def more(self):
        return self.step < len(self.orders[0])


def per_device(
    tokens_long, tokens_mid, tokens_short, lengths_long, lengths_mid, lengths_short,
    w_query, b_query, w_key, w_value, b_value, w_out, b_out, gain_attn, beta_attn,
    w_inner, b_inner, w_outer, b_outer, gain_ffn, beta_ffn,
    cotangent_long, cotangent_mid, cotangent_short,
):
    toks = (tokens_long, tokens_mid, tokens_short)
    cots = (cotangent_long, cotangent_mid, cotangent_short)
    locals_ = tuple(tok.shape[1] for tok in toks)
    width = w_query.shape[0]
    inner_width = w_inner.shape[1]
    n = lax.axis_size("batch")
    bits = n.bit_length() - 1
    later = list(range(3, bits))
    orders = [[0, 1, 2] + later, [1, 2, 0] + later, [2, 0, 1] + later]
    firsts = [order[0] for order in orders]
    core = lax.axis_index("blk")
    place = lax.axis_index("batch")
    scalars = jnp.concatenate(
        [lengths_long, lengths_mid, lengths_short, jnp.stack([core, place]).astype(jnp.int32)]
    )
    others = [swap(tok, "blk", 1) for tok in toks]
    qa, keys, values, mixed, paired, turned, extra = attend_forward(scalars, toks, others, w_query, w_key, w_value, b_query, b_value)
    out_long, out_mid, out_short, grad_sum, grad_mixed, vectors, keep_outer, send_outer, keep_inner, send_inner = ffn(
        scalars, mixed, toks, cots, w_out, b_out, gain_attn, beta_attn, w_inner, b_inner, w_outer, b_outer, gain_ffn, beta_ffn
    )
    came_outer = swap(send_outer, "blk", 1)
    came_inner = swap(send_inner, "blk", 1)
    pieces = []
    keeps, cames = [], []
    groups = width // LANES
    chain = None
    earlier = None
    for group in range(groups):
        if group == 1:
            vectors, keep_outer, keep_inner = tie(vectors, keep_outer, keep_inner)
            merged = ffn_merge(n, firsts, scalars, keep_outer, came_outer, keep_inner, came_inner)
            chain = Chain("ffn_step", scalars, orders, merged)
        if group > 2:
            done = (group - 1) // 2
            vectors, chain.keeps, cames[:done] = tie(vectors, chain.keeps, cames[:done])
            chain.advance()
        if group == 1 or group > 2:
            vectors, chain.sends = tie(vectors, chain.sends)
            chain.send()
        found = attend_backward(scalars, locals_, qa, keys, values, paired, grad_mixed, turned, extra, vectors, group, earlier)
        pieces.append(found[:3])
        vectors = found[3]
        earlier = found[4]
        if group % 2:
            keeps.append(found[4])
            cames.append(swap(found[5], "blk", 1))
    grad_queries, grad_keys, grad_values = zip(*pieces)
    send = input_grads(1, jnp.bfloat16, w_key, w_value, grad_keys, grad_values)
    chain.cames, send = tie(chain.cames, send)
    while chain.more():
        chain.advance()
        chain.send()
    keeps, send = tie(keeps, send)
    tail = Chain("attend_step", scalars, orders, attend_merge(n, firsts, scalars, vectors, keeps, cames))
    grad_sum, tail.sends = tie(grad_sum, tail.sends)
    tail.send()
    came = swap(send, "blk", 1)
    own = input_grads(0, jnp.float32, w_key, w_value, grad_keys, grad_values, w_query, grad_sum, grad_queries)
    own, tail.keeps = tie(own, tail.keeps)
    tail.advance()
    chain.keeps, own, tail.sends = tie(chain.keeps, own, tail.sends)
    tail.send()
    whole = last_sum(chain.keeps[0], chain.cames[0])
    grad_parts = list(finish_grads(toks, own, came))
    square = (width // n, width)
    grad_w_outer, grad_w_inner, grad_w_out = results(
        ffn_result_kernel, "ffn_results", scalars, whole, [(inner_width // n, width), (width // n, inner_width), square]
    )
    grad_parts, tail.keeps = tie(grad_parts, tail.keeps)
    tail.advance()
    tail.send()
    while tail.more():
        tail.advance()
        tail.send()
    (
        grad_w_query, grad_w_key, grad_w_value, grad_b_inner, grad_gain_ffn, grad_beta_ffn, grad_b_outer,
        grad_gain_attn, grad_beta_attn, grad_b_out, grad_b_query, grad_b_value,
    ) = results(
        partial(attend_result_kernel, groups // 2), "attend_results", scalars, last_sum(tail.keeps[0], tail.cames[0]),
        [square] * 3 + [(inner_width // n,)] + [(width // n,)] * 8,
    )
    return (
        out_long, out_mid, out_short, *grad_parts, grad_w_query, grad_b_query, grad_w_key, grad_w_value, grad_b_value,
        grad_w_out, grad_b_out, grad_gain_attn, grad_beta_attn, grad_w_inner, grad_b_inner, grad_w_outer, grad_b_outer,
        grad_gain_ffn, grad_beta_ffn,
    )


def solution(mesh):
    in_specs = (
        P("batch", "blk", None),
        P("batch", "blk", None),
        P("batch", "blk", None),
        P("batch"),
        P("batch"),
        P("batch"),
        P(),
        P(),
        P(),
        P(),
        P(),
        P(),
        P(),
        P(),
        P(),
        P(),
        P(),
        P(),
        P(),
        P(),
        P(),
        P("batch", "blk", None),
        P("batch", "blk", None),
        P("batch", "blk", None),
    )
    out_specs = (
        P("batch", "blk", None),
        P("batch", "blk", None),
        P("batch", "blk", None),
        P("batch", "blk", None),
        P("batch", "blk", None),
        P("batch", "blk", None),
        P("batch", None),
        P("batch"),
        P("batch", None),
        P("batch", None),
        P("batch"),
        P("batch", None),
        P("batch"),
        P("batch"),
        P("batch"),
        P("batch", None),
        P("batch"),
        P("batch", None),
        P("batch"),
        P("batch"),
        P("batch"),
    )
    return jax.shard_map(
        per_device, mesh=mesh, in_specs=in_specs, out_specs=out_specs, check_vma=False
    )
```

```python
import math
from functools import partial

import jax
import jax.numpy as jnp
from jax import lax
from jax.experimental import pallas as pl
from jax.experimental.pallas import tpu as pltpu
from jax.sharding import PartitionSpec as P

HEADS = 12
LANES = 128
NT = (((1,), (1,)), ((), ()))
TN = (((0,), (0,)), ((), ()))
LOG2E = 1.4426950408889634
CHUNK = 1024
LIMIT = 58 * 1024 * 1024
MIDDLE = 32 * 1024 * 1024
FFN_LIMIT = 60 * 1024 * 1024
SMALL = 24 * 1024 * 1024
STEPS = 2
ANY = pl.BlockSpec(memory_space=pl.ANY)


def cost(microseconds):
    return pl.CostEstimate(flops=microseconds * 1_100_000_000, bytes_accessed=1_000_000, transcendentals=0)


def shapes(*items):
    return [jax.ShapeDtypeStruct(shape, dtype) for shape, dtype in items]


def sum_rows(field):
    return jnp.sum(field, axis=0, keepdims=True)


def dot(left, right, dims=(((1,), (0,)), ((), ()))):
    return lax.dot_general(left, right, dims, preferred_element_type=jnp.float32)


def split_low(value):
    high = value.astype(jnp.bfloat16).astype(jnp.float32)
    rest = value - high
    middle = rest.astype(jnp.bfloat16).astype(jnp.float32)
    return high, middle, rest - middle


def lane_ids(rows):
    return lax.broadcasted_iota(jnp.int32, (rows, LANES), 1)


def pick_head(block, head):
    lanes = lane_ids(block.shape[0])
    half = LANES // 2
    keep = (lanes < half) if head == 0 else (lanes >= half)
    return jnp.where(keep, block.astype(jnp.float32), 0.0).astype(jnp.bfloat16)


def pick_extra(block, head):
    lanes = lane_ids(block.shape[0])
    keep = (lanes == 0) | ((lanes >= 1 + 3 * head) & (lanes < 4 + 3 * head))
    return jnp.where(keep, block.astype(jnp.float32), 0.0).astype(jnp.bfloat16)


def place_extra(first, pieces):
    lanes = lane_ids(pieces[0].shape[0])
    block = jnp.where(lanes == 0, first, 0.0)
    for place, piece in enumerate(pieces):
        block = jnp.where(lanes == 1 + place, piece, block)
    return block.astype(jnp.bfloat16)


class Copies:
    def __init__(self, sems):
        self.sems, self.used, self.waiting = sems, 0, {}

    def start(self, name, source, target):
        copy = pltpu.make_async_copy(source, target, self.sems.at[self.used])
        copy.start()
        self.used += 1
        self.waiting[name] = copy

    def wait(self, name):
        copy = self.waiting.pop(name, None)
        if copy is not None:
            copy.wait()

    def wait_all(self):
        for name in list(self.waiting):
            self.wait(name)


def marks_of(scalars, bucket, local):
    lanes = lane_ids(2 * local)
    row = lax.broadcasted_iota(jnp.int32, (2 * local, LANES), 0)
    core = scalars[3]
    place = jnp.where(row < local, row + core * local, row - core * local)
    bias = jnp.where(place < scalars[bucket], 0.0, -1e9)
    return jnp.where(lanes == 0, bias, jnp.where(lanes < 7, 1.0, 0.0)).astype(jnp.bfloat16)


def spans_of(locals_):
    spans = []
    start = 0
    for local in locals_:
        spans.append((slice(start, start + local), slice(sum(locals_) + start, sum(locals_) + start + local)))
        start += local
    return spans


def pipelined(items, first, rest):
    ready = first(items[0])
    for place, item in enumerate(items):
        following = first(items[place + 1]) if place + 1 < len(items) else None
        rest(item, ready)
        ready = following


def forward_kernel(locals_, scalars, x_long, x_mid, x_short, y_long, y_mid, y_short,
                   w_query, w_key, w_value, b_query, b_value,
                   qa_out, keys_out, values_out, paired_out, turned_out, x, sems):
    step = pl.program_id(0)
    rows = sum(locals_)

    @pl.when(step == 0)
    def _():
        copies = Copies(sems)
        offset = 0
        for i, ref in enumerate((x_long, x_mid, x_short, y_long, y_mid, y_short)):
            copies.start(i, ref.at[0], x.at[pl.ds(offset, ref.shape[1])])
            offset += ref.shape[1]
        copies.wait_all()

    wide = w_query.shape[1]
    pairs = wide // LANES
    both = dot(x[...], jnp.concatenate([w_key[...], w_value[...]], 1))
    keys = both[:, :wide].astype(jnp.bfloat16)
    values = (both[:, wide:] + b_value[...][None, :]).astype(jnp.bfloat16)
    for pair in range(pairs):
        keys_out[pair] = keys[:, pair * LANES : (pair + 1) * LANES]
        values_out[pair] = values[:, pair * LANES : (pair + 1) * LANES]
    queries = ((dot(x[pl.ds(0, rows), :], w_query[...]) + b_query[...][None, :]) * (0.125 * LOG2E)).astype(jnp.bfloat16)
    chunk = turned_out.shape[1]
    for i in range(chunk // LANES):
        start = pl.multiple_of(step * chunk + i * LANES, LANES)
        turned_out[:, pl.ds(i * LANES, LANES)] = x[pl.ds(start, LANES), :].T

    spans = spans_of(locals_)
    joint = lambda value, bucket: jnp.concatenate([value[span] for span in spans[bucket]], 0)
    cols = [slice(pair * LANES, (pair + 1) * LANES) for pair in range(pairs)]
    key_blocks, marks, found = {}, {}, {}

    def scores_of(item):
        bucket, pair, head = item
        local = locals_[bucket]
        if head == 0:
            if pair == 0:
                marks[bucket] = marks_of(scalars, bucket, local)
            key_blocks[bucket, pair] = jnp.concatenate([joint(keys[:, cols[pair]], bucket), marks[bucket]], 1)
        one = jnp.where(lane_ids(local) == 0, 1.0, 0.0).astype(jnp.bfloat16)
        query = pick_head(queries[spans[bucket][0], cols[pair]], head)
        return dot(jnp.concatenate([query, one], 1), key_blocks[bucket, pair], NT)

    def mix(item, scores):
        bucket, pair, head = item
        top = jnp.max(scores, axis=-1, keepdims=True)
        weights = jnp.exp2(scores - top).astype(jnp.bfloat16)
        value = pick_head(joint(values[:, cols[pair]], bucket), head)
        result = dot(weights, jnp.concatenate([value, jnp.ones(value.shape, jnp.bfloat16)], 1))
        bulk = result[:, LANES:]
        found[item] = result[:, :LANES] / bulk, split_low(-(top + jnp.log2(bulk)))
        if head == 1:
            (left, some), (right, more) = found.pop((bucket, pair, 0)), found.pop(item)
            own = spans[bucket][0]
            mixed = (left + right).astype(jnp.bfloat16)
            paired_out[pair, own, :] = mixed
            qa_out[pair, own, :LANES] = queries[own, cols[pair]]
            qa_out[pair, own, LANES:] = place_extra(1.0, some + more)

    pipelined([(b, p, h) for b in range(len(locals_)) for p in range(pairs) for h in range(2)], scores_of, mix)


def attend_forward(scalars, mine, others, w_query, w_key, w_value, b_query, b_value):
    locals_ = tuple(part.shape[1] for part in mine)
    rows = sum(locals_)
    width = w_query.shape[0]
    steps = 3
    near = [pl.BlockSpec(part.shape, lambda g: (0, 0, 0)) for part in others]
    wide = width // steps
    low = jnp.bfloat16
    pairs = width // LANES
    by_pair = lambda count, lanes: pl.BlockSpec((pairs // steps, count, lanes), lambda g: (g, 0, 0))
    column = pl.BlockSpec((width, wide), lambda g: (0, g))
    bias = pl.BlockSpec((wide,), lambda g: (g,))
    return pl.pallas_call(
        partial(forward_kernel, locals_),
        grid=(steps,),
        in_specs=[pl.BlockSpec(memory_space=pltpu.SMEM)] + [ANY] * 3 + near + [column] * 3 + [bias] * 2,
        out_specs=[
            by_pair(rows, 2 * LANES),
            by_pair(2 * rows, LANES),
            by_pair(2 * rows, LANES),
            by_pair(rows, LANES),
            pl.BlockSpec((width, 2 * rows // steps), lambda g: (0, g)),
        ],
        out_shape=shapes(
            ((pairs, rows, 2 * LANES), low), ((pairs, 2 * rows, LANES), low), ((pairs, 2 * rows, LANES), low),
            ((pairs, rows, LANES), low), ((width, 2 * rows), low),
        ),
        scratch_shapes=[pltpu.VMEM((2 * rows, width), low), pltpu.SemaphoreType.DMA((6,))],
        compiler_params=pltpu.CompilerParams(vmem_limit_bytes=LIMIT),
        cost_estimate=cost(26),
        name="attend_forward",
    )(scalars, *mine, *others, w_query, w_key, w_value, b_query, b_value)


def backward_kernel(locals_, group, scalars, qa, keys, values, mixed, grad_mixed, turned, vectors_in, *refs):
    if group % 2:
        earlier, *refs = refs
    grad_query, grad_keys, grad_values, vectors, *grad_w_refs = refs
    vectors[...] = vectors_in[...]
    spans = spans_of(locals_)
    joint = lambda ref, bucket: jnp.concatenate([ref[span, :] for span in spans[bucket]], 0)
    held = {}

    def prepare(bucket):
        own = spans[bucket][0]
        local = locals_[bucket]
        cot = grad_mixed[own, :]
        product = cot.astype(jnp.float32) * mixed[own, :].astype(jnp.float32)
        lanes = lane_ids(local)
        pieces = []
        for head in range(2):
            keep = (lanes < 64) if head == 0 else (lanes >= 64)
            delta = jnp.sum(jnp.where(keep, product, 0.0), axis=-1, keepdims=True)
            pieces.extend(split_low(-jnp.broadcast_to(delta, (local, LANES))))
        marks = marks_of(scalars, bucket, local)
        key = joint(keys, bucket)
        return (
            qa[own, :LANES], qa[own, LANES:], cot, place_extra(0.0, pieces), key,
            jnp.concatenate([key, marks], 1), jnp.concatenate([joint(values, bucket), marks], 1),
        )

    def scores_of(item):
        bucket, head = item
        if head == 0:
            held[bucket] = prepare(bucket)
        query, more, cot, cot_more, _, key_block, value_block = held[bucket]
        query_one, cot_one = pick_head(query, head), pick_head(cot, head)
        return (
            dot(key_block, jnp.concatenate([query_one, pick_extra(more, head)], 1), NT),
            dot(value_block, jnp.concatenate([cot_one, pick_extra(cot_more, head)], 1), NT),
            query_one, cot_one,
        )

    sums = {}

    def spread(item, ready):
        bucket, head = item
        scores, change, query_one, cot_one = ready
        probs = jnp.exp2(scores)
        grad_scores = (probs * change).astype(jnp.bfloat16)
        terms = (
            dot(probs.astype(jnp.bfloat16), cot_one),
            dot(grad_scores, query_one),
            dot(grad_scores, pick_head(held[bucket][4], head), TN),
        )
        if head == 0:
            sums[bucket] = terms
            return
        value, key, query = (old + term for old, term in zip(sums.pop(bucket), terms))
        own, other = spans[bucket]
        local = locals_[bucket]
        grad_query[own, :] = (query * 0.125).astype(jnp.bfloat16)
        key = (key * (1.0 / LOG2E)).astype(jnp.bfloat16)
        value = value.astype(jnp.bfloat16)
        grad_keys[own, :], grad_keys[other, :] = key[:local], key[local:]
        grad_values[own, :], grad_values[other, :] = value[:local], value[local:]

    pipelined([(bucket, head) for bucket in range(len(locals_)) for head in range(2)], scores_of, spread)
    both = dot(turned[...], jnp.concatenate([grad_keys[...], grad_values[...]], 1))
    query = dot(turned[:, : sum(locals_)], grad_query[...])
    grad_w = [part.astype(jnp.bfloat16) for part in (query, both[:, :LANES], both[:, LANES:])]
    for i in range(3):
        if group % 2:
            store_halves(scalars[3], grad_w_refs[0].at[i], grad_w_refs[1].at[i], earlier[i], grad_w[i])
        else:
            grad_w_refs[0][i] = grad_w[i]
    cs = pl.ds(group * LANES, LANES)
    vectors[6:7, cs] = sum_rows(grad_query[...].astype(jnp.float32))
    vectors[7:8, cs] = sum_rows(grad_values[...].astype(jnp.float32))


def attend_backward(scalars, locals_, qa, keys, values, mixed, grad_mixed, turned, vectors, group, earlier):
    rows = sum(locals_)
    width = turned.shape[0]
    low = jnp.bfloat16

    def col(n, w=LANES):
        return pl.BlockSpec((None, n, w), lambda g: (group, 0, 0))

    def whole(shape):
        return pl.BlockSpec(shape, lambda g: (0,) * len(shape))

    weights = (3, width, LANES)
    last = group % 2
    qa, keys, values, mixed, grad_mixed = (
        pltpu.with_memory_space_constraint(value, pltpu.HBM) for value in (qa, keys, values, mixed, grad_mixed)
    )
    return pl.pallas_call(
        partial(backward_kernel, locals_, group),
        grid=(1,),
        in_specs=[pl.BlockSpec(memory_space=pltpu.SMEM), col(rows, 2 * LANES), col(2 * rows), col(2 * rows), col(rows), col(rows),
                  pl.BlockSpec(memory_space=pltpu.VMEM), whole(vectors.shape)] + [whole(weights)] * last,
        out_specs=[whole((rows, LANES)), whole((2 * rows, LANES)), whole((2 * rows, LANES)), whole(vectors.shape)]
        + [whole(weights)] * (1 + last),
        out_shape=[pltpu.HBM((rows, LANES), low), pltpu.HBM((2 * rows, LANES), low), pltpu.HBM((2 * rows, LANES), low),
                   jax.ShapeDtypeStruct(vectors.shape, jnp.float32)] + [pltpu.HBM(weights, low)] * (1 + last),
        compiler_params=pltpu.CompilerParams(vmem_limit_bytes=MIDDLE),
        cost_estimate=cost(9),
        name="attend_backward",
    )(scalars, qa, keys, values, mixed, grad_mixed, turned, vectors, *([earlier] if last else []))


def gelu_and_slope(inner):
    share = 0.5 + 0.5 * lax.erf(inner * 0.7071067811865476)
    bell = jnp.exp2(inner * inner * (-0.5 * LOG2E))
    return inner * share, share + inner * bell * 0.3989422804014327


def mean_of(field):
    return jnp.sum(field, axis=-1, keepdims=True) * (1.0 / field.shape[-1])


def normalize(field):
    centered = field - mean_of(field)
    inverse = lax.rsqrt(mean_of(centered * centered) + 1e-12)
    return centered * inverse, inverse


def norm_back(grad, normed, inverse):
    return inverse * (grad - mean_of(grad) - normed * mean_of(grad * normed))


def store_halves(core, keep, send, low, high):
    first = core == 0
    keep[...] = jnp.where(first, low, high).astype(keep.dtype)
    send[...] = jnp.where(first, high, low).astype(send.dtype)


def ffn_kernel(blocks, scalars, mixed_h, tok_long, tok_mid, tok_short, cot_long, cot_mid, cot_short,
               w_out_h, b_out, gain_attn, beta_attn, w_inner_h, b_inner, w_outer_h, b_outer, gain_ffn, beta_ffn,
               out_long, out_mid, out_short, grad_sum_h, grad_mixed_h, vectors, keep_outer_h, send_outer_h, keep_inner_h, send_inner_h,
               mixed, toks, cots, w_out, w_inner, w_outer, hidden_s, slope_s, normed_s, second_s, first_s, outer_s, branch_s,
               out_s, grad_mixed, keep_outer, send_outer, keep_inner, send_inner, sems):
    width, inner_width = w_inner.shape
    chunks = inner_width // CHUNK
    copies = Copies(sems)
    for pair in range(width // LANES):
        copies.start(("mixed", pair), mixed_h.at[pair], mixed.at[:, pl.ds(pair * LANES, LANES)])
    copies.start("w_out", w_out_h, w_out)
    places = []
    at = 0
    for i, ref in enumerate((tok_long, tok_mid, tok_short)):
        places.append(pl.ds(at, ref.shape[1]))
        copies.start(("tok", i), ref.at[0], toks.at[places[i]])
        at += ref.shape[1]
    columns = [pl.ds(j * CHUNK, CHUNK) for j in range(chunks)]
    for j, cs in enumerate(columns):
        copies.start(("inner", j), w_inner_h.at[:, cs], w_inner.at[:, cs])
        copies.start(("outer", j), w_outer_h.at[cs, :], w_outer.at[cs, :])
    for i, ref in enumerate((cot_long, cot_mid, cot_short)):
        copies.start(("cot", i), ref.at[0], cots.at[places[i]])

    full = jnp.float32
    low = jnp.bfloat16
    spans = [pl.ds(0, blocks[0]), pl.ds(blocks[0], blocks[1])]
    inverses, sums = [None] * 2, {}

    def add(name, value):
        sums[name] = value if name not in sums else sums[name] + value

    def enter(b):
        rs = spans[b]
        field = toks[rs, :].astype(full) + dot(mixed[rs, :], w_out[...]) + b_out[...][None, :]
        normed, inverses[b] = normalize(field)
        normed_s[rs, :] = normed
        first = normed * gain_attn[...][None, :] + beta_attn[...][None, :]
        first_s[rs, :] = first.astype(low)
        second_s[rs, :] = first + b_outer[...][None, :]

    def forward(b, between):
        rs = spans[b]
        copies.wait(("inner", 0))
        work = {0: dot(first_s[rs, :], w_inner[:, columns[0]])}
        for j, cs in enumerate(columns):
            if j + 1 < chunks:
                copies.wait(("inner", j + 1))
                work[j + 1] = dot(first_s[rs, :], w_inner[:, columns[j + 1]])
            value, rate = gelu_and_slope(work.pop(j) + b_inner[cs][None, :])
            hidden = value.astype(low)
            hidden_s[rs, cs] = hidden
            slope_s[rs, cs] = rate.astype(low)
            copies.wait(("outer", j))
            second_s[rs, :] += dot(hidden_s[rs, cs], w_outer[cs, :])
            if j == 0:
                between()

    def leave(b):
        rs = spans[b]
        normed, inverse = normalize(second_s[rs, :])
        out_s[rs, :] = (normed * gain_ffn[...][None, :] + beta_ffn[...][None, :]).astype(low)
        cot = cots[rs, :].astype(full)
        back = norm_back(cot * gain_ffn[...][None, :], normed, inverse)
        second_s[rs, :] = back
        rounded = back.astype(low)
        outer_s[rs, :] = rounded
        add("gain_ffn", sum_rows(cot * normed))
        add("beta_ffn", sum_rows(cot))
        add("b_outer", sum_rows(rounded.astype(full)))

    def backward(b, between):
        rs = spans[b]
        work = {0: dot(outer_s[rs, :], w_outer[columns[0], :], NT)}
        for j, cs in enumerate(columns):
            if j + 1 < chunks:
                work[j + 1] = dot(outer_s[rs, :], w_outer[columns[j + 1], :], NT)
            rounded = (work.pop(j) * slope_s[rs, cs].astype(full)).astype(low)
            slope_s[rs, cs] = rounded
            add(("b_inner", j), sum_rows(rounded.astype(full)))
            second_s[rs, :] += dot(slope_s[rs, cs], w_inner[:, cs], NT)
            if j == 0:
                between()

    def finish(b):
        rs = spans[b]
        total = second_s[rs, :]
        normed = normed_s[rs, :]
        back = norm_back(total * gain_attn[...][None, :], normed, inverses[b])
        add("gain_attn", sum_rows(total * normed))
        add("beta_attn", sum_rows(total))
        normed_s[rs, :] = back
        rounded = back.astype(low)
        branch_s[rs, :] = rounded
        add("b_out", sum_rows(rounded.astype(full)))
        change = dot(rounded, w_out[...], NT).astype(low)
        for pair in range(width // LANES):
            grad_mixed[pair, rs, :] = change[:, pair * LANES : (pair + 1) * LANES]

    core = scalars[3]
    half = width // 2

    def outer_weights(chosen):
        for j in chosen:
            cs = columns[j]
            whole = dot(hidden_s[:, cs], outer_s[...], TN)
            for p in range(3):
                near, far = whole[:, p * LANES : (p + 1) * LANES], whole[:, half + p * LANES : half + (p + 1) * LANES]
                store_halves(core, keep_outer.at[p, cs, :], send_outer.at[p, cs, :], near, far)

    for pair in range(width // LANES):
        copies.wait(("mixed", pair))
    copies.wait("w_out")
    for i in range(3):
        copies.wait(("tok", i))
    enter(0)
    forward(0, lambda: enter(1))
    for i in range(3):
        copies.wait(("cot", i))
    forward(1, lambda: leave(0))
    backward(0, lambda: leave(1))
    for i, ref in enumerate((out_long, out_mid, out_short)):
        copies.start(("out", i), out_s.at[places[i]], ref.at[0])
    outer_weights(range(chunks // 3))
    backward(1, lambda: finish(0))
    outer_weights(range(chunks // 3, chunks - 1))
    finish(1)
    outer_weights(range(chunks - 1, chunks))
    for p in range(3):
        copies.start(("send_outer", p), send_outer.at[p], send_outer_h.at[p])
        copies.start(("keep_outer", p), keep_outer.at[p], keep_outer_h.at[p])
    copies.start("grad_mixed", grad_mixed, grad_mixed_h)
    copies.start("grad_sum", normed_s, grad_sum_h)
    part = inner_width // 6
    whole = dot(mixed[...], branch_s[...], TN)
    for p in range(3):
        near, far = whole[:, p * LANES : (p + 1) * LANES], whole[:, half + p * LANES : half + (p + 1) * LANES]
        cs = pl.ds(part, LANES)
        store_halves(core, keep_inner.at[p, :, cs], send_inner.at[p, :, cs], near, far)
    turned = first_s[...].T
    for p in range(3):
        near = dot(turned, slope_s[:, pl.ds(p * part, part)])
        far = dot(turned, slope_s[:, pl.ds(inner_width // 2 + p * part, part)])
        cs = pl.ds(0, part)
        store_halves(core, keep_inner.at[p, :, cs], send_inner.at[p, :, cs], near, far)
        copies.start(("send_inner", p), send_inner.at[p], send_inner_h.at[p])
        copies.start(("keep_inner", p), keep_inner.at[p], keep_inner_h.at[p])
    for i, name in enumerate(("gain_ffn", "beta_ffn", "b_outer", "gain_attn", "beta_attn", "b_out")):
        vectors[pl.ds(i, 1), :] = sums[name]
    vectors[6:16, :] = jnp.zeros((10, width), full)
    line = jnp.concatenate([sums["b_inner", j] for j in range(chunks)], 1)
    for i in range(inner_width // width):
        vectors[pl.ds(16 + i, 1), :] = line[:, i * width : (i + 1) * width]
    copies.wait_all()


def ffn(scalars, mixed, toks, cots, w_out, b_out, gain_attn, beta_attn, w_inner, b_inner, w_outer, b_outer, gain_ffn, beta_ffn):
    rows, width = mixed.shape[1], w_out.shape[1]
    inner_width = w_inner.shape[1]
    low, full = jnp.bfloat16, jnp.float32
    blocks = (toks[0].shape[1], toks[1].shape[1] + toks[2].shape[1])
    vm = pl.BlockSpec(memory_space=pltpu.VMEM)
    outer = (3, inner_width, LANES)
    inner = (3, width, inner_width // 6 + LANES)
    square = (rows, width)
    wide = (rows, inner_width)
    by_pair = (width // LANES, rows, LANES)
    vectors = (16 + inner_width // width, width)
    scratch = [
        (square, low), (square, low), (square, low), (w_out.shape, low), (w_inner.shape, low), (w_outer.shape, low),
        (wide, low), (wide, low), (square, full), (square, full), (square, low), (square, low), (square, low),
        (square, low), (by_pair, low), (outer, low), (outer, low), (inner, low), (inner, low),
    ]
    return pl.pallas_call(
        partial(ffn_kernel, blocks),
        in_specs=[pl.BlockSpec(memory_space=pltpu.SMEM)] + [ANY] * 7 + [ANY, vm, vm, vm, ANY, vm, ANY, vm, vm, vm],
        out_specs=[ANY] * 5 + [vm] + [ANY] * 4,
        out_shape=shapes(
            *[(tok.shape, low) for tok in toks], (square, full), (by_pair, low), (vectors, full),
            (outer, low), (outer, low), (inner, low), (inner, low),
        ),
        scratch_shapes=[pltpu.VMEM(shape, dtype) for shape, dtype in scratch]
        + [pltpu.SemaphoreType.DMA((7 + width // LANES + 2 * (inner_width // CHUNK) + 17,))],
        compiler_params=pltpu.CompilerParams(vmem_limit_bytes=FFN_LIMIT),
        cost_estimate=cost(50),
        name="ffn_all",
    )(scalars, mixed, *toks, *cots, w_out, b_out, gain_attn, beta_attn, w_inner, b_inner, w_outer, b_outer, gain_ffn, beta_ffn)


def input_kernel(half, count, *refs):
    out = refs[-1]
    w_key, w_value, *parts = refs[:-1]
    keys, values, parts = parts[:count], parts[count : 2 * count], parts[2 * count :]
    beside = lambda blocks: jnp.concatenate([block[...] for block in blocks], 1)
    total = dot(beside(keys), w_key[...], NT) + dot(beside(values), w_value[...], NT)
    if half == 0:
        w_query, grad_sum, *queries = parts
        total = total + dot(beside(queries), w_query[...], NT) + grad_sum[...]
    out[...] = total.astype(out.dtype)


def input_grads(half, dtype, w_key, w_value, keys, values, *more):
    width = w_key.shape[0]
    rows = keys[0].shape[0] // 2
    steps = 3
    size = rows // steps
    square = pl.BlockSpec(w_key.shape, lambda k: (0, 0))
    row = lambda cols, shift=0: pl.BlockSpec((size, cols), lambda k: (k + shift, 0))
    operands = [w_key, w_value, *keys, *values]
    specs = [square] * 2 + [row(LANES, half * steps)] * (2 * len(keys))
    if half == 0:
        w_query, grad_sum, queries = more
        operands += [w_query, grad_sum, *queries]
        specs += [square, row(width)] + [row(LANES)] * len(queries)
    return pl.pallas_call(
        partial(input_kernel, half, len(keys)),
        grid=(steps,),
        in_specs=specs,
        out_specs=row(width),
        out_shape=jax.ShapeDtypeStruct((rows, width), dtype),
        compiler_params=pltpu.CompilerParams(vmem_limit_bytes=MIDDLE),
        cost_estimate=cost(7 - 2 * half),
        name="input_grads",
    )(*operands)


def swap(value, axis, bit):
    return lax.ppermute(value, axis, [(i, i ^ bit) for i in range(lax.axis_size(axis))])


def up16(rows):
    return -(-rows // 16) * 16


def halves_of(shards, left, bit):
    place = left.index(bit)
    return 2**place, shards // 2 ** (place + 1)


def steps_of(pairs):
    steps = min(pairs, STEPS)
    return steps, pairs // steps


def half_spec(array, above, below, lead=None):
    _, many = steps_of(above * below)
    if below >= many:
        block = (1, 2, many)
        index = lambda k: (k * many // below, 0, k * many % below // many)
    else:
        block = (many // below, 2, below)
        index = lambda k: (k, 0, 0)
    shape = block + array.shape[-2:]
    if lead is None:
        return pl.BlockSpec(shape, lambda k, s: index(k) + (0, 0))
    return pl.BlockSpec((None,) + shape, lambda k, s: (lead,) + index(k) + (0, 0))


def pairs_in(ref):
    above, below = ref.shape[0], ref.shape[2]
    return [(a * below + b, a, b) for a in range(above) for b in range(below)]


def call_halving(body, name, scalars, pairs, operands, specs, outs):
    steps, many = steps_of(pairs)
    blocks = [(many,) + tuple(out) for out in outs for _ in range(2)]
    large = 2 * pairs * sum(math.prod(out) for out in outs) > 1000000
    kind = pltpu.HBM if large else jax.ShapeDtypeStruct
    return pl.pallas_call(
        body,
        grid_spec=pltpu.PrefetchScalarGridSpec(
            num_scalar_prefetch=1,
            grid=(steps,),
            in_specs=specs,
            out_specs=[pl.BlockSpec(block, lambda k, s: (k, 0, 0)) for block in blocks],
        ),
        out_shape=[kind((pairs,) + block[1:], jnp.bfloat16) for block in blocks],
        compiler_params=pltpu.CompilerParams(vmem_limit_bytes=SMALL),
        cost_estimate=cost(2),
        name=name,
    )(scalars, *operands)


def bit_of(scalars, bit):
    return (scalars[4] >> bit) & 1


def ffn_merge_kernel(bits, scalars, *refs):
    ins, outs = refs[:12], refs[12:]
    for p in range(3):
        keep_outer, came_outer, keep_inner, came_inner = ins[4 * p : 4 * p + 4]
        mine = bit_of(scalars, bits[p])
        for out, which in zip(outs[2 * p : 2 * p + 2], (1 - mine, mine)):
            for k, a, b in pairs_in(keep_outer):
                first = keep_outer[a, which, b] + came_outer[a, which, b]
                rows = first.shape[0]
                out[k, pl.ds(0, rows), :] = first
                second = keep_inner[a, which, b] + came_inner[a, which, b]
                at = up16(rows)
                rows = second.shape[0]
                for q in range(second.shape[1] // LANES):
                    out[k, pl.ds(at, rows), :] = second[:, q * LANES : (q + 1) * LANES]
                    at += up16(rows)


def ffn_merge(n, bits, scalars, keep_outer, came_outer, keep_inner, came_inner):
    operands, specs = [], []
    left = list(range(n.bit_length() - 1))[::-1]
    for p in range(3):
        above, below = halves_of(n, left, bits[p])
        for array in (keep_outer, came_outer, keep_inner, came_inner):
            view = array.reshape(3, above, 2, below, array.shape[1] // n, array.shape[2])
            operands.append(view)
            specs.append(half_spec(view, above, below, p))
    height = up16(keep_outer.shape[1] // n) + keep_inner.shape[2] // LANES * up16(keep_inner.shape[1] // n)
    return call_halving(
        partial(ffn_merge_kernel, bits), "ffn_merge", scalars, n // 2, operands, specs, [(height, LANES)] * 3
    )


def own_columns(line, start, size):
    width = line.shape[1]
    lanes = -(-size // LANES) * LANES
    from_ = lax.broadcasted_iota(jnp.int32, (width, lanes), 0)
    to = lax.broadcasted_iota(jnp.int32, (width, lanes), 1)
    chosen = jnp.where((from_ == start + to) & (to < size), 1.0, 0.0).astype(jnp.bfloat16)
    return dot(line.astype(jnp.bfloat16), chosen)


def attend_merge_kernel(n, bits, scalars, vectors, *refs):
    count = (len(refs) - 6) // 6
    ins, outs = refs[: 6 * count], refs[6 * count :]
    many = outs[0].shape[0]
    for p in range(3):
        mine = bit_of(scalars, bits[p])
        for out, which in zip(outs[2 * p : 2 * p + 2], (1 - mine, mine)):
            at = 0
            for t in range(count):
                keep, came = ins[2 * (p * count + t) : 2 * (p * count + t) + 2]
                for k, a, b in pairs_in(keep):
                    total = keep[a, which, b] + came[a, which, b]
                    rows = total.shape[0]
                    out[k, pl.ds(at, rows), :] = total
                at += up16(rows)
            if p > 0:
                continue
            below = 2 ** bits[0]
            for k in range(many):
                pair = pl.program_id(0) * many + k
                shard = (pair // below * 2 + which) * below + pair % below
                small = vectors[...]
                width = small.shape[1]
                found = own_columns(small, shard * (width // n), width // n)
                inner = small.shape[0] - 16
                per = inner * width // n
                span = n // inner
                line = jnp.zeros((1, width), jnp.float32)
                for i in range(inner):
                    line = jnp.where(shard // span == i, small[16 + i : 17 + i], line)
                wide = own_columns(jnp.broadcast_to(line, (8, width)), shard % span * per, per)
                groups = [wide[:1, g * LANES : (g + 1) * LANES] for g in range(wide.shape[1] // LANES)]
                block = jnp.concatenate([found[: 16 - len(groups)]] + groups, 0)
                out[k, pl.ds(at, 16), :] = block.astype(out.dtype)


def attend_merge(n, bits, scalars, vectors, keeps, cames):
    whole = pl.BlockSpec(vectors.shape, lambda k, s: (0, 0))
    operands, specs = [vectors], [whole]
    left = list(range(n.bit_length() - 1))[::-1]
    for p in range(3):
        above, below = halves_of(n, left, bits[p])
        for pair in zip(keeps, cames):
            for array in pair:
                view = array.reshape(3, above, 2, below, array.shape[1] // n, array.shape[2])
                operands.append(view)
                specs.append(half_spec(view, above, below, p))
    height = len(keeps) * up16(keeps[0].shape[1] // n)
    return call_halving(
        partial(attend_merge_kernel, n, bits), "attend_merge", scalars, n // 2, operands, specs,
        [(height + 16, LANES), (height, LANES), (height, LANES)],
    )


def advance_kernel(bits, scalars, *refs):
    count = len(bits)
    for p, bit in enumerate(bits):
        keep, came = refs[2 * p : 2 * p + 2]
        mine = bit_of(scalars, bit)
        for out, which in zip(refs[2 * (count + p) : 2 * (count + p) + 2], (1 - mine, mine)):
            for k, a, b in pairs_in(keep):
                out[k] = keep[a, which, b] + came[a, which, b]


def advance(name, scalars, lefts, bits, keeps, cames):
    operands, specs = [], []
    shards = keeps[0].shape[0]
    for left, bit, keep, came in zip(lefts, bits, keeps, cames):
        above, below = halves_of(shards, left, bit)
        for array in (keep, came):
            view = array.reshape(above, 2, below, *array.shape[1:])
            operands.append(view)
            specs.append(half_spec(view, above, below))
    return call_halving(
        partial(advance_kernel, bits), name, scalars, shards // 2, operands, specs, [keep.shape[1:] for keep in keeps]
    )


def join_kernel(bit, count, scalars, *refs):
    send, kept = refs[2 * count :]
    mine = bit_of(scalars, bit)
    at = 0
    for p in range(count):
        keep, came = refs[2 * p : 2 * p + 2]
        rows = keep.shape[-2]
        for out, which in ((send, 1 - mine), (kept, mine)):
            for k, a, b in pairs_in(keep):
                out[k, pl.ds(at, rows), :] = keep[a, which, b] + came[a, which, b]
        at += rows


def join(scalars, left, bit, keeps, cames):
    operands, specs = [], []
    shards = keeps[0].shape[0]
    above, below = halves_of(shards, left, bit)
    for keep, came in zip(keeps, cames):
        for array in (keep, came):
            view = array.reshape(above, 2, below, *array.shape[1:])
            operands.append(view)
            specs.append(half_spec(view, above, below))
    height = sum(keep.shape[1] for keep in keeps)
    return call_halving(
        partial(join_kernel, bit, len(keeps)), "join_portions", scalars, shards // 2, operands, specs, [(height, LANES)]
    )


def last_kernel(keep, came, out):
    out[...] = keep[0] + came[0]


def last_sum(keep, came):
    vm = pl.BlockSpec(memory_space=pltpu.VMEM)
    return pl.pallas_call(
        last_kernel,
        in_specs=[vm] * 2,
        out_specs=vm,
        out_shape=jax.ShapeDtypeStruct(keep.shape[1:], keep.dtype),
        cost_estimate=cost(2),
        name="last_sum",
    )(keep, came)


def placer(scalars, mine, other):
    first = scalars[3] == 0
    at = 0

    def place(ref, left, right, size):
        nonlocal at
        a = mine[pl.ds(at, size), :].astype(jnp.float32)
        b = other[pl.ds(at, size), :].astype(jnp.float32)
        ref[:, pl.ds(left, LANES)] = jnp.where(first, a, b)
        ref[:, pl.ds(right, LANES)] = jnp.where(first, b, a)
        at += up16(size)

    def skip(size):
        nonlocal at
        at += size
        return at - size

    return place, skip


def ffn_result_kernel(scalars, mine, other, w_outer, w_inner, w_out):
    place, _ = placer(scalars, mine, other)
    rows, width = w_out.shape
    half = width // 2
    inner_half = w_inner.shape[1] // 2
    for p in range(3):
        place(w_outer, p * LANES, half + p * LANES, w_outer.shape[0])
        for q in range(inner_half // 3 // LANES):
            column = p * (inner_half // 3) + q * LANES
            place(w_inner, column, inner_half + column, rows)
        place(w_out, p * LANES, half + p * LANES, rows)


def attend_result_kernel(count, scalars, mine, other, w_query, w_key, w_value, b_inner, *lines):
    place, skip = placer(scalars, mine, other)
    rows = w_query.shape[0]
    for ref in (w_query, w_key, w_value):
        for t in range(count):
            place(ref, 2 * t * LANES, (2 * t + 1) * LANES, rows)
        if ref is w_query:
            rs = pl.ds(skip(16), 16)
            small = mine[rs, :].astype(jnp.float32) + other[rs, :].astype(jnp.float32)
    for i, ref in enumerate(lines):
        ref[...] = small[i, :rows]
    size = b_inner.shape[0]
    groups = -(-size // LANES)
    for g in range(groups):
        part = min(LANES, size - g * LANES)
        b_inner[pl.ds(g * LANES, part)] = small[16 - groups + g, :part]


def results(body, name, scalars, mine, outs):
    vm = pl.BlockSpec(memory_space=pltpu.VMEM)
    return pl.pallas_call(
        body,
        in_specs=[pl.BlockSpec(memory_space=pltpu.SMEM), vm, vm],
        out_specs=[vm] * len(outs),
        out_shape=shapes(*[(out, jnp.float32) for out in outs]),
        compiler_params=pltpu.CompilerParams(vmem_limit_bytes=SMALL),
        cost_estimate=cost(2),
        name=name,
    )(scalars, mine, swap(mine, "blk", 1))


def finish_kernel(own, came, *outs):
    start = 0
    for out in outs:
        rs = pl.ds(start, out.shape[1])
        out[0] = (own[rs, :] + came[rs, :].astype(jnp.float32)).astype(out.dtype)
        start += out.shape[1]


def finish_grads(toks, own, came):
    vm = pl.BlockSpec(memory_space=pltpu.VMEM)
    return pl.pallas_call(
        finish_kernel,
        in_specs=[vm] * 2,
        out_specs=[vm] * len(toks),
        out_shape=shapes(*[(tok.shape, tok.dtype) for tok in toks]),
        compiler_params=pltpu.CompilerParams(vmem_limit_bytes=SMALL),
        cost_estimate=cost(2),
        name="finish_grads",
    )(own, came)


def tie(*groups):
    flat, tree = jax.tree.flatten(groups)
    return jax.tree.unflatten(tree, lax.optimization_barrier(flat))


class Chain:
    def __init__(self, name, scalars, orders, arrays):
        self.name, self.scalars, self.orders = name, scalars, orders
        bits = len(orders[0])
        self.lefts = [[bit for bit in range(bits)[::-1] if bit != order[0]] for order in orders]
        self.step = 0
        self.hold(arrays)

    def hold(self, arrays):
        self.sends, self.keeps = list(arrays[0::2]), list(arrays[1::2])

    def send(self):
        self.cames = [swap(value, "batch", 1 << order[self.step]) for value, order in zip(self.sends, self.orders)]
        self.step += 1

    def advance(self):
        bits = [order[self.step] for order in self.orders]
        if any(left != self.lefts[0] for left in self.lefts):
            self.hold(advance(self.name, self.scalars, self.lefts, bits, self.keeps, self.cames))
        else:
            self.hold(join(self.scalars, self.lefts[0], bits[0], self.keeps, self.cames))
            self.lefts, self.orders = self.lefts[:1], self.orders[:1]
        for left, bit in zip(self.lefts, bits):
            left.remove(bit)

    def more(self):
        return self.step < len(self.orders[0])


def per_device(
    tokens_long, tokens_mid, tokens_short, lengths_long, lengths_mid, lengths_short,
    w_query, b_query, w_key, w_value, b_value, w_out, b_out, gain_attn, beta_attn,
    w_inner, b_inner, w_outer, b_outer, gain_ffn, beta_ffn,
    cotangent_long, cotangent_mid, cotangent_short,
):
    toks = (tokens_long, tokens_mid, tokens_short)
    cots = (cotangent_long, cotangent_mid, cotangent_short)
    locals_ = tuple(tok.shape[1] for tok in toks)
    width = w_query.shape[0]
    inner_width = w_inner.shape[1]
    n = lax.axis_size("batch")
    bits = n.bit_length() - 1
    later = list(range(3, bits))
    orders = [[0, 1, 2] + later, [1, 2, 0] + later, [2, 0, 1] + later]
    firsts = [order[0] for order in orders]
    core = lax.axis_index("blk")
    place = lax.axis_index("batch")
    scalars = jnp.concatenate(
        [lengths_long, lengths_mid, lengths_short, jnp.stack([core, place]).astype(jnp.int32)]
    )
    others = [swap(tok, "blk", 1) for tok in toks]
    qa, keys, values, paired, turned = attend_forward(scalars, toks, others, w_query, w_key, w_value, b_query, b_value)
    out_long, out_mid, out_short, grad_sum, grad_mixed, vectors, keep_outer, send_outer, keep_inner, send_inner = ffn(
        scalars, paired, toks, cots, w_out, b_out, gain_attn, beta_attn, w_inner, b_inner, w_outer, b_outer, gain_ffn, beta_ffn
    )
    came_outer = swap(send_outer, "blk", 1)
    came_inner = swap(send_inner, "blk", 1)
    pieces = []
    keeps, cames = [], []
    groups = width // LANES
    chain = None
    earlier = None
    for group in range(groups):
        if group == 1:
            vectors, keep_outer, keep_inner = tie(vectors, keep_outer, keep_inner)
            merged = ffn_merge(n, firsts, scalars, keep_outer, came_outer, keep_inner, came_inner)
            chain = Chain("ffn_step", scalars, orders, merged)
        if group > 2:
            done = (group - 1) // 2
            vectors, chain.keeps, cames[:done] = tie(vectors, chain.keeps, cames[:done])
            chain.advance()
        if group == 1 or group > 2:
            vectors, chain.sends = tie(vectors, chain.sends)
            chain.send()
        found = attend_backward(scalars, locals_, qa, keys, values, paired, grad_mixed, turned, vectors, group, earlier)
        pieces.append(found[:3])
        vectors = found[3]
        earlier = found[4]
        if group % 2:
            keeps.append(found[4])
            cames.append(swap(found[5], "blk", 1))
    grad_queries, grad_keys, grad_values = zip(*pieces)
    send = input_grads(1, jnp.bfloat16, w_key, w_value, grad_keys, grad_values)
    chain.cames, send = tie(chain.cames, send)
    while chain.more():
        chain.advance()
        chain.send()
    keeps, send = tie(keeps, send)
    tail = Chain("attend_step", scalars, orders, attend_merge(n, firsts, scalars, vectors, keeps, cames))
    grad_sum, tail.sends = tie(grad_sum, tail.sends)
    tail.send()
    came = swap(send, "blk", 1)
    own = input_grads(0, jnp.float32, w_key, w_value, grad_keys, grad_values, w_query, grad_sum, grad_queries)
    own, tail.keeps = tie(own, tail.keeps)
    tail.advance()
    chain.keeps, own, tail.sends = tie(chain.keeps, own, tail.sends)
    tail.send()
    whole = last_sum(chain.keeps[0], chain.cames[0])
    grad_parts = list(finish_grads(toks, own, came))
    square = (width // n, width)
    grad_w_outer, grad_w_inner, grad_w_out = results(
        ffn_result_kernel, "ffn_results", scalars, whole, [(inner_width // n, width), (width // n, inner_width), square]
    )
    grad_parts, tail.keeps = tie(grad_parts, tail.keeps)
    tail.advance()
    tail.send()
    while tail.more():
        tail.advance()
        tail.send()
    (
        grad_w_query, grad_w_key, grad_w_value, grad_b_inner, grad_gain_ffn, grad_beta_ffn, grad_b_outer,
        grad_gain_attn, grad_beta_attn, grad_b_out, grad_b_query, grad_b_value,
    ) = results(
        partial(attend_result_kernel, groups // 2), "attend_results", scalars, last_sum(tail.keeps[0], tail.cames[0]),
        [square] * 3 + [(inner_width // n,)] + [(width // n,)] * 8,
    )
    return (
        out_long, out_mid, out_short, *grad_parts, grad_w_query, grad_b_query, grad_w_key, grad_w_value, grad_b_value,
        grad_w_out, grad_b_out, grad_gain_attn, grad_beta_attn, grad_w_inner, grad_b_inner, grad_w_outer, grad_b_outer,
        grad_gain_ffn, grad_beta_ffn,
    )


def solution(mesh):
    in_specs = (
        P("batch", "blk", None),
        P("batch", "blk", None),
        P("batch", "blk", None),
        P("batch"),
        P("batch"),
        P("batch"),
        P(),
        P(),
        P(),
        P(),
        P(),
        P(),
        P(),
        P(),
        P(),
        P(),
        P(),
        P(),
        P(),
        P(),
        P(),
        P("batch", "blk", None),
        P("batch", "blk", None),
        P("batch", "blk", None),
    )
    out_specs = (
        P("batch", "blk", None),
        P("batch", "blk", None),
        P("batch", "blk", None),
        P("batch", "blk", None),
        P("batch", "blk", None),
        P("batch", "blk", None),
        P("batch", None),
        P("batch"),
        P("batch", None),
        P("batch", None),
        P("batch"),
        P("batch", None),
        P("batch"),
        P("batch"),
        P("batch"),
        P("batch", None),
        P("batch"),
        P("batch", None),
        P("batch"),
        P("batch"),
        P("batch"),
    )
    return jax.shard_map(
        per_device, mesh=mesh, in_specs=in_specs, out_specs=out_specs, check_vma=False
    )
```
